32 devices in a mesh: trade: 8 (over z, y), path: 4 (over x, core).
Axes of the slice: x: 2, y: 2, z: 4, core: 2. Of those that a mesh axis runs over, the one named last changes fastest.
Arguments:
- shocks: bfloat16 [80, 32, 512], P(None, None, 'path'), may hold values from -6 to 6
- forward_start: float32 [80], replicated, may hold values from 0.01 to 0.06
- loading: float32 [80, 80], replicated, may hold values from -0.30186918 to 0.30186918
- coefficient: bfloat16 [4096, 160], P('trade'), may hold values from -0.5 to 0.5
- notional: float32 [4096], P('trade'), may hold values from -4 to 4
- ns_of_trade: int32 [4096], replicated, may hold values from 0 to 63, as said below
- agr_of_ns: int32 [64], P('trade'), may hold values from 0 to 31, as said below
- cpty_of_agr: int32 [32], P('trade'), may hold values from 0 to 31, as said below
- margin_lag: int32 [32], P('trade'), may hold values from 1 to 4
- default_weight: float32 [32, 32], P('trade'), may hold values from 0.02 to 0.2
Outputs:
- allocation: float32 [4096], P('trade')
- cva: float32 [32], P('trade')
The draws below stay inside these ranges and needn't reach their ends.
Inputs may be any that keep to these rules, and one draw needn't show every extreme that they name: `ns_of_trade`: the trades of each block of 512 consecutive trades fall in exactly 2 netting sets of every block of 8 consecutive netting sets, and at most 96 of them in one such block of sets; in every block of trades half of the blocks of sets receive exactly 96. `agr_of_ns`: netting set n belongs to an agreement of block n // 8 of 4 consecutive agreements. `cpty_of_agr`: agreement a belongs to a counterparty of block a // 4 of 4 consecutive counterparties.
All inputs are finite; a program needn't handle non-finite values.
Results may differ from the reference program's by a relative error of at most 0.025.
Values may be sent and summed in bfloat16 or wider, within the bound.
No kernel may reach another device: no remote copies, remote signals or barrier semaphores. Data moves between devices by JAX's collectives and lax.ppermute only.
A program may use at most 64 MiB of HBM per device.

```python
import math
import jax
import jax.numpy as jnp
import numpy as np
from jax import lax

TEN = 80
DATES = 32
TR_DEV = 512
NS_DEV = 8
AG_DEV = 4
CP_DEV = 4
CAP = 2
LAG_MAX = 4
PATHS = 512
TRADES = 4096
NETS = 64
AGRS = 32
CPTY = 32


def owner_layout(counts):
    owner_seq = np.repeat(np.arange(counts.shape[0]), counts)
    starts = np.concatenate([np.zeros(1, np.int64), np.cumsum(counts)[:-1]])
    rank_seq = np.arange(owner_seq.shape[0]) - starts[owner_seq]
    return (owner_seq.astype(np.int32), rank_seq.astype(np.int32))


def draw_shocks(key, part):
    key = jax.random.fold_in(key, 14)
    position = jnp.arange(PATHS, dtype=jnp.float32) / max(PATHS - 1, 1)
    scale = 0.5 + position
    noise = jnp.clip(jax.random.normal(key, (TEN, DATES, PATHS), jnp.float32), -4.0, 4.0)
    return (noise * scale[None, None, :]).astype(jnp.bfloat16)


def draw_ns_of_trade(key, part):
    key = jax.random.fold_in(key, 11)
    blocks = TRADES // TR_DEV
    owners = NETS // NS_DEV
    share = TR_DEV // owners
    heavy = share + share // 2
    light = share - share // 2
    key_one, key_two, key_three, key_four = jax.random.split(key, 4)
    scores = jax.random.randint(key_one, (blocks, owners, NS_DEV), 0, 1 << 20) * NS_DEV + jnp.arange(NS_DEV)
    chosen = jnp.argsort(scores, axis=-1)[:, :, :CAP].reshape(blocks, owners * CAP)
    even_owner = np.arange(owners) % 2 == 0
    seq_first, rank_first = owner_layout(np.where(even_owner, heavy, light))
    seq_second, rank_second = owner_layout(np.where(even_owner, light, heavy))
    flip = jax.random.randint(key_two, (blocks, 1), 0, 2)
    owner_seq = jnp.where(flip == 0, jnp.asarray(seq_first)[None, :], jnp.asarray(seq_second)[None, :])
    rank_seq = jnp.where(flip == 0, jnp.asarray(rank_first)[None, :], jnp.asarray(rank_second)[None, :])
    extra = jax.random.randint(key_three, (blocks, TR_DEV), 0, CAP)
    slot = jnp.where(rank_seq < CAP, rank_seq, extra)
    picked = jnp.take_along_axis(chosen, owner_seq * CAP + slot, axis=1)
    sets = owner_seq * NS_DEV + picked
    perms = jax.vmap(lambda sub_key: jax.random.permutation(sub_key, TR_DEV))(jax.random.split(key_four, blocks))
    placed = jnp.take_along_axis(sets, perms, axis=1)
    return placed.reshape(TRADES).astype(jnp.int32)


def draw_agr_of_ns(key, part):
    key = jax.random.fold_in(key, 12)
    offset = jax.random.randint(key, (NETS,), 0, AG_DEV)
    return (jnp.arange(NETS) // NS_DEV * AG_DEV + offset).astype(jnp.int32)


def draw_cpty_of_agr(key, part):
    key = jax.random.fold_in(key, 13)
    offset = jax.random.randint(key, (AGRS,), 0, CP_DEV)
    return (jnp.arange(AGRS) // AG_DEV * CP_DEV + offset).astype(jnp.int32)


def set_ends(values, key, least, top_value):
    spot = [jax.random.randint(jax.random.fold_in(key, axis), (), 0, length) for axis, length in enumerate(values.shape)]
    main_axis = values.shape.index(max(values.shape))
    next_to = spot[:main_axis] + [(spot[main_axis] + 1) % values.shape[main_axis]] + spot[main_axis + 1:]
    return values.at[tuple(spot)].set(least).at[tuple(next_to)].set(top_value)


def shard_levels(rng, dims, shards, least, largest):
    level = 1.0
    for dim, parts in shards:
        steps = jax.random.uniform(jax.random.fold_in(jax.random.fold_in(rng, 6), dim), (parts,), jnp.float32, least / len(shards), largest / len(shards))
        level = level * jnp.repeat(jnp.exp(steps), dims[dim] // parts).reshape((-1,) + (1,) * (len(dims) - 1 - dim))
    return level


def scatter_about(stream_key, shape, deviation, limit, cuts=(), kind=jnp.bfloat16):
    entries = deviation * jax.random.normal(stream_key, shape, jnp.float32)
    if cuts:
        entries = entries * shard_levels(stream_key, shape, cuts, -0.22, 0.18)
    return jnp.clip(entries, -limit, limit).astype(kind)


def setup_inputs(seed: int = 0) -> dict:
    splits = jax.random.split(jax.random.key(seed), 11)
    return {
        "shocks": draw_shocks(jax.random.fold_in(splits[10], 71), 0),
        "forward_start": jnp.clip(jax.random.uniform(splits[1], (TEN,), jnp.float32, 0.01, 0.06), 0.01, 0.06),
        "loading": scatter_about(splits[2], (TEN, TEN), (0.45 / TEN ** 0.5), 0.30186918, (), jnp.float32),
        "coefficient": scatter_about(splits[3], (TRADES, 2 * TEN), (2 * TEN) ** -0.5, 0.5, ((0, 8),)),
        "notional": scatter_about(splits[4], (TRADES,), 1.0, 4.0, ((0, 8),), jnp.float32),
        "ns_of_trade": draw_ns_of_trade(jax.random.fold_in(splits[10], 71), 0),
        "agr_of_ns": draw_agr_of_ns(jax.random.fold_in(splits[10], 71), 0),
        "cpty_of_agr": draw_cpty_of_agr(jax.random.fold_in(splits[10], 71), 0),
        "margin_lag": set_ends(jax.random.randint(splits[8], (AGRS,), 1, LAG_MAX + 1), jax.random.fold_in(splits[8], 1), 1, LAG_MAX).astype(jnp.int32),
        "default_weight": jnp.clip(jnp.exp(math.log(0.2) - 2.3025851 * jax.random.uniform(splits[9], (CPTY, DATES), jnp.float32) ** shard_levels(splits[9], (CPTY, DATES), ((0, 8),), -0.2, 0.2)), 0.02, 0.2),
    }


RATE_UNIT = 0.03
STEP = 0.25
SMOOTH = 0.5

def make_basis(walk, date_index, forward_start, loading):
    drift = 0.5 * STEP * lax.optimization_barrier(jnp.sum(loading * loading, axis=0))
    moved = jnp.dot(loading.T, walk, precision=lax.Precision.HIGHEST, preferred_element_type=jnp.float32)
    log_fwd = jnp.log(forward_start)[:, None] + jnp.sqrt(STEP) * moved - (date_index + 1.0)[None, :] * drift[:, None]
    fwd = jnp.exp(log_fwd)
    bond = jnp.exp(-jnp.cumsum(jnp.log1p(STEP * fwd), axis=0))
    return jnp.concatenate([bond * fwd / RATE_UNIT, bond], axis=0).astype(jnp.bfloat16)

def collateral_terms(agreement, margin_lag, agr_weight, path_total):
    lagged = jnp.zeros_like(agreement)
    for lag_step in range(1, LAG_MAX + 1):
        shifted = jnp.pad(agreement[:, :-lag_step], ((0, 0), (lag_step, 0), (0, 0)))
        lagged = lagged + jnp.where((margin_lag == lag_step)[:, None, None], shifted, 0.0)
    excess = agreement - lagged
    spread_root = jnp.sqrt(excess * excess + SMOOTH * SMOOTH)
    exposure = 0.5 * (excess + spread_root)
    slope = 0.5 * (1.0 + excess / spread_root)
    weighted = agr_weight[:, :, None] * slope
    ahead = jnp.zeros_like(weighted)
    for lag_step in range(1, LAG_MAX + 1):
        shifted = jnp.pad(weighted[:, lag_step:], ((0, 0), (0, lag_step), (0, 0)))
        ahead = ahead + jnp.where((margin_lag == lag_step)[:, None, None], shifted, 0.0)
    grads = ((weighted - ahead) / path_total).astype(jnp.bfloat16)
    return (exposure, grads)

def reference(shocks, forward_start, loading, coefficient, notional, ns_of_trade, agr_of_ns, cpty_of_agr, margin_lag, default_weight):
    columns = DATES * PATHS
    walk = jnp.cumsum(shocks.astype(jnp.float32), axis=1).reshape(TEN, columns)
    date_index = (jnp.arange(columns) // PATHS).astype(jnp.float32)
    basis = make_basis(walk, date_index, forward_start, loading).astype(jnp.float32)
    blocks = TRADES // TR_DEV
    coef_blocks = coefficient.reshape(blocks, TR_DEV, 2 * TEN)
    notional_blocks = notional.reshape(blocks, TR_DEV)
    set_blocks = ns_of_trade.reshape(blocks, TR_DEV)

    def price(coef_block, notional_block):
        underlying = jnp.dot(coef_block.astype(jnp.float32), basis, precision=lax.Precision.HIGHEST, preferred_element_type=jnp.float32)
        return (notional_block[:, None] * jnp.maximum(underlying, 0.0)).astype(jnp.bfloat16)

    def add_block(netted, inputs):
        coef_block, notional_block, set_block = inputs
        values = price(coef_block, notional_block)
        return (netted.at[set_block].add(values.astype(jnp.float32)), None)
    netted, _ = lax.scan(add_block, jnp.zeros((NETS, columns), jnp.float32), (coef_blocks, notional_blocks, set_blocks))
    agreement = jax.ops.segment_sum(netted, agr_of_ns, num_segments=AGRS).reshape(AGRS, DATES, PATHS)
    agr_weight = default_weight[cpty_of_agr]
    exposure, grads = collateral_terms(agreement, margin_lag, agr_weight, jnp.float32(PATHS))
    expected = jax.ops.segment_sum(lax.optimization_barrier(jnp.sum(exposure, axis=2)), cpty_of_agr, num_segments=CPTY) / PATHS
    cva = lax.optimization_barrier(jnp.sum(default_weight * expected, axis=1))
    grad_rows = grads.reshape(AGRS, columns)

    def alloc_block(carry, inputs):
        coef_block, notional_block, set_block = inputs
        values = price(coef_block, notional_block)
        rows = grad_rows[agr_of_ns[set_block]]
        return (carry, lax.optimization_barrier(jnp.sum(values.astype(jnp.float32) * rows.astype(jnp.float32), axis=1)))
    _, allocation = lax.scan(alloc_block, jnp.zeros((), jnp.float32), (coef_blocks, notional_blocks, set_blocks))
    return (allocation.reshape(TRADES), cva)
```

```python
import functools

import jax
import jax.numpy as jnp
from jax import lax
from jax.experimental import pallas as pl
from jax.experimental.pallas import tpu as pltpu
from jax.sharding import PartitionSpec as P

NS_DEV = 8
AG_DEV = 4
LAG_MAX = 4
LANES = 128
TAIL = 16
OWNERS_PER_ROW = LANES // NS_DEV

RATE_UNIT = 0.03
STEP = 0.25
SMOOTH = 0.5

F32 = jnp.float32
BF16 = jnp.bfloat16
VMEM = pl.BlockSpec(memory_space=pltpu.VMEM)
SMEM = pl.BlockSpec(memory_space=pltpu.SMEM)


def iota(shape, dim):
    return lax.broadcasted_iota(jnp.int32, shape, dim)


def split_bf16(x, parts):
    pieces = []
    for _ in range(parts):
        piece = x.astype(BF16).astype(F32)
        pieces.append(piece)
        x = x - piece
    return pieces


def pack_kernel(me_ref, agr_ref, cpty_ref, lag_ref, coef_ref, notional_ref, weight_ref, out_ref):
    me = me_ref[0]
    rows, basis_rows = coef_ref.shape
    groups = rows // LANES
    out_ref[0:rows, :] = coef_ref[:, 0:LANES]
    out_ref[rows : rows + LANES, :] = jnp.concatenate(
        [coef_ref[LANES * g : LANES * (g + 1), LANES:basis_rows] for g in range(groups)], axis=1
    )
    high, low = split_bf16(notional_ref[...], 2)
    lane = iota((1, LANES), 1)
    set_row = jnp.zeros((1, LANES), F32)
    for n in range(NS_DEV):
        spot = NS_DEV * lax.rem(me, OWNERS_PER_ROW) + n
        set_row = jnp.where(lane == spot, (agr_ref[n] - me * AG_DEV).astype(F32), set_row)
    set_rows = jnp.where(iota((4, LANES), 0) == 0, set_row, 0.0)
    weight = weight_ref[...]
    dates = weight.shape[1]
    picked, lags = [], []
    for a in range(AG_DEV):
        row = weight[0:1]
        for c in range(1, weight.shape[0]):
            row = jnp.where(cpty_ref[a] - me * weight.shape[0] == c, weight[c : c + 1], row)
        picked.append(row)
        lags.append(jnp.full((1, LANES - 3 * dates), lag_ref[a].astype(F32)))
    picked = jnp.concatenate(picked, axis=0)
    table = jnp.concatenate(split_bf16(picked, 3) + [jnp.concatenate(lags, axis=0)], axis=1)
    tail = jnp.concatenate([high, low, set_rows, table], axis=0)
    out_ref[rows + LANES :, :] = tail.astype(BF16)


def basis_kernel(dates, paths, cols, me_ref, shocks_ref, start_ref, loading_ref, out_ref, wide_ref):
    me = me_ref[0]
    tenors = loading_ref.shape[0]
    wide_ref[...] = shocks_ref[...].astype(F32)
    lane = iota((tenors, LANES), 1)
    walk = jnp.zeros((tenors, LANES), F32)
    tiles = [jnp.zeros((tenors, LANES), F32) for _ in range(cols // LANES)]
    for s in range(dates):
        walk = walk + wide_ref[pl.ds(s, tenors, stride=dates), :]
        tile, offset = divmod(s * paths, LANES)
        moved = pltpu.roll(walk, lax.rem(offset + LANES - paths * me, LANES), 1)
        tiles[tile] = jnp.where((lane >= offset) & (lane < offset + paths), moved, tiles[tile])
    walk = jnp.concatenate(tiles, axis=1)
    loading_t = jnp.transpose(loading_ref[...])
    drift = 0.5 * STEP * jnp.sum(loading_t * loading_t, axis=1, keepdims=True)
    diag = iota((tenors, tenors), 0) == iota((tenors, tenors), 1)
    log_start = jnp.log(
        jnp.sum(jnp.where(diag, start_ref[...], 0.0), axis=1, keepdims=True)
    )
    moved = jnp.dot(
        loading_t, walk, precision=lax.Precision.HIGHEST, preferred_element_type=F32
    )
    date = (iota((1, cols), 1) // paths + 1).astype(F32)
    fwd = jnp.exp(log_start + (STEP**0.5) * moved - date * drift)
    lower = (iota((tenors, tenors), 1) <= iota((tenors, tenors), 0)).astype(F32)
    summed = jnp.dot(
        lower,
        jnp.log1p(STEP * fwd),
        precision=lax.Precision.HIGHEST,
        preferred_element_type=F32,
    )
    bond = jnp.exp(-summed)
    out_ref[0:tenors, :] = (bond * fwd / RATE_UNIT).astype(BF16)
    out_ref[tenors:, :] = bond.astype(BF16)


def main_kernel(
    owners, chunk, dates, paths, path_total, gath_ref, basis_ref, sets_ref, out_ref, val_ref, acc_ref
):
    groups = sets_ref.shape[0] // owners
    rows = groups * LANES
    cols = basis_ref.shape[1]
    extra = basis_ref.shape[0] - LANES
    agrs = owners * AG_DEV
    set_count = owners * NS_DEV
    chunks = owners // chunk
    span = chunk * LANES

    tail = rows + LANES
    set_rows = [jnp.zeros((1, LANES), F32) for _ in range(-(-owners // OWNERS_PER_ROW))]
    tables = []
    for b in range(owners):
        block = gath_ref[b, tail : tail + TAIL, :].astype(F32)
        set_rows[b // OWNERS_PER_ROW] = set_rows[b // OWNERS_PER_ROW] + block[8:9]
        tables.append(block[12:16])
    table = jnp.concatenate(tables, axis=0)
    lag = table[:, 3 * dates : 3 * dates + 1]
    spread = (
        (iota((3 * dates, cols), 0) % dates == iota((3 * dates, cols), 1) // paths)
    ).astype(F32).astype(BF16)
    weight = jnp.dot(
        table[:, 0 : 3 * dates].astype(BF16), spread, preferred_element_type=F32
    )

    def row_of(ref_rows, g):
        return jnp.concatenate([ref_rows[groups * b + g : groups * b + g + 1] for b in range(chunk)], axis=1)

    def hot_of(k, g):
        sets = sets_ref[pl.ds(pl.multiple_of(k * chunk * groups, 8), chunk * groups), :]
        sets = row_of(sets, g)
        local = jnp.zeros((8, span), F32)
        for q, row in enumerate(set_rows):
            width = min(LANES, set_count - q * LANES)
            hot = (iota((width, span), 0) + q * LANES == sets).astype(F32).astype(BF16)
            local = local + jnp.dot(
                jnp.broadcast_to(row[:, 0:width], (8, width)).astype(BF16),
                hot,
                preferred_element_type=F32,
            )
        agr = lax.shift_right_logical(sets, 3) * AG_DEV + local[0:1].astype(jnp.int32)
        return iota((agrs, span), 0) == agr

    acc_ref[...] = jnp.zeros_like(acc_ref)

    def price(k, g):
        block = pl.ds(k * chunk, chunk)
        left = gath_ref[block, LANES * g : LANES * (g + 1), :].reshape(span, LANES)
        right = gath_ref[block, rows : rows + LANES, :].reshape(span, LANES)
        parts = [basis_ref[0:LANES, :]]
        if g:
            parts.append(jnp.zeros((extra * g, cols), BF16))
        parts.append(basis_ref[LANES:, :])
        if g < groups - 1:
            parts.append(jnp.zeros((extra * (groups - 1 - g), cols), BF16))
        under = jnp.dot(
            jnp.concatenate([left, right], axis=1),
            jnp.concatenate(parts, axis=0),
            preferred_element_type=F32,
        )
        value = jnp.maximum(under, 0.0).astype(BF16)
        val_ref[k * groups + g] = value
        pieces = gath_ref[block, tail : tail + TAIL, :].astype(F32)
        high = jnp.concatenate([pieces[b, g : g + 1] for b in range(chunk)], axis=1)
        low = jnp.concatenate([pieces[b, groups + g : groups + g + 1] for b in range(chunk)], axis=1)
        hot = hot_of(k, g)
        left = jnp.concatenate([jnp.where(hot, high, 0.0), jnp.where(hot, low, 0.0)], axis=0)
        acc_ref[...] += jnp.dot(left.astype(BF16), value, preferred_element_type=F32)

    def price_chunk(k):
        for g in range(groups):
            price(k, g)

    run(chunks, price_chunk)

    agreement = acc_ref[0:agrs] + acc_ref[agrs:]
    lane = iota((1, cols), 1)
    lagged = jnp.zeros_like(agreement)
    for step in range(1, LAG_MAX + 1):
        back = pltpu.roll(agreement, step * paths, 1)
        lagged = jnp.where((lag == step) & (lane >= step * paths), back, lagged)
    excess = agreement - lagged
    root = jnp.sqrt(excess * excess + SMOOTH * SMOOTH)
    exposure = 0.5 * (excess + root)
    weighted = weight * (0.5 * (1.0 + excess / root))
    ahead = jnp.zeros_like(weighted)
    for step in range(1, LAG_MAX + 1):
        front = pltpu.roll(weighted, cols - step * paths, 1)
        ahead = jnp.where((lag == step) & (lane < cols - step * paths), front, ahead)
    grads = ((weighted - ahead) * (1.0 / path_total)).astype(BF16)
    spent = jnp.sum(weight * exposure, axis=1, keepdims=True) * (1.0 / path_total)

    def allocate_chunk(k):
        lines = []
        for g in range(groups):
            dots = lax.dot_general(
                grads, val_ref[k * groups + g], (((1,), (1,)), ((), ())), preferred_element_type=F32
            )
            lines.append(jnp.sum(jnp.where(hot_of(k, g), dots, 0.0), axis=0, keepdims=True))
        for b in range(chunk):
            alloc = [line[:, LANES * b : LANES * (b + 1)] for line in lines]
            out_ref[pl.ds(pl.multiple_of((k * chunk + b) * 8, 8), groups), :] = jnp.concatenate(alloc, axis=0)

    run(chunks, allocate_chunk)
    for b in range(owners):
        out_ref[8 * b + groups : 8 * b + groups + AG_DEV, :] = jnp.broadcast_to(
            spent[AG_DEV * b : AG_DEV * (b + 1)], (AG_DEV, LANES)
        )


def run(count, step):
    if count == 1:
        step(0)
    else:

        def loop_body(k, carry):
            step(k)
            return carry

        lax.fori_loop(0, count, loop_body, 0)


def body(
    shocks,
    forward_start,
    loading,
    coefficient,
    notional,
    ns_of_trade,
    agr_of_ns,
    cpty_of_agr,
    margin_lag,
    default_weight,
):
    owners = lax.axis_size("trade")
    path_total = float(shocks.shape[2] * lax.axis_size("path"))
    tenors, dates, path_dev = shocks.shape
    rows = coefficient.shape[0]
    groups = rows // LANES
    paths = path_dev // owners
    cols = max(dates * paths, LANES)
    chunk = min(owners, 8)
    me = lax.axis_index("trade").astype(jnp.int32).reshape(1)

    packed_rows = rows + LANES + TAIL
    packed = pl.pallas_call(
        pack_kernel,
        out_shape=jax.ShapeDtypeStruct((packed_rows, LANES), BF16),
        in_specs=[SMEM] * 4 + [VMEM] * 3,
        out_specs=VMEM,
        name="pack",
    )(
        me,
        agr_of_ns,
        cpty_of_agr,
        margin_lag,
        coefficient,
        notional.reshape(groups, LANES),
        default_weight,
    )
    gathered = lax.all_gather(packed, "trade", axis=0, tiled=False)

    basis = pl.pallas_call(
        functools.partial(basis_kernel, dates, paths, cols),
        out_shape=jax.ShapeDtypeStruct((2 * tenors, cols), BF16),
        in_specs=[SMEM] + [VMEM] * 3,
        out_specs=VMEM,
        scratch_shapes=[pltpu.VMEM((tenors * dates, path_dev), F32)],
        name="basis",
        compiler_params=pltpu.CompilerParams(vmem_limit_bytes=16 << 20),
        cost_estimate=pl.CostEstimate(
            flops=2 * 12 * tenors * tenors * cols, bytes_accessed=1 << 20, transcendentals=1 << 17
        ),
    )(me, shocks.reshape(tenors * dates, path_dev), forward_start.reshape(1, tenors), loading)

    need = 2 * owners * (packed_rows * LANES + rows * cols) + (12 << 20)
    partial = pl.pallas_call(
        functools.partial(main_kernel, owners, chunk, dates, paths, path_total),
        out_shape=jax.ShapeDtypeStruct((8 * owners, LANES), F32),
        in_specs=[VMEM] * 3,
        out_specs=VMEM,
        scratch_shapes=[
            pltpu.VMEM((owners * groups // chunk, chunk * LANES, cols), BF16),
            pltpu.VMEM((2 * owners * AG_DEV, cols), F32),
        ],
        name="value_and_allocate",
        compiler_params=pltpu.CompilerParams(vmem_limit_bytes=need),
    )(gathered, basis, ns_of_trade.reshape(owners * groups, LANES))

    total = lax.psum(partial, ("trade", "path"))
    own = lax.dynamic_slice_in_dim(total, 8 * me[0], 8, 0)
    allocation = own[0:groups].reshape(rows) * notional
    local = cpty_of_agr - me[0] * default_weight.shape[0]
    spent = own[groups : groups + AG_DEV, 0]
    picks = local[None, :] == jnp.arange(default_weight.shape[0], dtype=jnp.int32)[:, None]
    cva = jnp.sum(jnp.where(picks, spent[None, :], 0.0), axis=1)
    return (allocation, cva)


def solution(mesh):
    placed = (
        P(None, None, "path"),
        P(),
        P(),
        P("trade", None),
        P("trade"),
        P(),
        P("trade"),
        P("trade"),
        P("trade"),
        P("trade", None),
    )
    return jax.shard_map(
        body, mesh=mesh, in_specs=placed, out_specs=(P("trade"), P("trade")), check_vma=False
    )
```

```python
import functools

import jax
import jax.numpy as jnp
from jax import lax
from jax.experimental import pallas as pl
from jax.experimental.pallas import tpu as pltpu
from jax.sharding import PartitionSpec as P

NS_DEV = 8
AG_DEV = 4
LAG_MAX = 4
LANES = 128
SUBS = 8
DIRECT = 16

RATE_UNIT = 0.03
STEP = 0.25
SMOOTH = 0.5

F32 = jnp.float32
BF16 = jnp.bfloat16
VMEM = pl.BlockSpec(memory_space=pltpu.VMEM)
SMEM = pl.BlockSpec(memory_space=pltpu.SMEM)
BOTH_LANES = (((1,), (1,)), ((), ()))


def iota(shape, dim):
    return lax.broadcasted_iota(jnp.int32, shape, dim)


def mask_bf16(mask):
    return mask.astype(F32).astype(BF16)


def split_bf16(x, parts):
    pieces = []
    for _ in range(parts):
        piece = x.astype(BF16)
        pieces.append(piece)
        x = x - piece.astype(F32)
    return pieces


def in_a_row(x):
    return jnp.concatenate([x[r : r + 1] for r in range(x.shape[0])], axis=1)


class Plan:
    def __init__(self, owners, rows, tenors, dates):
        most = 3 * rows // (2 * owners)
        self.owners = owners
        self.direct = owners <= DIRECT
        self.groups = 3 if most % 48 == 0 else 1
        self.part = -(-most // (16 * self.groups)) * 16
        self.room = self.groups * self.part
        self.height = self.room + self.part
        self.extra = 2 * tenors - LANES
        self.per_line = LANES // self.part
        self.lines = owners * self.part // LANES
        self.trades = owners * self.room
        self.tile = -(-(self.groups * self.lines + 1) // SUBS) * SUBS
        self.dates = dates
        self.width = 512


def pack_kernel(plan, me_ref, sets_ref, coef_ref, notional_ref, place_ref, *out_refs):
    me = me_ref[0]
    owners, part, room, extra = plan.owners, plan.part, plan.room, plan.extra
    lines = notional_ref.shape[0]
    rows = lines * LANES
    shared = SUBS // lines
    block = sets_ref[pl.ds(pl.multiple_of(me // shared * SUBS, SUBS), SUBS), :]
    own = block[0:lines]
    for b in range(1, shared):
        own = jnp.where(lax.rem(me, shared) == b, block[b * lines : (b + 1) * lines], own)
    sets = in_a_row(own)
    key = lax.shift_right_logical(sets, 3)
    local = sets - key * NS_DEV
    if plan.direct:
        key = lax.bitwise_xor(key, me)
    hot = iota((owners, rows), 0) == key
    before = mask_bf16(iota((rows, rows), 0) < iota((rows, rows), 1))
    count = jnp.dot(mask_bf16(hot), before, preferred_element_type=F32)
    rank = jnp.sum(jnp.where(hot, count, 0.0), axis=0, keepdims=True)
    place_ref[...] = jnp.concatenate(
        [key.astype(F32), rank, jnp.zeros((SUBS - 2, rows), F32)], axis=0
    )
    spot = key * room + rank.astype(jnp.int32)
    chosen = mask_bf16(iota((owners * room, rows), 0) == spot)
    notional = in_a_row(notional_ref[...])
    high = notional.astype(BF16).astype(F32)
    info = jnp.concatenate(
        [high, notional - high, local.astype(F32), jnp.zeros((13, rows), F32)], axis=0
    )
    table = jnp.concatenate([coef_ref[...], info.astype(BF16)], axis=0)
    moved = lax.dot_general(chosen, table, BOTH_LANES, preferred_element_type=F32)
    ids = LANES + extra
    for d in range(owners):
        message = out_refs[d] if plan.direct else out_refs[0].at[d]
        block = moved[d * room : (d + 1) * room]
        message[0:room, :] = block[:, 0:LANES].astype(BF16)
        split = [block[part * g : part * (g + 1)] for g in range(plan.groups)]
        lanes = [x[:, LANES:ids] for x in split]
        if plan.groups < 3:
            lanes.append(jnp.zeros((part, extra * (3 - plan.groups)), F32))
        lanes += [x[:, ids : ids + SUBS] for x in split]
        lanes.append(jnp.zeros((part, SUBS * (4 - plan.groups)), F32))
        message[room:, :] = jnp.concatenate(lanes, axis=1).astype(BF16)


def basis_kernel(plan, shocks_ref, start_ref, loading_ref, out_ref, wide_ref):
    tenors = loading_ref.shape[0]
    dates = plan.dates
    wide_ref[...] = shocks_ref[...].astype(F32)
    loading_t = jnp.transpose(loading_ref[...])
    drift = 0.5 * STEP * jnp.sum(loading_t * loading_t, axis=1, keepdims=True)
    diag = iota((tenors, tenors), 0) == iota((tenors, tenors), 1)
    log_start = jnp.log(jnp.sum(jnp.where(diag, start_ref[...], 0.0), axis=1, keepdims=True))
    loads = jnp.concatenate(split_bf16((STEP**0.5) * loading_t, 3), axis=1)
    lower = mask_bf16(iota((tenors, tenors), 1) <= iota((tenors, tenors), 0))
    lower = jnp.concatenate([lower, lower], axis=1)
    log_fwd = jnp.broadcast_to(log_start, (tenors, LANES))
    drift = jnp.broadcast_to(drift, (tenors, LANES))
    head = LANES - tenors
    step = plan.width // LANES
    for c in range(dates // step):
        shock = jnp.concatenate(
            [
                wide_ref[pl.ds(c * step + j, tenors, stride=dates), :].astype(BF16)
                for j in range(step)
            ],
            axis=1,
        )
        change = jnp.dot(
            loads, jnp.concatenate([shock] * 3, axis=0), preferred_element_type=F32
        )
        logs = []
        for j in range(step):
            log_fwd = log_fwd + (change[:, LANES * j : LANES * (j + 1)] - drift)
            logs.append(log_fwd)
        fwd = jnp.exp(jnp.concatenate(logs, axis=1))
        growth = split_bf16(jnp.log(1.0 + STEP * fwd), 2)
        summed = jnp.dot(lower, jnp.concatenate(growth, axis=0), preferred_element_type=F32)
        bond = jnp.exp(-summed)
        cols = slice(c * plan.width, (c + 1) * plan.width)
        out_ref[0:tenors, cols] = (bond * fwd * (1.0 / RATE_UNIT)).astype(BF16)
        bond = bond.astype(BF16)
        out_ref[tenors:LANES, cols] = bond[0:head]
        for g in range(plan.groups):
            out_ref[LANES + plan.extra * g : LANES + plan.extra * (g + 1), cols] = bond[head:]
        used = LANES + plan.extra * plan.groups
        out_ref[used:, cols] = jnp.zeros((2 * LANES - used, plan.width), BF16)


def main_kernel(plan, path_total, me_ref, agr_ref, cpty_ref, lag_ref, weight_ref, basis_ref, *refs):
    *in_refs, out_ref, val_ref = refs
    me = me_ref[0]
    part, room, dates = plan.part, plan.room, plan.dates
    cpty_dev = weight_ref.shape[0]

    def rows_of(first):
        if plan.direct:
            return jnp.concatenate([ref[first : first + part, :] for ref in in_refs], axis=0)
        return in_refs[0][:, first : first + part, :].reshape(plan.owners * part, LANES)

    rest = rows_of(room)
    lane = iota((1, LANES), 1)
    left, info = [], []
    for g in range(plan.groups):
        keep = mask_bf16((lane >= plan.extra * g) & (lane < plan.extra * (g + 1)))
        left.append(jnp.concatenate([rows_of(part * g), rest * keep], axis=1))
        pick = mask_bf16(iota((SUBS, LANES), 1) == 3 * plan.extra + SUBS * g + iota((SUBS, LANES), 0))
        info.append(lax.dot_general(pick, rest, BOTH_LANES, preferred_element_type=F32))
    left = jnp.concatenate(left, axis=0)
    info = jnp.concatenate(info, axis=1)
    local = info[2:3].astype(jnp.int32)
    agr = jnp.zeros_like(local)
    for n in range(NS_DEV):
        agr = jnp.where(local == n, agr_ref[n] - me * AG_DEV, agr)
    row = iota((SUBS, plan.trades), 0)
    hot = lax.rem(row, AG_DEV) == agr
    netting = jnp.where(hot, jnp.where(row < AG_DEV, info[0:1], info[1:2]), 0.0).astype(BF16)

    owed = []
    width = plan.width
    chunks = dates * LANES // width
    for c in range(chunks):
        under = jnp.dot(
            left, basis_ref[:, c * width : (c + 1) * width], preferred_element_type=F32
        )
        value = jnp.maximum(under, 0.0).astype(BF16)
        val_ref[c] = value
        both = jnp.dot(netting, value, preferred_element_type=F32)
        both = both + pltpu.roll(both, AG_DEV, 0)
        owed += [both[:, LANES * j : LANES * (j + 1)] for j in range(width // LANES)]

    member = lax.rem(iota((SUBS, LANES), 0), AG_DEV)
    lag = jnp.zeros((SUBS, LANES), jnp.int32)
    cpty = jnp.zeros((SUBS, LANES), jnp.int32)
    for a in range(AG_DEV):
        lag = jnp.where(member == a, lag_ref[a], lag)
        cpty = jnp.where(member == a, cpty_ref[a] - me * cpty_dev, cpty)
    lags = [lag == s for s in range(1, LAG_MAX + 1)]
    weight = jnp.zeros((SUBS, dates), F32)
    for c in range(cpty_dev):
        weight = jnp.where(cpty[:, 0:dates] == c, weight_ref[c : c + 1, :], weight)
    zero = jnp.zeros((SUBS, LANES), F32)
    spent, slopes = zero, []
    for t in range(dates):
        before = zero
        for s in range(1, min(t, LAG_MAX) + 1):
            before = jnp.where(lags[s - 1], owed[t - s], before)
        excess = owed[t] - before
        square = excess * excess + SMOOTH * SMOOTH
        root = jnp.sqrt(square)
        due = weight[:, t : t + 1]
        spent = spent + due * (0.5 * (excess + root))
        slopes.append(due * (0.5 * (1.0 + excess / root)))
    grads = []
    for t in range(dates):
        after = zero
        for s in range(1, min(dates - 1 - t, LAG_MAX) + 1):
            after = jnp.where(lags[s - 1], slopes[t + s], after)
        grads.append(((slopes[t] - after) * (1.0 / path_total)).astype(BF16))

    dots = jnp.zeros((SUBS, plan.trades), F32)
    step = width // LANES
    for c in range(chunks):
        part_grads = jnp.concatenate(grads[c * step : (c + 1) * step], axis=1)
        dots = dots + lax.dot_general(
            part_grads, val_ref[c], BOTH_LANES, preferred_element_type=F32
        )
    share = jnp.sum(jnp.where(hot & (row < AG_DEV), dots, 0.0), axis=0, keepdims=True)
    lines = [share[:, LANES * k : LANES * (k + 1)] for k in range(plan.trades // LANES)]
    spent = jnp.sum(spent, axis=1, keepdims=True) * (1.0 / path_total)
    mine = (lane == cpty) & (iota((SUBS, LANES), 0) < AG_DEV)
    lines.append(jnp.sum(jnp.where(mine, spent, 0.0), axis=0, keepdims=True))
    if len(lines) < plan.tile:
        lines.append(jnp.zeros((plan.tile - len(lines), LANES), F32))
    out_ref[...] = jnp.concatenate(lines, axis=0)


def finish_kernel(plan, me_ref, place_ref, notional_ref, own_ref, *refs):
    *in_refs, alloc_ref, cva_ref = refs
    me = me_ref[0]
    part, per_line = plan.part, plan.per_line
    rows = place_ref.shape[1]
    key = place_ref[0:1, :].astype(jnp.int32)
    rank = place_ref[1:2, :].astype(jnp.int32)
    group = lax.div(rank, part)
    slot = key if plan.direct else jnp.full_like(key, me)
    line = group * plan.lines + lax.div(slot, per_line)
    lane = lax.rem(slot, per_line) * part + (rank - group * part)
    if plan.direct:
        tiles = jnp.concatenate([ref[...] for ref in in_refs], axis=0)
    else:
        tiles = in_refs[0][...].reshape(plan.owners * plan.tile, LANES)
    hot = mask_bf16(iota((LANES, rows), 0) == lane)
    found = jnp.zeros((tiles.shape[0], rows), F32)
    for piece in split_bf16(tiles, 3):
        found = found + jnp.dot(piece, hot, preferred_element_type=F32)
    wanted = iota(found.shape, 0) == key * plan.tile + line
    share = jnp.sum(jnp.where(wanted, found, 0.0), axis=0, keepdims=True)
    alloc_ref[...] = share * in_a_row(notional_ref[...])
    last = plan.groups * plan.lines
    cva_ref[...] = own_ref[last : last + 1, 0 : cva_ref.shape[1]]


def permuted(x, axis, size, d):
    return lax.ppermute(x, axis, [(i, i ^ d) for i in range(size)])


def body(
    shocks,
    forward_start,
    loading,
    coefficient,
    notional,
    ns_of_trade,
    agr_of_ns,
    cpty_of_agr,
    margin_lag,
    default_weight,
):
    owners = lax.axis_size("trade")
    path_parts = lax.axis_size("path")
    tenors, dates, path_dev = shocks.shape
    path_total = float(path_dev * path_parts)
    rows = coefficient.shape[0]
    lines = rows // LANES
    plan = Plan(owners, rows, tenors, dates)
    cols = dates * path_dev
    me = lax.axis_index("trade").astype(jnp.int32).reshape(1)
    notional = notional.reshape(lines, LANES)

    message = jax.ShapeDtypeStruct((plan.height, LANES), BF16)
    if plan.direct:
        messages = [message] * owners
    else:
        messages = [jax.ShapeDtypeStruct((owners,) + message.shape, BF16)]
    place, *outgoing = pl.pallas_call(
        functools.partial(pack_kernel, plan),
        out_shape=[jax.ShapeDtypeStruct((SUBS, rows), F32)] + messages,
        in_specs=[SMEM] + [VMEM] * 3,
        out_specs=[VMEM] * (1 + len(messages)),
        name="pack",
        compiler_params=pltpu.CompilerParams(vmem_limit_bytes=24 << 20),
    )(me, ns_of_trade.reshape(owners * lines, LANES), coefficient.T, notional)
    if plan.direct:
        incoming = [outgoing[0]] + [
            permuted(outgoing[d], "trade", owners, d) for d in range(1, owners)
        ]
    else:
        incoming = [lax.all_to_all(outgoing[0], "trade", split_axis=0, concat_axis=0, tiled=True)]

    basis = pl.pallas_call(
        functools.partial(basis_kernel, plan),
        out_shape=jax.ShapeDtypeStruct((2 * LANES, cols), BF16),
        in_specs=[VMEM] * 3,
        out_specs=VMEM,
        scratch_shapes=[pltpu.VMEM((tenors * dates, path_dev), F32)],
        name="basis",
        compiler_params=pltpu.CompilerParams(vmem_limit_bytes=16 << 20),
        cost_estimate=pl.CostEstimate(
            flops=2 * 400 * tenors * cols, bytes_accessed=4 << 20, transcendentals=3 * tenors * cols
        ),
    )(shocks.reshape(tenors * dates, path_dev), forward_start.reshape(1, tenors), loading)

    need = 2 * plan.trades * cols + 16 * plan.trades * plan.width + (8 << 20)
    tile = pl.pallas_call(
        functools.partial(main_kernel, plan, path_total),
        out_shape=jax.ShapeDtypeStruct((plan.tile, LANES), F32),
        in_specs=[SMEM] * 4 + [VMEM] * (2 + len(incoming)),
        out_specs=VMEM,
        scratch_shapes=[pltpu.VMEM((cols // plan.width, plan.trades, plan.width), BF16)],
        name="value_and_allocate",
        compiler_params=pltpu.CompilerParams(vmem_limit_bytes=need),
    )(me, agr_of_ns, cpty_of_agr, margin_lag, default_weight, basis, *incoming)

    others = [permuted(tile, "path", path_parts, d) for d in range(1, path_parts)]
    for other in others:
        tile = tile + other
    if plan.direct:
        tiles = [tile] + [permuted(tile, "trade", owners, d) for d in range(1, owners)]
    else:
        tiles = [lax.all_gather(tile, "trade", axis=0, tiled=False)]
    allocation, cva = pl.pallas_call(
        functools.partial(finish_kernel, plan),
        out_shape=[
            jax.ShapeDtypeStruct((1, rows), F32),
            jax.ShapeDtypeStruct((1, default_weight.shape[0]), F32),
        ],
        in_specs=[SMEM] + [VMEM] * (3 + len(tiles)),
        out_specs=[VMEM, VMEM],
        name="finish",
        compiler_params=pltpu.CompilerParams(vmem_limit_bytes=32 << 20),
    )(me, place, notional, tile, *tiles)
    return (allocation.reshape(rows), cva.reshape(default_weight.shape[0]))


def solution(mesh):
    placed = (
        P(None, None, "path"),
        P(),
        P(),
        P("trade", None),
        P("trade"),
        P(),
        P("trade"),
        P("trade"),
        P("trade"),
        P("trade", None),
    )
    return jax.shard_map(
        body, mesh=mesh, in_specs=placed, out_specs=(P("trade"), P("trade")), check_vma=False
    )
```

```python
import functools

import jax
import jax.numpy as jnp
from jax import lax
from jax.experimental import pallas as pl
from jax.experimental.pallas import tpu as pltpu
from jax.sharding import PartitionSpec as P

NS_DEV = 8
AG_DEV = 4
LAG_MAX = 4
LANES = 128
SUBS = 8
DIRECT = 0

RATE_UNIT = 0.03
STEP = 0.25
SMOOTH = 0.5

F32 = jnp.float32
BF16 = jnp.bfloat16
VMEM = pl.BlockSpec(memory_space=pltpu.VMEM)
SMEM = pl.BlockSpec(memory_space=pltpu.SMEM)
HBM = pl.BlockSpec(memory_space=pltpu.HBM)
BOTH_LANES = (((1,), (1,)), ((), ()))


def iota(shape, dim):
    return lax.broadcasted_iota(jnp.int32, shape, dim)


def mask_bf16(mask):
    return mask.astype(F32).astype(BF16)


def split_bf16(x, parts):
    pieces = []
    for _ in range(parts):
        piece = x.astype(BF16)
        pieces.append(piece)
        x = x - piece.astype(F32)
    return pieces


def fetch(sources, targets, sems):
    copies = [pltpu.make_async_copy(a, b, sems.at[n]) for n, (a, b) in enumerate(zip(sources, targets))]
    for copy in copies:
        copy.start()
    return copies


def in_a_row(x):
    return jnp.concatenate([x[r : r + 1] for r in range(x.shape[0])], axis=1)


class Plan:
    def __init__(self, owners, rows, tenors, dates):
        most = 3 * rows // (2 * owners)
        self.owners = owners
        self.direct = owners <= DIRECT
        self.groups = 3 if most % 48 == 0 else 1
        self.part = -(-most // (16 * self.groups)) * 16
        self.room = self.groups * self.part
        self.height = self.room + self.part
        self.extra = 2 * tenors - LANES
        self.per_line = LANES // self.part
        self.lines = owners * self.part // LANES
        self.trades = owners * self.room
        self.tile = -(-(self.groups * self.lines + 1) // SUBS) * SUBS
        self.dates = dates
        self.width = 512


def pack_kernel(plan, me_ref, sets_hbm, coef_hbm, notional_hbm, place_ref, *refs):
    *out_refs, sets_ref, coef_ref, notional_ref, sems = refs
    copies = fetch(
        [sets_hbm, notional_hbm, coef_hbm], [sets_ref, notional_ref, coef_ref], sems
    )
    me = me_ref[0]
    owners, part, room, extra = plan.owners, plan.part, plan.room, plan.extra
    lines = notional_ref.shape[0]
    rows = lines * LANES
    shared = SUBS // lines
    copies[0].wait()
    block = sets_ref[pl.ds(pl.multiple_of(me // shared * SUBS, SUBS), SUBS), :]
    own = block[0:lines]
    for b in range(1, shared):
        own = jnp.where(lax.rem(me, shared) == b, block[b * lines : (b + 1) * lines], own)
    sets = in_a_row(own)
    key = lax.shift_right_logical(sets, 3)
    local = sets - key * NS_DEV
    if plan.direct:
        key = lax.bitwise_xor(key, me)
    hot = iota((owners, rows), 0) == key
    before = mask_bf16(iota((rows, rows), 0) < iota((rows, rows), 1))
    count = jnp.dot(mask_bf16(hot), before, preferred_element_type=F32)
    rank = jnp.sum(jnp.where(hot, count, 0.0), axis=0, keepdims=True)
    place_ref[...] = jnp.concatenate(
        [key.astype(F32), rank, jnp.zeros((SUBS - 2, rows), F32)], axis=0
    )
    spot = key * room + rank.astype(jnp.int32)
    chosen = mask_bf16(iota((owners * room, rows), 0) == spot)
    copies[1].wait()
    notional = in_a_row(notional_ref[...])
    high = notional.astype(BF16).astype(F32)
    info = jnp.concatenate(
        [high, notional - high, local.astype(F32), jnp.zeros((13, rows), F32)], axis=0
    )
    copies[2].wait()
    table = jnp.concatenate([coef_ref[...], info.astype(BF16)], axis=0)
    moved = lax.dot_general(chosen, table, BOTH_LANES, preferred_element_type=F32)
    ids = LANES + extra
    for d in range(owners):
        message = out_refs[d] if plan.direct else out_refs[0].at[d]
        block = moved[d * room : (d + 1) * room]
        message[0:room, :] = block[:, 0:LANES].astype(BF16)
        split = [block[part * g : part * (g + 1)] for g in range(plan.groups)]
        lanes = [x[:, LANES:ids] for x in split]
        if plan.groups < 3:
            lanes.append(jnp.zeros((part, extra * (3 - plan.groups)), F32))
        lanes += [x[:, ids : ids + SUBS] for x in split]
        lanes.append(jnp.zeros((part, SUBS * (4 - plan.groups)), F32))
        message[room:, :] = jnp.concatenate(lanes, axis=1).astype(BF16)


def basis_kernel(plan, shocks_hbm, start_hbm, loading_hbm, out_ref, *refs):
    shocks_ref, start_ref, loading_ref, wide_ref, sems = refs
    copies = fetch(
        [loading_hbm, start_hbm, shocks_hbm], [loading_ref, start_ref, shocks_ref], sems
    )
    tenors = loading_ref.shape[0]
    dates = plan.dates
    copies[0].wait()
    copies[1].wait()
    loading_t = jnp.transpose(loading_ref[...])
    drift = 0.5 * STEP * jnp.sum(loading_t * loading_t, axis=1, keepdims=True)
    diag = iota((tenors, tenors), 0) == iota((tenors, tenors), 1)
    log_start = jnp.log(jnp.sum(jnp.where(diag, start_ref[...], 0.0), axis=1, keepdims=True))
    loads = jnp.concatenate(split_bf16((STEP**0.5) * loading_t, 3), axis=1)
    lower = mask_bf16(iota((tenors, tenors), 1) <= iota((tenors, tenors), 0))
    lower = jnp.concatenate([lower, lower], axis=1)
    log_fwd = jnp.broadcast_to(log_start, (tenors, LANES))
    drift = jnp.broadcast_to(drift, (tenors, LANES))
    head = LANES - tenors
    copies[2].wait()
    wide_ref[...] = shocks_ref[...].astype(F32)
    step = plan.width // LANES
    for c in range(dates // step):
        shock = jnp.concatenate(
            [
                wide_ref[pl.ds(c * step + j, tenors, stride=dates), :].astype(BF16)
                for j in range(step)
            ],
            axis=1,
        )
        change = jnp.dot(
            loads, jnp.concatenate([shock] * 3, axis=0), preferred_element_type=F32
        )
        logs = []
        for j in range(step):
            log_fwd = log_fwd + (change[:, LANES * j : LANES * (j + 1)] - drift)
            logs.append(log_fwd)
        fwd = jnp.exp(jnp.concatenate(logs, axis=1))
        growth = split_bf16(jnp.log(1.0 + STEP * fwd), 2)
        summed = jnp.dot(lower, jnp.concatenate(growth, axis=0), preferred_element_type=F32)
        bond = jnp.exp(-summed)
        cols = slice(c * plan.width, (c + 1) * plan.width)
        out_ref[0:tenors, cols] = (bond * fwd * (1.0 / RATE_UNIT)).astype(BF16)
        bond = bond.astype(BF16)
        out_ref[tenors:LANES, cols] = bond[0:head]
        for g in range(plan.groups):
            out_ref[LANES + plan.extra * g : LANES + plan.extra * (g + 1), cols] = bond[head:]
        used = LANES + plan.extra * plan.groups
        out_ref[used:, cols] = jnp.zeros((2 * LANES - used, plan.width), BF16)


def main_kernel(plan, path_total, me_ref, agr_ref, cpty_ref, lag_ref, weight_ref, basis_ref, *refs):
    *in_refs, out_ref, val_ref = refs
    me = me_ref[0]
    part, room, dates = plan.part, plan.room, plan.dates
    cpty_dev = weight_ref.shape[0]

    def rows_of(first):
        if plan.direct:
            return jnp.concatenate([ref[first : first + part, :] for ref in in_refs], axis=0)
        return in_refs[0][:, first : first + part, :].reshape(plan.owners * part, LANES)

    rest = rows_of(room)
    lane = iota((1, LANES), 1)
    left, info = [], []
    for g in range(plan.groups):
        keep = mask_bf16((lane >= plan.extra * g) & (lane < plan.extra * (g + 1)))
        left.append(jnp.concatenate([rows_of(part * g), rest * keep], axis=1))
        pick = mask_bf16(iota((SUBS, LANES), 1) == 3 * plan.extra + SUBS * g + iota((SUBS, LANES), 0))
        info.append(lax.dot_general(pick, rest, BOTH_LANES, preferred_element_type=F32))
    left = jnp.concatenate(left, axis=0)
    info = jnp.concatenate(info, axis=1)
    local = info[2:3].astype(jnp.int32)
    agr = jnp.zeros_like(local)
    for n in range(NS_DEV):
        agr = jnp.where(local == n, agr_ref[n] - me * AG_DEV, agr)
    row = iota((SUBS, plan.trades), 0)
    hot = lax.rem(row, AG_DEV) == agr
    netting = jnp.where(hot, jnp.where(row < AG_DEV, info[0:1], info[1:2]), 0.0).astype(BF16)

    owed = []
    width = plan.width
    chunks = dates * LANES // width
    for c in range(chunks):
        under = jnp.dot(
            left, basis_ref[:, c * width : (c + 1) * width], preferred_element_type=F32
        )
        value = jnp.maximum(under, 0.0).astype(BF16)
        val_ref[c] = value
        both = jnp.dot(netting, value, preferred_element_type=F32)
        both = both + pltpu.roll(both, AG_DEV, 0)
        owed += [both[:, LANES * j : LANES * (j + 1)] for j in range(width // LANES)]

    member = lax.rem(iota((SUBS, LANES), 0), AG_DEV)
    lag = jnp.zeros((SUBS, LANES), jnp.int32)
    cpty = jnp.zeros((SUBS, LANES), jnp.int32)
    for a in range(AG_DEV):
        lag = jnp.where(member == a, lag_ref[a], lag)
        cpty = jnp.where(member == a, cpty_ref[a] - me * cpty_dev, cpty)
    lags = [lag == s for s in range(1, LAG_MAX + 1)]
    weight = jnp.zeros((SUBS, dates), F32)
    for c in range(cpty_dev):
        weight = jnp.where(cpty[:, 0:dates] == c, weight_ref[c : c + 1, :], weight)
    zero = jnp.zeros((SUBS, LANES), F32)
    spent, slopes = zero, []
    for t in range(dates):
        before = zero
        for s in range(1, min(t, LAG_MAX) + 1):
            before = jnp.where(lags[s - 1], owed[t - s], before)
        excess = owed[t] - before
        square = excess * excess + SMOOTH * SMOOTH
        root = jnp.sqrt(square)
        due = weight[:, t : t + 1]
        spent = spent + due * (0.5 * (excess + root))
        slopes.append(due * (0.5 * (1.0 + excess / root)))
    grads = []
    for t in range(dates):
        after = zero
        for s in range(1, min(dates - 1 - t, LAG_MAX) + 1):
            after = jnp.where(lags[s - 1], slopes[t + s], after)
        grads.append(((slopes[t] - after) * (1.0 / path_total)).astype(BF16))

    dots = jnp.zeros((SUBS, plan.trades), F32)
    step = width // LANES
    for c in range(chunks):
        part_grads = jnp.concatenate(grads[c * step : (c + 1) * step], axis=1)
        dots = dots + lax.dot_general(
            part_grads, val_ref[c], BOTH_LANES, preferred_element_type=F32
        )
    share = jnp.sum(jnp.where(hot & (row < AG_DEV), dots, 0.0), axis=0, keepdims=True)
    lines = [share[:, LANES * k : LANES * (k + 1)] for k in range(plan.trades // LANES)]
    spent = jnp.sum(spent, axis=1, keepdims=True) * (1.0 / path_total)
    mine = (lane == cpty) & (iota((SUBS, LANES), 0) < AG_DEV)
    lines.append(jnp.sum(jnp.where(mine, spent, 0.0), axis=0, keepdims=True))
    if len(lines) < plan.tile:
        lines.append(jnp.zeros((plan.tile - len(lines), LANES), F32))
    out_ref[...] = jnp.concatenate(lines, axis=0)


def finish_kernel(plan, me_ref, place_ref, notional_ref, own_ref, *refs):
    *in_refs, alloc_ref, cva_ref = refs
    me = me_ref[0]
    part, per_line = plan.part, plan.per_line
    rows = place_ref.shape[1]
    key = place_ref[0:1, :].astype(jnp.int32)
    rank = place_ref[1:2, :].astype(jnp.int32)
    group = lax.div(rank, part)
    slot = key if plan.direct else jnp.full_like(key, me)
    line = group * plan.lines + lax.div(slot, per_line)
    lane = lax.rem(slot, per_line) * part + (rank - group * part)
    if plan.direct:
        tiles = jnp.concatenate([ref[...] for ref in in_refs], axis=0)
    else:
        tiles = in_refs[0][...].reshape(plan.owners * plan.tile, LANES)
    hot = mask_bf16(iota((LANES, rows), 0) == lane)
    found = jnp.zeros((tiles.shape[0], rows), F32)
    for piece in split_bf16(tiles, 3):
        found = found + jnp.dot(piece, hot, preferred_element_type=F32)
    wanted = iota(found.shape, 0) == key * plan.tile + line
    share = jnp.sum(jnp.where(wanted, found, 0.0), axis=0, keepdims=True)
    alloc_ref[...] = share * in_a_row(notional_ref[...])
    last = plan.groups * plan.lines
    cva_ref[...] = own_ref[last : last + 1, 0 : cva_ref.shape[1]]


def permuted(x, axis, size, d):
    return lax.ppermute(x, axis, [(i, i ^ d) for i in range(size)])


def body(
    shocks,
    forward_start,
    loading,
    coefficient,
    notional,
    ns_of_trade,
    agr_of_ns,
    cpty_of_agr,
    margin_lag,
    default_weight,
):
    owners = lax.axis_size("trade")
    path_parts = lax.axis_size("path")
    tenors, dates, path_dev = shocks.shape
    path_total = float(path_dev * path_parts)
    rows = coefficient.shape[0]
    lines = rows // LANES
    plan = Plan(owners, rows, tenors, dates)
    cols = dates * path_dev
    me = lax.axis_index("trade").astype(jnp.int32).reshape(1)
    notional = notional.reshape(lines, LANES)

    message = jax.ShapeDtypeStruct((plan.height, LANES), BF16)
    if plan.direct:
        messages = [message] * owners
    else:
        messages = [jax.ShapeDtypeStruct((owners,) + message.shape, BF16)]
    place, *outgoing = pl.pallas_call(
        functools.partial(pack_kernel, plan),
        out_shape=[jax.ShapeDtypeStruct((SUBS, rows), F32)] + messages,
        in_specs=[SMEM] + [HBM] * 3,
        out_specs=[VMEM] * (1 + len(messages)),
        scratch_shapes=[
            pltpu.VMEM((owners * lines, LANES), jnp.int32),
            pltpu.VMEM((2 * tenors, rows), BF16),
            pltpu.VMEM((lines, LANES), F32),
            pltpu.SemaphoreType.DMA((3,)),
        ],
        name="pack",
    )(me, ns_of_trade.reshape(owners * lines, LANES), coefficient.T, notional)
    if plan.direct:
        incoming = [outgoing[0]] + [
            permuted(outgoing[d], "trade", owners, d) for d in range(1, owners)
        ]
    else:
        incoming = [lax.all_to_all(outgoing[0], "trade", split_axis=0, concat_axis=0, tiled=True)]

    basis = pl.pallas_call(
        functools.partial(basis_kernel, plan),
        out_shape=jax.ShapeDtypeStruct((2 * LANES, cols), BF16),
        in_specs=[HBM] * 3,
        out_specs=VMEM,
        scratch_shapes=[
            pltpu.VMEM((tenors * dates, path_dev), BF16),
            pltpu.VMEM((1, tenors), F32),
            pltpu.VMEM((tenors, tenors), F32),
            pltpu.VMEM((tenors * dates, path_dev), F32),
            pltpu.SemaphoreType.DMA((3,)),
        ],
        name="basis",
        cost_estimate=pl.CostEstimate(
            flops=2 * 400 * tenors * cols, bytes_accessed=4 << 20, transcendentals=3 * tenors * cols
        ),
    )(shocks.reshape(tenors * dates, path_dev), forward_start.reshape(1, tenors), loading)

    need = 2 * plan.trades * cols + 16 * plan.trades * plan.width + (8 << 20)
    tile = pl.pallas_call(
        functools.partial(main_kernel, plan, path_total),
        out_shape=jax.ShapeDtypeStruct((plan.tile, LANES), F32),
        in_specs=[SMEM] * 4 + [VMEM] * (2 + len(incoming)),
        out_specs=VMEM,
        scratch_shapes=[pltpu.VMEM((cols // plan.width, plan.trades, plan.width), BF16)],
        name="value_and_allocate",
        compiler_params=pltpu.CompilerParams(vmem_limit_bytes=need),
    )(me, agr_of_ns, cpty_of_agr, margin_lag, default_weight, basis, *incoming)

    others = [permuted(tile, "path", path_parts, d) for d in range(1, path_parts)]
    for other in others:
        tile = tile + other
    if plan.direct:
        tiles = [tile] + [permuted(tile, "trade", owners, d) for d in range(1, owners)]
    else:
        spread = jnp.broadcast_to(tile, (owners,) + tile.shape)
        tiles = [lax.all_to_all(spread, "trade", split_axis=0, concat_axis=0, tiled=True)]
    allocation, cva = pl.pallas_call(
        functools.partial(finish_kernel, plan),
        out_shape=[
            jax.ShapeDtypeStruct((1, rows), F32),
            jax.ShapeDtypeStruct((1, default_weight.shape[0]), F32),
        ],
        in_specs=[SMEM] + [VMEM] * (3 + len(tiles)),
        out_specs=[VMEM, VMEM],
        name="finish",
        compiler_params=pltpu.CompilerParams(vmem_limit_bytes=32 << 20),
    )(me, place, notional, tile, *tiles)
    return (allocation.reshape(rows), cva.reshape(default_weight.shape[0]))


def solution(mesh):
    placed = (
        P(None, None, "path"),
        P(),
        P(),
        P("trade", None),
        P("trade"),
        P(),
        P("trade"),
        P("trade"),
        P("trade"),
        P("trade", None),
    )
    return jax.shard_map(
        body, mesh=mesh, in_specs=placed, out_specs=(P("trade"), P("trade")), check_vma=False
    )
```

```python
import functools

import jax
import jax.numpy as jnp
from jax import lax
from jax.experimental import pallas as pl
from jax.experimental.pallas import tpu as pltpu
from jax.sharding import PartitionSpec as P

NS_DEV = 8
AG_DEV = 4
LAG_MAX = 4
LANES = 128
SUBS = 8
DIRECT = 8

RATE_UNIT = 0.03
STEP = 0.25
SMOOTH = 0.5

F32 = jnp.float32
BF16 = jnp.bfloat16
VMEM = pl.BlockSpec(memory_space=pltpu.VMEM)
SMEM = pl.BlockSpec(memory_space=pltpu.SMEM)
HBM = pl.BlockSpec(memory_space=pltpu.HBM)
BOTH_LANES = (((1,), (1,)), ((), ()))


def iota(shape, dim):
    return lax.broadcasted_iota(jnp.int32, shape, dim)


def mask_bf16(mask):
    return mask.astype(F32).astype(BF16)


def split_bf16(x, parts):
    pieces = []
    for _ in range(parts):
        piece = x.astype(BF16)
        pieces.append(piece)
        x = x - piece.astype(F32)
    return pieces


def fetch(sources, targets, sems):
    copies = [pltpu.make_async_copy(a, b, sems.at[n]) for n, (a, b) in enumerate(zip(sources, targets))]
    for copy in copies:
        copy.start()
    return copies


def in_a_row(x):
    return jnp.concatenate([x[r : r + 1] for r in range(x.shape[0])], axis=1)


class Plan:
    def __init__(self, owners, rows, tenors, dates):
        most = 3 * rows // (2 * owners)
        self.owners = owners
        self.direct = owners <= DIRECT
        self.groups = 3 if most % 48 == 0 else 1
        self.part = -(-most // (16 * self.groups)) * 16
        self.room = self.groups * self.part
        self.height = self.room + self.part
        self.extra = 2 * tenors - LANES
        self.per_line = LANES // self.part
        self.lines = owners * self.part // LANES
        self.trades = owners * self.room
        self.tile = -(-(self.groups * self.lines + 1) // SUBS) * SUBS
        self.dates = dates
        self.width = 512


def pack_kernel(
    plan,
    me_ref,
    sets_hbm,
    coef_hbm,
    notional_hbm,
    place_ref,
    out_hbm,
    out_ref,
    sets_ref,
    coef_ref,
    notional_ref,
    sems,
    out_sems,
):
    copies = fetch(
        [sets_hbm, notional_hbm, coef_hbm], [sets_ref, notional_ref, coef_ref], sems
    )
    me = me_ref[0]
    owners, part, room, extra = plan.owners, plan.part, plan.room, plan.extra
    lines = notional_ref.shape[0]
    rows = lines * LANES
    shared = SUBS // lines
    copies[0].wait()
    block = sets_ref[pl.ds(pl.multiple_of(me // shared * SUBS, SUBS), SUBS), :]
    own = block[0:lines]
    for b in range(1, shared):
        own = jnp.where(lax.rem(me, shared) == b, block[b * lines : (b + 1) * lines], own)
    sets = in_a_row(own)
    key = lax.shift_right_logical(sets, 3)
    local = sets - key * NS_DEV
    hot = iota((owners, rows), 0) == key
    before = mask_bf16(iota((rows, rows), 0) < iota((rows, rows), 1))
    count = jnp.dot(mask_bf16(hot), before, preferred_element_type=F32)
    rank = jnp.sum(jnp.where(hot, count, 0.0), axis=0, keepdims=True)
    place_ref[...] = jnp.concatenate(
        [key.astype(F32), rank, jnp.zeros((SUBS - 2, rows), F32)], axis=0
    )
    spot = key * room + rank.astype(jnp.int32)
    chosen = mask_bf16(iota((owners * room, rows), 0) == spot)
    copies[1].wait()
    notional = in_a_row(notional_ref[...])
    high = notional.astype(BF16).astype(F32)
    info = jnp.concatenate(
        [high, notional - high, local.astype(F32), jnp.zeros((13, rows), F32)], axis=0
    )
    copies[2].wait()
    table = jnp.concatenate([coef_ref[...], info.astype(BF16)], axis=0)
    moved = lax.dot_general(chosen, table, BOTH_LANES, preferred_element_type=F32)
    ids = LANES + extra
    for d in range(owners):
        message = out_ref.at[d]
        block = moved[d * room : (d + 1) * room]
        message[0:room, :] = block[:, 0:LANES].astype(BF16)
        split = [block[part * g : part * (g + 1)] for g in range(plan.groups)]
        lanes = [x[:, LANES:ids] for x in split]
        if plan.groups < 3:
            lanes.append(jnp.zeros((part, extra * (3 - plan.groups)), F32))
        lanes += [x[:, ids : ids + SUBS] for x in split]
        lanes.append(jnp.zeros((part, SUBS * (4 - plan.groups)), F32))
        message[room:, :] = jnp.concatenate(lanes, axis=1).astype(BF16)
        pltpu.make_async_copy(message, out_hbm.at[d], out_sems.at[d]).start()
    for d in range(owners):
        pltpu.make_async_copy(out_ref.at[d], out_hbm.at[d], out_sems.at[d]).wait()


def basis_kernel(plan, shocks_hbm, start_hbm, loading_hbm, out_hbm, *refs):
    out_ref, shocks_ref, start_ref, loading_ref, wide_ref, sems, out_sems = refs
    copies = fetch(
        [loading_hbm, start_hbm, shocks_hbm], [loading_ref, start_ref, shocks_ref], sems
    )
    tenors = loading_ref.shape[0]
    dates = plan.dates
    copies[0].wait()
    copies[1].wait()
    loading_t = jnp.transpose(loading_ref[...])
    drift = 0.5 * STEP * jnp.sum(loading_t * loading_t, axis=1, keepdims=True)
    diag = iota((tenors, tenors), 0) == iota((tenors, tenors), 1)
    log_start = jnp.log(jnp.sum(jnp.where(diag, start_ref[...], 0.0), axis=1, keepdims=True))
    loads = jnp.concatenate(split_bf16((STEP**0.5) * loading_t, 3), axis=1)
    lower = mask_bf16(iota((tenors, tenors), 1) <= iota((tenors, tenors), 0))
    lower = jnp.concatenate([lower, lower], axis=1)
    log_fwd = jnp.broadcast_to(log_start, (tenors, LANES))
    drift = jnp.broadcast_to(drift, (tenors, LANES))
    head = LANES - tenors
    copies[2].wait()
    wide_ref[...] = shocks_ref[...].astype(F32)
    step = plan.width // LANES
    for c in range(dates // step):
        shock = jnp.concatenate(
            [
                wide_ref[pl.ds(c * step + j, tenors, stride=dates), :].astype(BF16)
                for j in range(step)
            ],
            axis=1,
        )
        change = jnp.dot(
            loads, jnp.concatenate([shock] * 3, axis=0), preferred_element_type=F32
        )
        logs = []
        for j in range(step):
            log_fwd = log_fwd + (change[:, LANES * j : LANES * (j + 1)] - drift)
            logs.append(log_fwd)
        fwd = jnp.exp(jnp.concatenate(logs, axis=1))
        growth = split_bf16(jnp.log(1.0 + STEP * fwd), 2)
        summed = jnp.dot(lower, jnp.concatenate(growth, axis=0), preferred_element_type=F32)
        bond = jnp.exp(-summed)
        out_ref[c, 0:tenors] = (bond * fwd * (1.0 / RATE_UNIT)).astype(BF16)
        bond = bond.astype(BF16)
        out_ref[c, tenors:LANES] = bond[0:head]
        for g in range(plan.groups):
            out_ref[c, LANES + plan.extra * g : LANES + plan.extra * (g + 1)] = bond[head:]
        used = LANES + plan.extra * plan.groups
        out_ref[c, used:] = jnp.zeros((2 * LANES - used, plan.width), BF16)
        pltpu.make_async_copy(out_ref.at[c], out_hbm.at[c], out_sems.at[c]).start()
    for c in range(dates // step):
        pltpu.make_async_copy(out_ref.at[c], out_hbm.at[c], out_sems.at[c]).wait()


def main_kernel(
    plan,
    path_total,
    me_ref,
    agr_ref,
    cpty_ref,
    lag_ref,
    weight_ref,
    in_ref,
    basis_hbm,
    out_ref,
    val_ref,
    basis_ref,
    sems,
):
    chunks = basis_hbm.shape[0]
    copies = fetch(
        [basis_hbm.at[c] for c in range(chunks)], [basis_ref.at[c] for c in range(chunks)], sems
    )
    me = me_ref[0]
    part, room, dates = plan.part, plan.room, plan.dates
    cpty_dev = weight_ref.shape[0]

    def rows_of(first):
        return in_ref[:, first : first + part, :].reshape(plan.owners * part, LANES)

    rest = rows_of(room)
    lane = iota((1, LANES), 1)
    left, info = [], []
    for g in range(plan.groups):
        keep = mask_bf16((lane >= plan.extra * g) & (lane < plan.extra * (g + 1)))
        left.append(jnp.concatenate([rows_of(part * g), rest * keep], axis=1))
        pick = mask_bf16(iota((SUBS, LANES), 1) == 3 * plan.extra + SUBS * g + iota((SUBS, LANES), 0))
        info.append(lax.dot_general(pick, rest, BOTH_LANES, preferred_element_type=F32))
    left = jnp.concatenate(left, axis=0)
    info = jnp.concatenate(info, axis=1)
    local = info[2:3].astype(jnp.int32)
    agr = jnp.zeros_like(local)
    for n in range(NS_DEV):
        agr = jnp.where(local == n, agr_ref[n] - me * AG_DEV, agr)
    row = iota((SUBS, plan.trades), 0)
    hot = lax.rem(row, AG_DEV) == agr
    netting = jnp.where(hot, jnp.where(row < AG_DEV, info[0:1], info[1:2]), 0.0).astype(BF16)

    owed = []
    width = plan.width
    for c in range(chunks):
        copies[c].wait()
        under = jnp.dot(left, basis_ref[c], preferred_element_type=F32)
        value = jnp.maximum(under, 0.0).astype(BF16)
        val_ref[c] = value
        both = jnp.dot(netting, value, preferred_element_type=F32)
        both = both + pltpu.roll(both, AG_DEV, 0)
        owed += [both[:, LANES * j : LANES * (j + 1)] for j in range(width // LANES)]

    member = lax.rem(iota((SUBS, LANES), 0), AG_DEV)
    lag = jnp.zeros((SUBS, LANES), jnp.int32)
    cpty = jnp.zeros((SUBS, LANES), jnp.int32)
    for a in range(AG_DEV):
        lag = jnp.where(member == a, lag_ref[a], lag)
        cpty = jnp.where(member == a, cpty_ref[a] - me * cpty_dev, cpty)
    lags = [lag == s for s in range(1, LAG_MAX + 1)]
    weight = jnp.zeros((SUBS, dates), F32)
    for c in range(cpty_dev):
        weight = jnp.where(cpty[:, 0:dates] == c, weight_ref[c : c + 1, :], weight)
    zero = jnp.zeros((SUBS, LANES), F32)
    spent, slopes = zero, []
    for t in range(dates):
        before = zero
        for s in range(1, min(t, LAG_MAX) + 1):
            before = jnp.where(lags[s - 1], owed[t - s], before)
        excess = owed[t] - before
        square = excess * excess + SMOOTH * SMOOTH
        root = jnp.sqrt(square)
        due = weight[:, t : t + 1]
        spent = spent + due * (0.5 * (excess + root))
        slopes.append(due * (0.5 * (1.0 + excess / root)))
    grads = []
    for t in range(dates):
        after = zero
        for s in range(1, min(dates - 1 - t, LAG_MAX) + 1):
            after = jnp.where(lags[s - 1], slopes[t + s], after)
        grads.append(((slopes[t] - after) * (1.0 / path_total)).astype(BF16))

    dots = jnp.zeros((SUBS, plan.trades), F32)
    step = width // LANES
    for c in range(chunks):
        part_grads = jnp.concatenate(grads[c * step : (c + 1) * step], axis=1)
        dots = dots + lax.dot_general(
            part_grads, val_ref[c], BOTH_LANES, preferred_element_type=F32
        )
    share = jnp.sum(jnp.where(hot & (row < AG_DEV), dots, 0.0), axis=0, keepdims=True)
    lines = [share[:, LANES * k : LANES * (k + 1)] for k in range(plan.trades // LANES)]
    spent = jnp.sum(spent, axis=1, keepdims=True) * (1.0 / path_total)
    mine = (lane == cpty) & (iota((SUBS, LANES), 0) < AG_DEV)
    lines.append(jnp.sum(jnp.where(mine, spent, 0.0), axis=0, keepdims=True))
    if len(lines) < plan.tile:
        lines.append(jnp.zeros((plan.tile - len(lines), LANES), F32))
    out_ref[...] = jnp.concatenate(lines, axis=0)


def finish_kernel(plan, me_ref, place_ref, notional_ref, own_ref, *refs):
    *in_refs, alloc_ref, cva_ref = refs
    me = me_ref[0]
    part, per_line = plan.part, plan.per_line
    rows = place_ref.shape[1]
    key = place_ref[0:1, :].astype(jnp.int32)
    rank = place_ref[1:2, :].astype(jnp.int32)
    group = lax.div(rank, part)
    line = group * plan.lines + me // per_line
    lane = lax.rem(me, per_line) * part + (rank - group * part)
    if plan.direct:
        key = lax.bitwise_xor(key, me)
        tiles = jnp.concatenate([ref[...] for ref in in_refs], axis=0)
    else:
        tiles = in_refs[0][...].reshape(plan.owners * plan.tile, LANES)
    hot = mask_bf16(iota((LANES, rows), 0) == lane)
    found = jnp.zeros((tiles.shape[0], rows), F32)
    for piece in split_bf16(tiles, 3):
        found = found + jnp.dot(piece, hot, preferred_element_type=F32)
    wanted = iota(found.shape, 0) == key * plan.tile + line
    share = jnp.sum(jnp.where(wanted, found, 0.0), axis=0, keepdims=True)
    alloc_ref[...] = share * in_a_row(notional_ref[...])
    last = plan.groups * plan.lines
    cva_ref[...] = own_ref[last : last + 1, 0 : cva_ref.shape[1]]


def permuted(x, axis, size, d):
    return lax.ppermute(x, axis, [(i, i ^ d) for i in range(size)])


def body(
    shocks,
    forward_start,
    loading,
    coefficient,
    notional,
    ns_of_trade,
    agr_of_ns,
    cpty_of_agr,
    margin_lag,
    default_weight,
):
    owners = lax.axis_size("trade")
    path_parts = lax.axis_size("path")
    tenors, dates, path_dev = shocks.shape
    path_total = float(path_dev * path_parts)
    rows = coefficient.shape[0]
    lines = rows // LANES
    plan = Plan(owners, rows, tenors, dates)
    cols = dates * path_dev
    chunks = cols // plan.width
    me = lax.axis_index("trade").astype(jnp.int32).reshape(1)
    notional = notional.reshape(lines, LANES)

    place, outgoing = pl.pallas_call(
        functools.partial(pack_kernel, plan),
        out_shape=[
            jax.ShapeDtypeStruct((SUBS, rows), F32),
            jax.ShapeDtypeStruct((owners, plan.height, LANES), BF16),
        ],
        in_specs=[SMEM] + [HBM] * 3,
        out_specs=[VMEM, HBM],
        scratch_shapes=[
            pltpu.VMEM((owners, plan.height, LANES), BF16),
            pltpu.VMEM((owners * lines, LANES), jnp.int32),
            pltpu.VMEM((2 * tenors, rows), BF16),
            pltpu.VMEM((lines, LANES), F32),
            pltpu.SemaphoreType.DMA((3,)),
            pltpu.SemaphoreType.DMA((owners,)),
        ],
        name="pack",
    )(me, ns_of_trade.reshape(owners * lines, LANES), coefficient.T, notional)
    incoming = lax.all_to_all(outgoing, "trade", split_axis=0, concat_axis=0, tiled=True)

    basis = pl.pallas_call(
        functools.partial(basis_kernel, plan),
        out_shape=jax.ShapeDtypeStruct((chunks, 2 * LANES, plan.width), BF16),
        in_specs=[HBM] * 3,
        out_specs=HBM,
        scratch_shapes=[
            pltpu.VMEM((chunks, 2 * LANES, plan.width), BF16),
            pltpu.VMEM((tenors * dates, path_dev), BF16),
            pltpu.VMEM((1, tenors), F32),
            pltpu.VMEM((tenors, tenors), F32),
            pltpu.VMEM((tenors * dates, path_dev), F32),
            pltpu.SemaphoreType.DMA((3,)),
            pltpu.SemaphoreType.DMA((chunks,)),
        ],
        name="basis",
        cost_estimate=pl.CostEstimate(
            flops=2 * 400 * tenors * cols, bytes_accessed=4 << 20, transcendentals=3 * tenors * cols
        ),
    )(shocks.reshape(tenors * dates, path_dev), forward_start.reshape(1, tenors), loading)

    tile = pl.pallas_call(
        functools.partial(main_kernel, plan, path_total),
        out_shape=jax.ShapeDtypeStruct((plan.tile, LANES), F32),
        in_specs=[SMEM] * 4 + [VMEM] * 2 + [HBM],
        out_specs=VMEM,
        scratch_shapes=[
            pltpu.VMEM((chunks, plan.trades, plan.width), BF16),
            pltpu.VMEM((chunks, 2 * LANES, plan.width), BF16),
            pltpu.SemaphoreType.DMA((chunks,)),
        ],
        name="value_and_allocate",
        compiler_params=pltpu.CompilerParams(vmem_limit_bytes=60 << 20),
    )(me, agr_of_ns, cpty_of_agr, margin_lag, default_weight, incoming, basis)

    others = [permuted(tile, "path", path_parts, d) for d in range(1, path_parts)]
    for other in others:
        tile = tile + other
    if plan.direct:
        pair = jnp.concatenate([tile, permuted(tile, "trade", owners, 1)], axis=0)
        tiles = [pair] + [permuted(pair, "trade", owners, d) for d in range(2, owners, 2)]
    else:
        spread = jnp.broadcast_to(tile, (owners,) + tile.shape)
        tiles = [lax.all_to_all(spread, "trade", split_axis=0, concat_axis=0, tiled=True)]
    allocation, cva = pl.pallas_call(
        functools.partial(finish_kernel, plan),
        out_shape=[
            jax.ShapeDtypeStruct((1, rows), F32),
            jax.ShapeDtypeStruct((1, default_weight.shape[0]), F32),
        ],
        in_specs=[SMEM] + [VMEM] * (3 + len(tiles)),
        out_specs=[VMEM, VMEM],
        name="finish",
        compiler_params=pltpu.CompilerParams(vmem_limit_bytes=32 << 20),
    )(me, place, notional, tile, *tiles)
    return (allocation.reshape(rows), cva.reshape(default_weight.shape[0]))


def solution(mesh):
    placed = (
        P(None, None, "path"),
        P(),
        P(),
        P("trade", None),
        P("trade"),
        P(),
        P("trade"),
        P("trade"),
        P("trade"),
        P("trade", None),
    )
    return jax.shard_map(
        body, mesh=mesh, in_specs=placed, out_specs=(P("trade"), P("trade")), check_vma=False
    )
```

```python
import functools

import jax
import jax.numpy as jnp
from jax import lax
from jax.experimental import pallas as pl
from jax.experimental.pallas import tpu as pltpu
from jax.sharding import PartitionSpec as P

NS_DEV = 8
AG_DEV = 4
LAG_MAX = 4
LANES = 128
SUBS = 8
DIRECT = 8

RATE_UNIT = 0.03
STEP = 0.25
SMOOTH = 0.5

F32 = jnp.float32
BF16 = jnp.bfloat16
VMEM = pl.BlockSpec(memory_space=pltpu.VMEM)
SMEM = pl.BlockSpec(memory_space=pltpu.SMEM)
HBM = pl.BlockSpec(memory_space=pltpu.HBM)
BOTH_LANES = (((1,), (1,)), ((), ()))


def iota(shape, dim):
    return lax.broadcasted_iota(jnp.int32, shape, dim)


def mask_bf16(mask):
    return mask.astype(F32).astype(BF16)


def split_bf16(x, parts):
    pieces = []
    for _ in range(parts):
        piece = x.astype(BF16)
        pieces.append(piece)
        x = x - piece.astype(F32)
    return pieces


def fetch(sources, targets, sems):
    copies = [pltpu.make_async_copy(a, b, sems.at[n]) for n, (a, b) in enumerate(zip(sources, targets))]
    for copy in copies:
        copy.start()
    return copies


def in_a_row(x):
    return jnp.concatenate([x[r : r + 1] for r in range(x.shape[0])], axis=1)


class Plan:
    def __init__(self, owners, rows, tenors, dates):
        most = 3 * rows // (2 * owners)
        self.owners = owners
        self.direct = owners <= DIRECT
        self.groups = 3 if most % 48 == 0 else 1
        self.part = -(-most // (16 * self.groups)) * 16
        self.room = self.groups * self.part
        self.height = self.room + self.part
        self.extra = 2 * tenors - LANES
        self.per_line = LANES // self.part
        self.lines = owners * self.part // LANES
        self.trades = owners * self.room
        self.tile = -(-(self.groups * self.lines + 1) // SUBS) * SUBS
        self.dates = dates
        self.width = 512


def pack_kernel(plan, me_ref, sets_hbm, coef_hbm, notional_hbm, place_ref, out_ref, *refs):
    sets_ref, coef_ref, notional_ref, sems = refs
    copies = fetch(
        [sets_hbm, notional_hbm, coef_hbm], [sets_ref, notional_ref, coef_ref], sems
    )
    me = me_ref[0]
    owners, part, room, extra = plan.owners, plan.part, plan.room, plan.extra
    lines = notional_ref.shape[0]
    rows = lines * LANES
    shared = SUBS // lines
    copies[0].wait()
    block = sets_ref[pl.ds(pl.multiple_of(me // shared * SUBS, SUBS), SUBS), :]
    own = block[0:lines]
    for b in range(1, shared):
        own = jnp.where(lax.rem(me, shared) == b, block[b * lines : (b + 1) * lines], own)
    sets = in_a_row(own)
    key = lax.shift_right_logical(sets, 3)
    local = sets - key * NS_DEV
    hot = iota((owners, rows), 0) == key
    before = mask_bf16(iota((rows, rows), 0) < iota((rows, rows), 1))
    count = jnp.dot(mask_bf16(hot), before, preferred_element_type=F32)
    rank = jnp.sum(jnp.where(hot, count, 0.0), axis=0, keepdims=True)
    place_ref[...] = jnp.concatenate(
        [key.astype(F32), rank, jnp.zeros((SUBS - 2, rows), F32)], axis=0
    )
    spot = key * room + rank.astype(jnp.int32)
    chosen = mask_bf16(iota((owners * room, rows), 0) == spot)
    copies[1].wait()
    notional = in_a_row(notional_ref[...])
    high = notional.astype(BF16).astype(F32)
    info = jnp.concatenate(
        [high, notional - high, local.astype(F32), jnp.zeros((13, rows), F32)], axis=0
    )
    copies[2].wait()
    table = jnp.concatenate([coef_ref[...], info.astype(BF16)], axis=0)
    moved = lax.dot_general(chosen, table, BOTH_LANES, preferred_element_type=F32)
    ids = LANES + extra
    for d in range(owners):
        message = out_ref.at[d]
        block = moved[d * room : (d + 1) * room]
        message[0:room, :] = block[:, 0:LANES].astype(BF16)
        split = [block[part * g : part * (g + 1)] for g in range(plan.groups)]
        lanes = [x[:, LANES:ids] for x in split]
        if plan.groups < 3:
            lanes.append(jnp.zeros((part, extra * (3 - plan.groups)), F32))
        lanes += [x[:, ids : ids + SUBS] for x in split]
        lanes.append(jnp.zeros((part, SUBS * (4 - plan.groups)), F32))
        message[room:, :] = jnp.concatenate(lanes, axis=1).astype(BF16)


def basis_kernel(plan, shocks_hbm, start_hbm, loading_hbm, out_ref, *refs):
    shocks_ref, start_ref, loading_ref, wide_ref, sems = refs
    copies = fetch(
        [loading_hbm, start_hbm, shocks_hbm], [loading_ref, start_ref, shocks_ref], sems
    )
    tenors = loading_ref.shape[0]
    dates = plan.dates
    copies[0].wait()
    copies[1].wait()
    loading_t = jnp.transpose(loading_ref[...])
    drift = 0.5 * STEP * jnp.sum(loading_t * loading_t, axis=1, keepdims=True)
    diag = iota((tenors, tenors), 0) == iota((tenors, tenors), 1)
    log_start = jnp.log(jnp.sum(jnp.where(diag, start_ref[...], 0.0), axis=1, keepdims=True))
    loads = jnp.concatenate(split_bf16((STEP**0.5) * loading_t, 3), axis=1)
    lower = mask_bf16(iota((tenors, tenors), 1) <= iota((tenors, tenors), 0))
    lower = jnp.concatenate([lower, lower], axis=1)
    log_fwd = jnp.broadcast_to(log_start, (tenors, LANES))
    drift = jnp.broadcast_to(drift, (tenors, LANES))
    head = LANES - tenors
    copies[2].wait()
    wide_ref[...] = shocks_ref[...].astype(F32)
    step = plan.width // LANES
    for c in range(dates // step):
        shock = jnp.concatenate(
            [
                wide_ref[pl.ds(c * step + j, tenors, stride=dates), :].astype(BF16)
                for j in range(step)
            ],
            axis=1,
        )
        change = jnp.dot(
            loads, jnp.concatenate([shock] * 3, axis=0), preferred_element_type=F32
        )
        logs = []
        for j in range(step):
            log_fwd = log_fwd + (change[:, LANES * j : LANES * (j + 1)] - drift)
            logs.append(log_fwd)
        fwd = jnp.exp(jnp.concatenate(logs, axis=1))
        growth = split_bf16(jnp.log(1.0 + STEP * fwd), 2)
        summed = jnp.dot(lower, jnp.concatenate(growth, axis=0), preferred_element_type=F32)
        bond = jnp.exp(-summed)
        cols = slice(c * plan.width, (c + 1) * plan.width)
        out_ref[0:tenors, cols] = (bond * fwd * (1.0 / RATE_UNIT)).astype(BF16)
        bond = bond.astype(BF16)
        out_ref[tenors:LANES, cols] = bond[0:head]
        for g in range(plan.groups):
            out_ref[LANES + plan.extra * g : LANES + plan.extra * (g + 1), cols] = bond[head:]
        used = LANES + plan.extra * plan.groups
        out_ref[used:, cols] = jnp.zeros((2 * LANES - used, plan.width), BF16)


def main_kernel(plan, path_total, me_ref, agr_ref, cpty_ref, lag_ref, weight_ref, basis_ref, *refs):
    in_ref, out_ref, val_ref = refs
    me = me_ref[0]
    part, room, dates = plan.part, plan.room, plan.dates
    cpty_dev = weight_ref.shape[0]

    def rows_of(first):
        return in_ref[:, first : first + part, :].reshape(plan.owners * part, LANES)

    rest = rows_of(room)
    lane = iota((1, LANES), 1)
    left, info = [], []
    for g in range(plan.groups):
        keep = mask_bf16((lane >= plan.extra * g) & (lane < plan.extra * (g + 1)))
        left.append(jnp.concatenate([rows_of(part * g), rest * keep], axis=1))
        pick = mask_bf16(iota((SUBS, LANES), 1) == 3 * plan.extra + SUBS * g + iota((SUBS, LANES), 0))
        info.append(lax.dot_general(pick, rest, BOTH_LANES, preferred_element_type=F32))
    left = jnp.concatenate(left, axis=0)
    info = jnp.concatenate(info, axis=1)
    local = info[2:3].astype(jnp.int32)
    agr = jnp.zeros_like(local)
    for n in range(NS_DEV):
        agr = jnp.where(local == n, agr_ref[n] - me * AG_DEV, agr)
    row = iota((SUBS, plan.trades), 0)
    hot = lax.rem(row, AG_DEV) == agr
    netting = jnp.where(hot, jnp.where(row < AG_DEV, info[0:1], info[1:2]), 0.0).astype(BF16)

    owed = []
    width = plan.width
    chunks = dates * LANES // width
    for c in range(chunks):
        under = jnp.dot(
            left, basis_ref[:, c * width : (c + 1) * width], preferred_element_type=F32
        )
        value = jnp.maximum(under, 0.0).astype(BF16)
        val_ref[c] = value
        both = jnp.dot(netting, value, preferred_element_type=F32)
        both = both + pltpu.roll(both, AG_DEV, 0)
        owed += [both[:, LANES * j : LANES * (j + 1)] for j in range(width // LANES)]

    member = lax.rem(iota((SUBS, LANES), 0), AG_DEV)
    lag = jnp.zeros((SUBS, LANES), jnp.int32)
    cpty = jnp.zeros((SUBS, LANES), jnp.int32)
    for a in range(AG_DEV):
        lag = jnp.where(member == a, lag_ref[a], lag)
        cpty = jnp.where(member == a, cpty_ref[a] - me * cpty_dev, cpty)
    lags = [lag == s for s in range(1, LAG_MAX + 1)]
    weight = jnp.zeros((SUBS, dates), F32)
    for c in range(cpty_dev):
        weight = jnp.where(cpty[:, 0:dates] == c, weight_ref[c : c + 1, :], weight)
    zero = jnp.zeros((SUBS, LANES), F32)
    spent, slopes = zero, []
    for t in range(dates):
        before = zero
        for s in range(1, min(t, LAG_MAX) + 1):
            before = jnp.where(lags[s - 1], owed[t - s], before)
        excess = owed[t] - before
        square = excess * excess + SMOOTH * SMOOTH
        root = jnp.sqrt(square)
        due = weight[:, t : t + 1]
        spent = spent + due * (0.5 * (excess + root))
        slopes.append(due * (0.5 * (1.0 + excess / root)))
    grads = []
    for t in range(dates):
        after = zero
        for s in range(1, min(dates - 1 - t, LAG_MAX) + 1):
            after = jnp.where(lags[s - 1], slopes[t + s], after)
        grads.append(((slopes[t] - after) * (1.0 / path_total)).astype(BF16))

    dots = jnp.zeros((SUBS, plan.trades), F32)
    step = width // LANES
    for c in range(chunks):
        part_grads = jnp.concatenate(grads[c * step : (c + 1) * step], axis=1)
        dots = dots + lax.dot_general(
            part_grads, val_ref[c], BOTH_LANES, preferred_element_type=F32
        )
    share = jnp.sum(jnp.where(hot & (row < AG_DEV), dots, 0.0), axis=0, keepdims=True)
    lines = [share[:, LANES * k : LANES * (k + 1)] for k in range(plan.trades // LANES)]
    spent = jnp.sum(spent, axis=1, keepdims=True) * (1.0 / path_total)
    mine = (lane == cpty) & (iota((SUBS, LANES), 0) < AG_DEV)
    lines.append(jnp.sum(jnp.where(mine, spent, 0.0), axis=0, keepdims=True))
    if len(lines) < plan.tile:
        lines.append(jnp.zeros((plan.tile - len(lines), LANES), F32))
    out_ref[...] = jnp.concatenate(lines, axis=0)


def finish_kernel(plan, me_ref, place_ref, notional_ref, in_ref, alloc_ref, cva_ref):
    me = me_ref[0]
    part, per_line = plan.part, plan.per_line
    rows = place_ref.shape[1]
    key = place_ref[0:1, :].astype(jnp.int32)
    rank = place_ref[1:2, :].astype(jnp.int32)
    group = lax.div(rank, part)
    line = group * plan.lines + me // per_line
    lane = lax.rem(me, per_line) * part + (rank - group * part)
    tiles, own = in_ref[:, 0], in_ref[me, 0]
    for p in range(1, in_ref.shape[1]):
        tiles = tiles + in_ref[:, p]
        own = own + in_ref[me, p]
    tiles = tiles.reshape(plan.owners * plan.tile, LANES)
    hot = mask_bf16(iota((LANES, rows), 0) == lane)
    found = jnp.zeros((tiles.shape[0], rows), F32)
    for piece in split_bf16(tiles, 3):
        found = found + jnp.dot(piece, hot, preferred_element_type=F32)
    wanted = iota(found.shape, 0) == key * plan.tile + line
    share = jnp.sum(jnp.where(wanted, found, 0.0), axis=0, keepdims=True)
    alloc_ref[...] = share * in_a_row(notional_ref[...])
    last = plan.groups * plan.lines
    cva_ref[...] = own[last : last + 1, 0 : cva_ref.shape[1]]


def permuted(x, axis, size, d):
    return lax.ppermute(x, axis, [(i, i ^ d) for i in range(size)])


def body(
    shocks,
    forward_start,
    loading,
    coefficient,
    notional,
    ns_of_trade,
    agr_of_ns,
    cpty_of_agr,
    margin_lag,
    default_weight,
):
    owners = lax.axis_size("trade")
    path_parts = lax.axis_size("path")
    tenors, dates, path_dev = shocks.shape
    path_total = float(path_dev * path_parts)
    rows = coefficient.shape[0]
    lines = rows // LANES
    plan = Plan(owners, rows, tenors, dates)
    cols = dates * path_dev
    me = lax.axis_index("trade").astype(jnp.int32).reshape(1)
    notional = notional.reshape(lines, LANES)

    place, outgoing = pl.pallas_call(
        functools.partial(pack_kernel, plan),
        out_shape=[
            jax.ShapeDtypeStruct((SUBS, rows), F32),
            jax.ShapeDtypeStruct((owners, plan.height, LANES), BF16),
        ],
        in_specs=[SMEM] + [HBM] * 3,
        out_specs=[VMEM, VMEM],
        scratch_shapes=[
            pltpu.VMEM((owners * lines, LANES), jnp.int32),
            pltpu.VMEM((2 * tenors, rows), BF16),
            pltpu.VMEM((lines, LANES), F32),
            pltpu.SemaphoreType.DMA((3,)),
        ],
        name="pack",
    )(me, ns_of_trade.reshape(owners * lines, LANES), coefficient.T, notional)
    incoming = lax.all_to_all(outgoing, "trade", split_axis=0, concat_axis=0, tiled=True)

    basis = pl.pallas_call(
        functools.partial(basis_kernel, plan),
        out_shape=jax.ShapeDtypeStruct((2 * LANES, cols), BF16),
        in_specs=[HBM] * 3,
        out_specs=VMEM,
        scratch_shapes=[
            pltpu.VMEM((tenors * dates, path_dev), BF16),
            pltpu.VMEM((1, tenors), F32),
            pltpu.VMEM((tenors, tenors), F32),
            pltpu.VMEM((tenors * dates, path_dev), F32),
            pltpu.SemaphoreType.DMA((3,)),
        ],
        name="basis",
        compiler_params=pltpu.CompilerParams(vmem_limit_bytes=16 << 20),
        cost_estimate=pl.CostEstimate(
            flops=2 * 400 * tenors * cols, bytes_accessed=4 << 20, transcendentals=3 * tenors * cols
        ),
    )(shocks.reshape(tenors * dates, path_dev), forward_start.reshape(1, tenors), loading)

    need = 2 * plan.trades * cols + 16 * plan.trades * plan.width + (8 << 20)
    tile = pl.pallas_call(
        functools.partial(main_kernel, plan, path_total),
        out_shape=jax.ShapeDtypeStruct((plan.tile, LANES), F32),
        in_specs=[SMEM] * 4 + [VMEM] * 3,
        out_specs=VMEM,
        scratch_shapes=[pltpu.VMEM((cols // plan.width, plan.trades, plan.width), BF16)],
        name="value_and_allocate",
        compiler_params=pltpu.CompilerParams(vmem_limit_bytes=need),
    )(me, agr_of_ns, cpty_of_agr, margin_lag, default_weight, basis, incoming)

    if plan.direct:
        spread = jnp.broadcast_to(tile, (owners * path_parts,) + tile.shape)
        tiles = lax.all_to_all(spread, ("trade", "path"), split_axis=0, concat_axis=0, tiled=True)
        tiles = tiles.reshape((owners, path_parts) + tile.shape)
    else:
        others = [permuted(tile, "path", path_parts, d) for d in range(1, path_parts)]
        for other in others:
            tile = tile + other
        spread = jnp.broadcast_to(tile, (owners,) + tile.shape)
        tiles = lax.all_to_all(spread, "trade", split_axis=0, concat_axis=0, tiled=True)
        tiles = tiles[:, None]
    allocation, cva = pl.pallas_call(
        functools.partial(finish_kernel, plan),
        out_shape=[
            jax.ShapeDtypeStruct((1, rows), F32),
            jax.ShapeDtypeStruct((1, default_weight.shape[0]), F32),
        ],
        in_specs=[SMEM] + [VMEM] * 3,
        out_specs=[VMEM, VMEM],
        name="finish",
        compiler_params=pltpu.CompilerParams(vmem_limit_bytes=32 << 20),
    )(me, place, notional, tiles)
    return (allocation.reshape(rows), cva.reshape(default_weight.shape[0]))


def solution(mesh):
    placed = (
        P(None, None, "path"),
        P(),
        P(),
        P("trade", None),
        P("trade"),
        P(),
        P("trade"),
        P("trade"),
        P("trade"),
        P("trade", None),
    )
    return jax.shard_map(
        body, mesh=mesh, in_specs=placed, out_specs=(P("trade"), P("trade")), check_vma=False
    )
```

```python
import functools

import jax
import jax.numpy as jnp
from jax import lax
from jax.experimental import pallas as pl
from jax.experimental.pallas import tpu as pltpu
from jax.sharding import PartitionSpec as P

NS_DEV = 8
AG_DEV = 4
LAG_MAX = 4
LANES = 128
SUBS = 8

RATE_UNIT = 0.03
STEP = 0.25
SMOOTH = 0.5

F32 = jnp.float32
BF16 = jnp.bfloat16
VMEM = pl.BlockSpec(memory_space=pltpu.VMEM)
SMEM = pl.BlockSpec(memory_space=pltpu.SMEM)
HBM = pl.BlockSpec(memory_space=pltpu.HBM)
BOTH_LANES = (((1,), (1,)), ((), ()))


def iota(shape, dim):
    return lax.broadcasted_iota(jnp.int32, shape, dim)


def mask_bf16(mask):
    return mask.astype(F32).astype(BF16)


def split_bf16(x, parts):
    pieces = []
    for _ in range(parts):
        piece = x.astype(BF16)
        pieces.append(piece)
        x = x - piece.astype(F32)
    return pieces


def fetch(sources, targets, sems):
    copies = [pltpu.make_async_copy(a, b, sems.at[n]) for n, (a, b) in enumerate(zip(sources, targets))]
    for copy in copies:
        copy.start()
    return copies


def in_a_row(x):
    return jnp.concatenate([x[r : r + 1] for r in range(x.shape[0])], axis=1)


class Plan:
    def __init__(self, owners, rows, tenors, dates):
        most = 3 * rows // (2 * owners)
        self.owners = owners
        self.groups = 3 if most % 48 == 0 else 1
        self.part = -(-most // (16 * self.groups)) * 16
        self.room = self.groups * self.part
        self.height = self.room + self.part
        self.extra = 2 * tenors - LANES
        self.per_line = LANES // self.part
        self.lines = owners * self.part // LANES
        self.trades = owners * self.room
        self.dates = dates
        self.width = 512
        self.step = 256


def pack_kernel(plan, me_ref, sets_hbm, coef_hbm, notional_hbm, place_ref, out_ref, *refs):
    sets_ref, coef_ref, notional_ref, sems = refs
    copies = fetch(
        [sets_hbm, notional_hbm, coef_hbm], [sets_ref, notional_ref, coef_ref], sems
    )
    me = me_ref[0]
    owners, part, room, extra = plan.owners, plan.part, plan.room, plan.extra
    lines = notional_ref.shape[0]
    rows = lines * LANES
    shared = SUBS // lines
    copies[0].wait()
    block = sets_ref[pl.ds(pl.multiple_of(me // shared * SUBS, SUBS), SUBS), :]
    own = block[0:lines]
    for b in range(1, shared):
        own = jnp.where(lax.rem(me, shared) == b, block[b * lines : (b + 1) * lines], own)
    sets = in_a_row(own)
    key = lax.shift_right_logical(sets, 3)
    local = sets - key * NS_DEV
    hot = iota((owners, rows), 0) == key
    before = mask_bf16(iota((rows, rows), 0) < iota((rows, rows), 1))
    count = jnp.dot(mask_bf16(hot), before, preferred_element_type=F32)
    rank = jnp.sum(jnp.where(hot, count, 0.0), axis=0, keepdims=True)
    place_ref[...] = jnp.concatenate(
        [key.astype(F32), rank, jnp.zeros((SUBS - 2, rows), F32)], axis=0
    )
    spot = key * room + rank.astype(jnp.int32)
    chosen = mask_bf16(iota((owners * room, rows), 0) == spot)
    copies[1].wait()
    notional = in_a_row(notional_ref[...])
    high = notional.astype(BF16).astype(F32)
    info = jnp.concatenate(
        [high, notional - high, local.astype(F32), jnp.zeros((13, rows), F32)], axis=0
    )
    copies[2].wait()
    table = jnp.concatenate([coef_ref[...], info.astype(BF16)], axis=0)
    moved = lax.dot_general(chosen, table, BOTH_LANES, preferred_element_type=F32)
    ids = LANES + extra
    for d in range(owners):
        message = out_ref.at[d]
        block = moved[d * room : (d + 1) * room]
        message[0:room, :] = block[:, 0:LANES].astype(BF16)
        split = [block[part * g : part * (g + 1)] for g in range(plan.groups)]
        lanes = [x[:, LANES:ids] for x in split]
        if plan.groups < 3:
            lanes.append(jnp.zeros((part, extra * (3 - plan.groups)), F32))
        lanes += [x[:, ids : ids + SUBS] for x in split]
        lanes.append(jnp.zeros((part, SUBS * (4 - plan.groups)), F32))
        message[room:, :] = jnp.concatenate(lanes, axis=1).astype(BF16)


def basis_kernel(plan, shocks_hbm, start_hbm, loading_hbm, out_ref, *refs):
    shocks_ref, start_ref, loading_ref, wide_ref, sems = refs
    copies = fetch(
        [loading_hbm, start_hbm, shocks_hbm], [loading_ref, start_ref, shocks_ref], sems
    )
    tenors = loading_ref.shape[0]
    dates = plan.dates
    copies[0].wait()
    copies[1].wait()
    loading_t = jnp.transpose(loading_ref[...])
    drift = 0.5 * STEP * jnp.sum(loading_t * loading_t, axis=1, keepdims=True)
    diag = iota((tenors, tenors), 0) == iota((tenors, tenors), 1)
    log_start = jnp.log(jnp.sum(jnp.where(diag, start_ref[...], 0.0), axis=1, keepdims=True))
    loads = jnp.concatenate(split_bf16((STEP**0.5) * loading_t, 3), axis=1)
    lower = mask_bf16(iota((tenors, tenors), 1) <= iota((tenors, tenors), 0))
    lower = jnp.concatenate([lower, lower], axis=1)
    log_fwd = jnp.broadcast_to(log_start, (tenors, LANES))
    drift = jnp.broadcast_to(drift, (tenors, LANES))
    head = LANES - tenors
    copies[2].wait()
    wide_ref[...] = shocks_ref[...].astype(F32)
    step = plan.width // LANES
    for c in range(dates // step):
        shock = jnp.concatenate(
            [
                wide_ref[pl.ds(c * step + j, tenors, stride=dates), :].astype(BF16)
                for j in range(step)
            ],
            axis=1,
        )
        change = jnp.dot(
            loads, jnp.concatenate([shock] * 3, axis=0), preferred_element_type=F32
        )
        logs = []
        for j in range(step):
            log_fwd = log_fwd + (change[:, LANES * j : LANES * (j + 1)] - drift)
            logs.append(log_fwd)
        fwd = jnp.exp(jnp.concatenate(logs, axis=1))
        growth = split_bf16(jnp.log(1.0 + STEP * fwd), 2)
        summed = jnp.dot(lower, jnp.concatenate(growth, axis=0), preferred_element_type=F32)
        bond = jnp.exp(-summed)
        cols = slice(c * plan.width, (c + 1) * plan.width)
        out_ref[0:tenors, cols] = (bond * fwd * (1.0 / RATE_UNIT)).astype(BF16)
        bond = bond.astype(BF16)
        out_ref[tenors:LANES, cols] = bond[0:head]
        for g in range(plan.groups):
            out_ref[LANES + plan.extra * g : LANES + plan.extra * (g + 1), cols] = bond[head:]
        used = LANES + plan.extra * plan.groups
        out_ref[used:, cols] = jnp.zeros((2 * LANES - used, plan.width), BF16)


def main_kernel(plan, path_total, me_ref, agr_ref, cpty_ref, lag_ref, weight_ref, basis_ref, *refs):
    in_ref, out_ref, val_ref = refs
    me = me_ref[0]
    part, room, dates = plan.part, plan.room, plan.dates
    cpty_dev = weight_ref.shape[0]

    def rows_of(first):
        return in_ref[:, first : first + part, :].reshape(plan.owners * part, LANES)

    rest = rows_of(room)
    lane = iota((1, LANES), 1)
    left, info = [], []
    for g in range(plan.groups):
        keep = mask_bf16((lane >= plan.extra * g) & (lane < plan.extra * (g + 1)))
        left.append(jnp.concatenate([rows_of(part * g), rest * keep], axis=1))
        pick = mask_bf16(iota((SUBS, LANES), 1) == 3 * plan.extra + SUBS * g + iota((SUBS, LANES), 0))
        info.append(lax.dot_general(pick, rest, BOTH_LANES, preferred_element_type=F32))
    left = jnp.concatenate(left, axis=0)
    info = jnp.concatenate(info, axis=1)
    local = info[2:3].astype(jnp.int32)
    agr = jnp.zeros_like(local)
    for n in range(NS_DEV):
        agr = jnp.where(local == n, agr_ref[n] - me * AG_DEV, agr)
    row = iota((SUBS, plan.trades), 0)
    hot = lax.rem(row, AG_DEV) == agr
    netting = jnp.where(hot, jnp.where(row < AG_DEV, info[0:1], info[1:2]), 0.0).astype(BF16)

    owed = []
    width = plan.step
    chunks = dates * LANES // width
    for c in range(chunks):
        under = jnp.dot(
            left, basis_ref[:, c * width : (c + 1) * width], preferred_element_type=F32
        )
        value = jnp.maximum(under, 0.0).astype(BF16)
        val_ref[c] = value
        both = jnp.dot(netting, value, preferred_element_type=F32)
        both = both + pltpu.roll(both, AG_DEV, 0)
        owed += [both[:, LANES * j : LANES * (j + 1)] for j in range(width // LANES)]

    member = lax.rem(iota((SUBS, LANES), 0), AG_DEV)
    lag = jnp.zeros((SUBS, LANES), jnp.int32)
    cpty = jnp.zeros((SUBS, LANES), jnp.int32)
    for a in range(AG_DEV):
        lag = jnp.where(member == a, lag_ref[a], lag)
        cpty = jnp.where(member == a, cpty_ref[a] - me * cpty_dev, cpty)
    lags = [lag == s for s in range(1, LAG_MAX + 1)]
    weight = jnp.zeros((SUBS, dates), F32)
    for c in range(cpty_dev):
        weight = jnp.where(cpty[:, 0:dates] == c, weight_ref[c : c + 1, :], weight)
    zero = jnp.zeros((SUBS, LANES), F32)
    spent, slopes = zero, []
    for t in range(dates):
        before = zero
        for s in range(1, min(t, LAG_MAX) + 1):
            before = jnp.where(lags[s - 1], owed[t - s], before)
        excess = owed[t] - before
        square = excess * excess + SMOOTH * SMOOTH
        root = jnp.sqrt(square)
        due = weight[:, t : t + 1]
        spent = spent + due * (0.5 * (excess + root))
        slopes.append(due * (0.5 * (1.0 + excess / root)))
    grads = []
    for t in range(dates):
        after = zero
        for s in range(1, min(dates - 1 - t, LAG_MAX) + 1):
            after = jnp.where(lags[s - 1], slopes[t + s], after)
        grads.append(((slopes[t] - after) * (1.0 / path_total)).astype(BF16))

    dots = jnp.zeros((SUBS, plan.trades), F32)
    step = width // LANES
    for c in range(chunks):
        part_grads = jnp.concatenate(grads[c * step : (c + 1) * step], axis=1)
        dots = dots + lax.dot_general(
            part_grads, val_ref[c], BOTH_LANES, preferred_element_type=F32
        )
    share = jnp.sum(jnp.where(hot & (row < AG_DEV), dots, 0.0), axis=0, keepdims=True)
    spent = jnp.sum(spent, axis=1, keepdims=True) * (1.0 / path_total)
    mine = (lane - room == cpty) & (iota((SUBS, LANES), 0) < AG_DEV)
    cva = jnp.sum(jnp.where(mine, spent, 0.0), axis=0, keepdims=True)
    block = lane // part
    count = plan.groups * plan.lines
    lines = jnp.concatenate([share[:, LANES * k : LANES * (k + 1)] for k in range(count)], axis=0)
    moved = [lines if m == 0 else pltpu.roll(lines, part * m, 1) for m in range(plan.per_line)]
    paths = out_ref.shape[0] // plan.owners
    for k in range(plan.lines):
        for s in range(plan.per_line):
            line = cva
            for g in range(plan.groups):
                n = g * plan.lines + k
                line = jnp.where(block == g, moved[(g - s) % plan.per_line][n : n + 1], line)
            for p in range(paths):
                out_ref[(k * plan.per_line + s) * paths + p] = line


def finish_kernel(plan, me_ref, place_ref, notional_ref, in_ref, alloc_ref, cva_ref):
    me = me_ref[0]
    rows = place_ref.shape[1]
    key = place_ref[0:1, :].astype(jnp.int32)
    rank = place_ref[1:2, :].astype(jnp.int32)
    lines = in_ref[...]
    count = lines.shape[0]
    paths = count // plan.owners
    hot = mask_bf16(iota((LANES, rows), 0) == rank)
    found = jnp.zeros((count, rows), F32)
    for piece in split_bf16(lines, 3):
        found = found + jnp.dot(piece, hot, preferred_element_type=F32)
    wanted = iota(found.shape, 0) // paths == key
    share = jnp.sum(jnp.where(wanted, found, 0.0), axis=0, keepdims=True)
    alloc_ref[...] = share * in_a_row(notional_ref[...])
    own = iota(lines.shape, 0) // paths == me
    cva = jnp.sum(jnp.where(own, lines, 0.0), axis=0, keepdims=True)
    cva_ref[...] = cva[:, plan.room : plan.room + cva_ref.shape[1]]


def body(
    shocks,
    forward_start,
    loading,
    coefficient,
    notional,
    ns_of_trade,
    agr_of_ns,
    cpty_of_agr,
    margin_lag,
    default_weight,
):
    owners = lax.axis_size("trade")
    path_parts = lax.axis_size("path")
    tenors, dates, path_dev = shocks.shape
    path_total = float(path_dev * path_parts)
    rows = coefficient.shape[0]
    lines = rows // LANES
    plan = Plan(owners, rows, tenors, dates)
    cols = dates * path_dev
    me = lax.axis_index("trade").astype(jnp.int32).reshape(1)
    notional = notional.reshape(lines, LANES)

    place, outgoing = pl.pallas_call(
        functools.partial(pack_kernel, plan),
        out_shape=[
            jax.ShapeDtypeStruct((SUBS, rows), F32),
            jax.ShapeDtypeStruct((owners, plan.height, LANES), BF16),
        ],
        in_specs=[SMEM] + [HBM] * 3,
        out_specs=[VMEM, VMEM],
        scratch_shapes=[
            pltpu.VMEM((owners * lines, LANES), jnp.int32),
            pltpu.VMEM((2 * tenors, rows), BF16),
            pltpu.VMEM((lines, LANES), F32),
            pltpu.SemaphoreType.DMA((3,)),
        ],
        name="pack",
    )(me, ns_of_trade.reshape(owners * lines, LANES), coefficient.T, notional)
    incoming = lax.all_to_all(outgoing, "trade", split_axis=0, concat_axis=0, tiled=True)

    basis = pl.pallas_call(
        functools.partial(basis_kernel, plan),
        out_shape=jax.ShapeDtypeStruct((2 * LANES, cols), BF16),
        in_specs=[HBM] * 3,
        out_specs=VMEM,
        scratch_shapes=[
            pltpu.VMEM((tenors * dates, path_dev), BF16),
            pltpu.VMEM((1, tenors), F32),
            pltpu.VMEM((tenors, tenors), F32),
            pltpu.VMEM((tenors * dates, path_dev), F32),
            pltpu.SemaphoreType.DMA((3,)),
        ],
        name="basis",
        compiler_params=pltpu.CompilerParams(vmem_limit_bytes=16 << 20),
        cost_estimate=pl.CostEstimate(
            flops=2 * 400 * tenors * cols, bytes_accessed=4 << 20, transcendentals=3 * tenors * cols
        ),
    )(shocks.reshape(tenors * dates, path_dev), forward_start.reshape(1, tenors), loading)

    need = 2 * plan.trades * cols + 16 * plan.trades * plan.width + (8 << 20)
    lines_out = pl.pallas_call(
        functools.partial(main_kernel, plan, path_total),
        out_shape=jax.ShapeDtypeStruct((owners * path_parts, 1, LANES), F32),
        in_specs=[SMEM] * 4 + [VMEM] * 3,
        out_specs=VMEM,
        scratch_shapes=[pltpu.VMEM((cols // plan.step, plan.trades, plan.step), BF16)],
        name="value_and_allocate",
        compiler_params=pltpu.CompilerParams(vmem_limit_bytes=need),
    )(me, agr_of_ns, cpty_of_agr, margin_lag, default_weight, basis, incoming)

    lines_in = lax.all_to_all(lines_out, ("trade", "path"), split_axis=0, concat_axis=0, tiled=True)
    lines_in = lines_in.reshape(owners * path_parts, LANES)
    allocation, cva = pl.pallas_call(
        functools.partial(finish_kernel, plan),
        out_shape=[
            jax.ShapeDtypeStruct((1, rows), F32),
            jax.ShapeDtypeStruct((1, default_weight.shape[0]), F32),
        ],
        in_specs=[SMEM] + [VMEM] * 3,
        out_specs=[VMEM, VMEM],
        name="finish",
        compiler_params=pltpu.CompilerParams(vmem_limit_bytes=32 << 20),
    )(me, place, notional, lines_in)
    return (allocation.reshape(rows), cva.reshape(default_weight.shape[0]))


def solution(mesh):
    placed = (
        P(None, None, "path"),
        P(),
        P(),
        P("trade", None),
        P("trade"),
        P(),
        P("trade"),
        P("trade"),
        P("trade"),
        P("trade", None),
    )
    return jax.shard_map(
        body, mesh=mesh, in_specs=placed, out_specs=(P("trade"), P("trade")), check_vma=False
    )
```

```python
import functools

import jax
import jax.numpy as jnp
from jax import lax
from jax.experimental import pallas as pl
from jax.experimental.pallas import tpu as pltpu
from jax.sharding import PartitionSpec as P

NS_DEV = 8
AG_DEV = 4
LAG_MAX = 4
LANES = 128
SUBS = 8

RATE_UNIT = 0.03
STEP = 0.25
SMOOTH = 0.5

F32 = jnp.float32
BF16 = jnp.bfloat16
VMEM = pl.BlockSpec(memory_space=pltpu.VMEM)
SMEM = pl.BlockSpec(memory_space=pltpu.SMEM)
HBM = pl.BlockSpec(memory_space=pltpu.HBM)
BOTH_LANES = (((1,), (1,)), ((), ()))


def iota(shape, dim):
    return lax.broadcasted_iota(jnp.int32, shape, dim)


def mask_bf16(mask):
    return mask.astype(F32).astype(BF16)


def split_bf16(x, parts):
    pieces = []
    for _ in range(parts):
        piece = x.astype(BF16)
        pieces.append(piece)
        x = x - piece.astype(F32)
    return pieces


def fetch(sources, targets, sems):
    copies = [pltpu.make_async_copy(a, b, sems.at[n]) for n, (a, b) in enumerate(zip(sources, targets))]
    for copy in copies:
        copy.start()
    return copies


def in_a_row(x):
    return jnp.concatenate([x[r : r + 1] for r in range(x.shape[0])], axis=1)


class Plan:
    def __init__(self, owners, rows, tenors, dates):
        most = 3 * rows // (2 * owners)
        self.owners = owners
        self.groups = 3 if most % 48 == 0 else 1
        self.part = -(-most // (16 * self.groups)) * 16
        self.room = self.groups * self.part
        self.height = self.room + self.part
        self.extra = 2 * tenors - LANES
        self.per_line = LANES // self.part
        self.lines = owners * self.part // LANES
        self.trades = owners * self.room
        self.dates = dates
        self.width = 512
        self.step = 1024


def pack_kernel(plan, me_ref, sets_hbm, coef_hbm, notional_hbm, place_ref, out_ref, *refs):
    sets_ref, coef_ref, notional_ref, sems = refs
    copies = fetch(
        [sets_hbm, notional_hbm, coef_hbm], [sets_ref, notional_ref, coef_ref], sems
    )
    me = me_ref[0]
    owners, part, room, extra = plan.owners, plan.part, plan.room, plan.extra
    lines = notional_ref.shape[0]
    rows = lines * LANES
    shared = SUBS // lines
    copies[0].wait()
    block = sets_ref[pl.ds(pl.multiple_of(me // shared * SUBS, SUBS), SUBS), :]
    own = block[0:lines]
    for b in range(1, shared):
        own = jnp.where(lax.rem(me, shared) == b, block[b * lines : (b + 1) * lines], own)
    sets = in_a_row(own)
    key = lax.shift_right_logical(sets, 3)
    local = sets - key * NS_DEV
    hot = iota((owners, rows), 0) == key
    before = mask_bf16(iota((rows, rows), 0) < iota((rows, rows), 1))
    count = jnp.dot(mask_bf16(hot), before, preferred_element_type=F32)
    rank = jnp.sum(jnp.where(hot, count, 0.0), axis=0, keepdims=True)
    place_ref[...] = jnp.concatenate(
        [key.astype(F32), rank, jnp.zeros((SUBS - 2, rows), F32)], axis=0
    )
    spot = key * room + rank.astype(jnp.int32)
    chosen = mask_bf16(iota((owners * room, rows), 0) == spot)
    copies[1].wait()
    notional = in_a_row(notional_ref[...])
    high = notional.astype(BF16).astype(F32)
    info = jnp.concatenate(
        [high, notional - high, local.astype(F32), jnp.zeros((13, rows), F32)], axis=0
    )
    copies[2].wait()
    table = jnp.concatenate([coef_ref[...], info.astype(BF16)], axis=0)
    moved = lax.dot_general(chosen, table, BOTH_LANES, preferred_element_type=F32)
    ids = LANES + extra
    for d in range(owners):
        message = out_ref.at[d]
        block = moved[d * room : (d + 1) * room]
        message[0:room, :] = block[:, 0:LANES].astype(BF16)
        split = [block[part * g : part * (g + 1)] for g in range(plan.groups)]
        lanes = [x[:, LANES:ids] for x in split]
        if plan.groups < 3:
            lanes.append(jnp.zeros((part, extra * (3 - plan.groups)), F32))
        lanes += [x[:, ids : ids + SUBS] for x in split]
        lanes.append(jnp.zeros((part, SUBS * (4 - plan.groups)), F32))
        message[room:, :] = jnp.concatenate(lanes, axis=1).astype(BF16)


def basis_kernel(plan, shocks_hbm, start_hbm, loading_hbm, out_ref, *refs):
    shocks_ref, start_ref, loading_ref, wide_ref, sems = refs
    copies = fetch(
        [loading_hbm, start_hbm, shocks_hbm], [loading_ref, start_ref, shocks_ref], sems
    )
    tenors = loading_ref.shape[0]
    dates = plan.dates
    copies[0].wait()
    copies[1].wait()
    loading_t = jnp.transpose(loading_ref[...])
    drift = 0.5 * STEP * jnp.sum(loading_t * loading_t, axis=1, keepdims=True)
    diag = iota((tenors, tenors), 0) == iota((tenors, tenors), 1)
    log_start = jnp.log(jnp.sum(jnp.where(diag, start_ref[...], 0.0), axis=1, keepdims=True))
    loads = jnp.concatenate(split_bf16((STEP**0.5) * loading_t, 3), axis=1)
    lower = mask_bf16(iota((tenors, tenors), 1) <= iota((tenors, tenors), 0))
    lower = jnp.concatenate([lower, lower], axis=1)
    log_fwd = jnp.broadcast_to(log_start, (tenors, LANES))
    drift = jnp.broadcast_to(drift, (tenors, LANES))
    head = LANES - tenors
    copies[2].wait()
    wide_ref[...] = shocks_ref[...].astype(F32)
    step = plan.width // LANES
    for c in range(dates // step):
        shock = jnp.concatenate(
            [
                wide_ref[pl.ds(c * step + j, tenors, stride=dates), :].astype(BF16)
                for j in range(step)
            ],
            axis=1,
        )
        change = jnp.dot(
            loads, jnp.concatenate([shock] * 3, axis=0), preferred_element_type=F32
        )
        logs = []
        for j in range(step):
            log_fwd = log_fwd + (change[:, LANES * j : LANES * (j + 1)] - drift)
            logs.append(log_fwd)
        fwd = jnp.exp(jnp.concatenate(logs, axis=1))
        growth = split_bf16(jnp.log(1.0 + STEP * fwd), 2)
        summed = jnp.dot(lower, jnp.concatenate(growth, axis=0), preferred_element_type=F32)
        bond = jnp.exp(-summed)
        cols = slice(c * plan.width, (c + 1) * plan.width)
        out_ref[0:tenors, cols] = (bond * fwd * (1.0 / RATE_UNIT)).astype(BF16)
        bond = bond.astype(BF16)
        out_ref[tenors:LANES, cols] = bond[0:head]
        for g in range(plan.groups):
            out_ref[LANES + plan.extra * g : LANES + plan.extra * (g + 1), cols] = bond[head:]
        used = LANES + plan.extra * plan.groups
        out_ref[used:, cols] = jnp.zeros((2 * LANES - used, plan.width), BF16)


def main_kernel(plan, path_total, me_ref, agr_ref, cpty_ref, lag_ref, weight_ref, basis_ref, *refs):
    in_ref, out_ref, val_ref = refs
    me = me_ref[0]
    part, room, dates = plan.part, plan.room, plan.dates
    cpty_dev = weight_ref.shape[0]

    def rows_of(first):
        return in_ref[:, first : first + part, :].reshape(plan.owners * part, LANES)

    rest = rows_of(room)
    lane = iota((1, LANES), 1)
    left, info = [], []
    for g in range(plan.groups):
        keep = mask_bf16((lane >= plan.extra * g) & (lane < plan.extra * (g + 1)))
        left.append(jnp.concatenate([rows_of(part * g), rest * keep], axis=1))
        pick = mask_bf16(iota((SUBS, LANES), 1) == 3 * plan.extra + SUBS * g + iota((SUBS, LANES), 0))
        info.append(lax.dot_general(pick, rest, BOTH_LANES, preferred_element_type=F32))
    left = jnp.concatenate(left, axis=0)
    info = jnp.concatenate(info, axis=1)
    local = info[2:3].astype(jnp.int32)
    agr = jnp.zeros_like(local)
    for n in range(NS_DEV):
        agr = jnp.where(local == n, agr_ref[n] - me * AG_DEV, agr)
    row = iota((SUBS, plan.trades), 0)
    hot = lax.rem(row, AG_DEV) == agr
    netting = jnp.where(hot, jnp.where(row < AG_DEV, info[0:1], info[1:2]), 0.0).astype(BF16)

    owed = []
    width = plan.step
    chunks = dates * LANES // width
    for c in range(chunks):
        under = jnp.dot(
            left, basis_ref[:, c * width : (c + 1) * width], preferred_element_type=F32
        )
        value = jnp.maximum(under, 0.0).astype(BF16)
        val_ref[:, c * width : (c + 1) * width] = value
        both = jnp.dot(netting, value, preferred_element_type=F32)
        both = both + pltpu.roll(both, AG_DEV, 0)
        owed += [both[:, LANES * j : LANES * (j + 1)] for j in range(width // LANES)]

    member = lax.rem(iota((SUBS, LANES), 0), AG_DEV)
    lag = jnp.zeros((SUBS, LANES), jnp.int32)
    cpty = jnp.zeros((SUBS, LANES), jnp.int32)
    for a in range(AG_DEV):
        lag = jnp.where(member == a, lag_ref[a], lag)
        cpty = jnp.where(member == a, cpty_ref[a] - me * cpty_dev, cpty)
    lags = [lag == s for s in range(1, LAG_MAX + 1)]
    weight = jnp.zeros((SUBS, dates), F32)
    for c in range(cpty_dev):
        weight = jnp.where(cpty[:, 0:dates] == c, weight_ref[c : c + 1, :], weight)
    zero = jnp.zeros((SUBS, LANES), F32)
    spent, slopes = zero, []
    for t in range(dates):
        before = zero
        for s in range(1, min(t, LAG_MAX) + 1):
            before = jnp.where(lags[s - 1], owed[t - s], before)
        excess = owed[t] - before
        square = excess * excess + SMOOTH * SMOOTH
        root = jnp.sqrt(square)
        due = weight[:, t : t + 1]
        spent = spent + due * (0.5 * (excess + root))
        slopes.append(due * (0.5 * (1.0 + excess / root)))
    grads = []
    for t in range(dates):
        after = zero
        for s in range(1, min(dates - 1 - t, LAG_MAX) + 1):
            after = jnp.where(lags[s - 1], slopes[t + s], after)
        grads.append(((slopes[t] - after) * (1.0 / path_total)).astype(BF16))

    dots = lax.dot_general(
        jnp.concatenate(grads, axis=1), val_ref[...], BOTH_LANES, preferred_element_type=F32
    )
    share = jnp.sum(jnp.where(hot & (row < AG_DEV), dots, 0.0), axis=0, keepdims=True)
    spent = jnp.sum(spent, axis=1, keepdims=True) * (1.0 / path_total)
    mine = (lane - room == cpty) & (iota((SUBS, LANES), 0) < AG_DEV)
    cva = jnp.sum(jnp.where(mine, spent, 0.0), axis=0, keepdims=True)
    block = lane // part
    count = plan.groups * plan.lines
    lines = jnp.concatenate([share[:, LANES * k : LANES * (k + 1)] for k in range(count)], axis=0)
    moved = [lines if m == 0 else pltpu.roll(lines, part * m, 1) for m in range(plan.per_line)]
    paths = out_ref.shape[0] // plan.owners
    for k in range(plan.lines):
        for s in range(plan.per_line):
            line = cva
            for g in range(plan.groups):
                n = g * plan.lines + k
                line = jnp.where(block == g, moved[(g - s) % plan.per_line][n : n + 1], line)
            for p in range(paths):
                out_ref[(k * plan.per_line + s) * paths + p] = line


def finish_kernel(plan, me_ref, place_ref, notional_ref, in_ref, alloc_ref, cva_ref):
    me = me_ref[0]
    rows = place_ref.shape[1]
    key = place_ref[0:1, :].astype(jnp.int32)
    rank = place_ref[1:2, :].astype(jnp.int32)
    lines = in_ref[...]
    count = lines.shape[0]
    paths = count // plan.owners
    hot = mask_bf16(iota((LANES, rows), 0) == rank)
    found = jnp.zeros((count, rows), F32)
    for piece in split_bf16(lines, 3):
        found = found + jnp.dot(piece, hot, preferred_element_type=F32)
    wanted = iota(found.shape, 0) // paths == key
    share = jnp.sum(jnp.where(wanted, found, 0.0), axis=0, keepdims=True)
    alloc_ref[...] = share * in_a_row(notional_ref[...])
    own = iota(lines.shape, 0) // paths == me
    cva = jnp.sum(jnp.where(own, lines, 0.0), axis=0, keepdims=True)
    cva_ref[...] = cva[:, plan.room : plan.room + cva_ref.shape[1]]


def body(
    shocks,
    forward_start,
    loading,
    coefficient,
    notional,
    ns_of_trade,
    agr_of_ns,
    cpty_of_agr,
    margin_lag,
    default_weight,
):
    owners = lax.axis_size("trade")
    path_parts = lax.axis_size("path")
    tenors, dates, path_dev = shocks.shape
    path_total = float(path_dev * path_parts)
    rows = coefficient.shape[0]
    lines = rows // LANES
    plan = Plan(owners, rows, tenors, dates)
    cols = dates * path_dev
    me = lax.axis_index("trade").astype(jnp.int32).reshape(1)
    notional = notional.reshape(lines, LANES)

    place, outgoing = pl.pallas_call(
        functools.partial(pack_kernel, plan),
        out_shape=[
            jax.ShapeDtypeStruct((SUBS, rows), F32),
            jax.ShapeDtypeStruct((owners, plan.height, LANES), BF16),
        ],
        in_specs=[SMEM] + [HBM] * 3,
        out_specs=[VMEM, VMEM],
        scratch_shapes=[
            pltpu.VMEM((owners * lines, LANES), jnp.int32),
            pltpu.VMEM((2 * tenors, rows), BF16),
            pltpu.VMEM((lines, LANES), F32),
            pltpu.SemaphoreType.DMA((3,)),
        ],
        name="pack",
    )(me, ns_of_trade.reshape(owners * lines, LANES), coefficient.T, notional)
    incoming = lax.all_to_all(outgoing, "trade", split_axis=0, concat_axis=0, tiled=True)

    basis = pl.pallas_call(
        functools.partial(basis_kernel, plan),
        out_shape=jax.ShapeDtypeStruct((2 * LANES, cols), BF16),
        in_specs=[HBM] * 3,
        out_specs=VMEM,
        scratch_shapes=[
            pltpu.VMEM((tenors * dates, path_dev), BF16),
            pltpu.VMEM((1, tenors), F32),
            pltpu.VMEM((tenors, tenors), F32),
            pltpu.VMEM((tenors * dates, path_dev), F32),
            pltpu.SemaphoreType.DMA((3,)),
        ],
        name="basis",
        compiler_params=pltpu.CompilerParams(vmem_limit_bytes=16 << 20),
        cost_estimate=pl.CostEstimate(
            flops=2 * 400 * tenors * cols, bytes_accessed=4 << 20, transcendentals=3 * tenors * cols
        ),
    )(shocks.reshape(tenors * dates, path_dev), forward_start.reshape(1, tenors), loading)

    need = 2 * plan.trades * cols + 8 * plan.trades * plan.step + (8 << 20)
    lines_out = pl.pallas_call(
        functools.partial(main_kernel, plan, path_total),
        out_shape=jax.ShapeDtypeStruct((owners * path_parts, 1, LANES), F32),
        in_specs=[SMEM] * 4 + [VMEM] * 3,
        out_specs=VMEM,
        scratch_shapes=[pltpu.VMEM((plan.trades, cols), BF16)],
        name="value_and_allocate",
        compiler_params=pltpu.CompilerParams(vmem_limit_bytes=need),
    )(me, agr_of_ns, cpty_of_agr, margin_lag, default_weight, basis, incoming)

    lines_in = lax.all_to_all(lines_out, ("trade", "path"), split_axis=0, concat_axis=0, tiled=True)
    lines_in = lines_in.reshape(owners * path_parts, LANES)
    allocation, cva = pl.pallas_call(
        functools.partial(finish_kernel, plan),
        out_shape=[
            jax.ShapeDtypeStruct((1, rows), F32),
            jax.ShapeDtypeStruct((1, default_weight.shape[0]), F32),
        ],
        in_specs=[SMEM] + [VMEM] * 3,
        out_specs=[VMEM, VMEM],
        name="finish",
        compiler_params=pltpu.CompilerParams(vmem_limit_bytes=32 << 20),
    )(me, place, notional, lines_in)
    return (allocation.reshape(rows), cva.reshape(default_weight.shape[0]))


def solution(mesh):
    placed = (
        P(None, None, "path"),
        P(),
        P(),
        P("trade", None),
        P("trade"),
        P(),
        P("trade"),
        P("trade"),
        P("trade"),
        P("trade", None),
    )
    return jax.shard_map(
        body, mesh=mesh, in_specs=placed, out_specs=(P("trade"), P("trade")), check_vma=False
    )
```

```python
import functools

import jax
import jax.numpy as jnp
from jax import lax
from jax.experimental import pallas as pl
from jax.experimental.pallas import tpu as pltpu
from jax.sharding import PartitionSpec as P

NS_DEV = 8
AG_DEV = 4
LAG_MAX = 4
LANES = 128
SUBS = 8

RATE_UNIT = 0.03
STEP = 0.25
SMOOTH = 0.5

F32 = jnp.float32
BF16 = jnp.bfloat16
VMEM = pl.BlockSpec(memory_space=pltpu.VMEM)
SMEM = pl.BlockSpec(memory_space=pltpu.SMEM)
HBM = pl.BlockSpec(memory_space=pltpu.HBM)
BOTH_LANES = (((1,), (1,)), ((), ()))


def iota(shape, dim):
    return lax.broadcasted_iota(jnp.int32, shape, dim)


def mask_bf16(mask):
    return mask.astype(F32).astype(BF16)


def split_bf16(x, parts):
    pieces = []
    for _ in range(parts):
        piece = x.astype(BF16)
        pieces.append(piece)
        x = x - piece.astype(F32)
    return pieces


def fetch(sources, targets, sems):
    copies = [pltpu.make_async_copy(a, b, sems.at[n]) for n, (a, b) in enumerate(zip(sources, targets))]
    for copy in copies:
        copy.start()
    return copies


def in_a_row(x):
    return jnp.concatenate([x[r : r + 1] for r in range(x.shape[0])], axis=1)


class Plan:
    def __init__(self, owners, rows, tenors, dates):
        most = 3 * rows // (2 * owners)
        self.owners = owners
        self.groups = 3 if most % 48 == 0 else 1
        self.part = -(-most // (16 * self.groups)) * 16
        self.room = self.groups * self.part
        self.height = self.room + self.part
        self.extra = 2 * tenors - LANES
        self.per_line = LANES // self.part
        self.lines = owners * self.part // LANES
        self.trades = owners * self.room
        self.dates = dates
        self.width = 512
        self.step = 2048 if self.trades <= 1024 else 512


def pack_kernel(plan, me_ref, sets_hbm, coef_hbm, notional_hbm, place_ref, out_ref, *refs):
    sets_ref, coef_ref, notional_ref, sems = refs
    copies = fetch(
        [sets_hbm, notional_hbm, coef_hbm], [sets_ref, notional_ref, coef_ref], sems
    )
    me = me_ref[0]
    owners, part, room, extra = plan.owners, plan.part, plan.room, plan.extra
    lines = notional_ref.shape[0]
    rows = lines * LANES
    shared = SUBS // lines
    copies[0].wait()
    block = sets_ref[pl.ds(pl.multiple_of(me // shared * SUBS, SUBS), SUBS), :]
    own = block[0:lines]
    for b in range(1, shared):
        own = jnp.where(lax.rem(me, shared) == b, block[b * lines : (b + 1) * lines], own)
    sets = in_a_row(own)
    key = lax.shift_right_logical(sets, 3)
    local = sets - key * NS_DEV
    hot = iota((owners, rows), 0) == key
    before = mask_bf16(iota((rows, rows), 0) < iota((rows, rows), 1))
    count = jnp.dot(mask_bf16(hot), before, preferred_element_type=F32)
    rank = jnp.sum(jnp.where(hot, count, 0.0), axis=0, keepdims=True)
    place_ref[...] = jnp.concatenate(
        [key.astype(F32), rank, jnp.zeros((SUBS - 2, rows), F32)], axis=0
    )
    spot = key * room + rank.astype(jnp.int32)
    chosen = mask_bf16(iota((owners * room, rows), 0) == spot)
    copies[1].wait()
    notional = in_a_row(notional_ref[...])
    high = notional.astype(BF16).astype(F32)
    info = jnp.concatenate(
        [high, notional - high, local.astype(F32), jnp.zeros((13, rows), F32)], axis=0
    )
    copies[2].wait()
    table = jnp.concatenate([coef_ref[...], info.astype(BF16)], axis=0)
    moved = lax.dot_general(chosen, table, BOTH_LANES, preferred_element_type=F32)
    ids = LANES + extra
    for d in range(owners):
        message = out_ref.at[d]
        block = moved[d * room : (d + 1) * room]
        message[0:room, :] = block[:, 0:LANES].astype(BF16)
        split = [block[part * g : part * (g + 1)] for g in range(plan.groups)]
        lanes = [x[:, LANES:ids] for x in split]
        if plan.groups < 3:
            lanes.append(jnp.zeros((part, extra * (3 - plan.groups)), F32))
        lanes += [x[:, ids : ids + SUBS] for x in split]
        lanes.append(jnp.zeros((part, SUBS * (4 - plan.groups)), F32))
        message[room:, :] = jnp.concatenate(lanes, axis=1).astype(BF16)


def basis_kernel(plan, shocks_hbm, start_hbm, loading_hbm, out_ref, *refs):
    shocks_ref, start_ref, loading_ref, wide_ref, sems = refs
    copies = fetch(
        [loading_hbm, start_hbm, shocks_hbm], [loading_ref, start_ref, shocks_ref], sems
    )
    tenors = loading_ref.shape[0]
    dates = plan.dates
    copies[0].wait()
    copies[1].wait()
    loading_t = jnp.transpose(loading_ref[...])
    drift = 0.5 * STEP * jnp.sum(loading_t * loading_t, axis=1, keepdims=True)
    diag = iota((tenors, tenors), 0) == iota((tenors, tenors), 1)
    log_start = jnp.log(jnp.sum(jnp.where(diag, start_ref[...], 0.0), axis=1, keepdims=True))
    loads = jnp.concatenate(split_bf16((STEP**0.5) * loading_t, 3), axis=1)
    lower = mask_bf16(iota((tenors, tenors), 1) <= iota((tenors, tenors), 0))
    lower = jnp.concatenate([lower, lower], axis=1)
    log_fwd = jnp.broadcast_to(log_start, (tenors, LANES))
    drift = jnp.broadcast_to(drift, (tenors, LANES))
    head = LANES - tenors
    copies[2].wait()
    wide_ref[...] = shocks_ref[...].astype(F32)
    step = plan.width // LANES
    for c in range(dates // step):
        shock = jnp.concatenate(
            [
                wide_ref[pl.ds(c * step + j, tenors, stride=dates), :].astype(BF16)
                for j in range(step)
            ],
            axis=1,
        )
        change = jnp.dot(
            loads, jnp.concatenate([shock] * 3, axis=0), preferred_element_type=F32
        )
        logs = []
        for j in range(step):
            log_fwd = log_fwd + (change[:, LANES * j : LANES * (j + 1)] - drift)
            logs.append(log_fwd)
        fwd = jnp.exp(jnp.concatenate(logs, axis=1))
        growth = split_bf16(jnp.log(1.0 + STEP * fwd), 2)
        summed = jnp.dot(lower, jnp.concatenate(growth, axis=0), preferred_element_type=F32)
        bond = jnp.exp(-summed)
        cols = slice(c * plan.width, (c + 1) * plan.width)
        out_ref[0:tenors, cols] = (bond * fwd * (1.0 / RATE_UNIT)).astype(BF16)
        bond = bond.astype(BF16)
        out_ref[tenors:LANES, cols] = bond[0:head]
        for g in range(plan.groups):
            out_ref[LANES + plan.extra * g : LANES + plan.extra * (g + 1), cols] = bond[head:]
        used = LANES + plan.extra * plan.groups
        out_ref[used:, cols] = jnp.zeros((2 * LANES - used, plan.width), BF16)


def main_kernel(plan, path_total, me_ref, agr_ref, cpty_ref, lag_ref, weight_ref, basis_ref, *refs):
    in_ref, out_ref, val_ref = refs
    me = me_ref[0]
    part, room, dates = plan.part, plan.room, plan.dates
    cpty_dev = weight_ref.shape[0]

    def rows_of(first):
        return in_ref[:, first : first + part, :].reshape(plan.owners * part, LANES)

    rest = rows_of(room)
    lane = iota((1, LANES), 1)
    left, info = [], []
    for g in range(plan.groups):
        keep = mask_bf16((lane >= plan.extra * g) & (lane < plan.extra * (g + 1)))
        left.append(jnp.concatenate([rows_of(part * g), rest * keep], axis=1))
        pick = mask_bf16(iota((SUBS, LANES), 1) == 3 * plan.extra + SUBS * g + iota((SUBS, LANES), 0))
        info.append(lax.dot_general(pick, rest, BOTH_LANES, preferred_element_type=F32))
    left = jnp.concatenate(left, axis=0)
    info = jnp.concatenate(info, axis=1)
    local = info[2:3].astype(jnp.int32)
    agr = jnp.zeros_like(local)
    for n in range(NS_DEV):
        agr = jnp.where(local == n, agr_ref[n] - me * AG_DEV, agr)
    row = iota((SUBS, plan.trades), 0)
    hot = lax.rem(row, AG_DEV) == agr
    netting = jnp.where(hot, jnp.where(row < AG_DEV, info[0:1], info[1:2]), 0.0).astype(BF16)

    width = plan.step
    for c in range(dates * LANES // width):
        cols = slice(c * width, (c + 1) * width)
        under = jnp.dot(left, basis_ref[:, cols], preferred_element_type=F32)
        val_ref[:, cols] = jnp.maximum(under.astype(BF16), 0)
    both = jnp.dot(netting, val_ref[...], preferred_element_type=F32)
    both = both + pltpu.roll(both, AG_DEV, 0)
    owed = [both[:, LANES * t : LANES * (t + 1)] for t in range(dates)]

    member = lax.rem(iota((SUBS, LANES), 0), AG_DEV)
    lag = jnp.zeros((SUBS, LANES), jnp.int32)
    cpty = jnp.zeros((SUBS, LANES), jnp.int32)
    for a in range(AG_DEV):
        lag = jnp.where(member == a, lag_ref[a], lag)
        cpty = jnp.where(member == a, cpty_ref[a] - me * cpty_dev, cpty)
    lags = [lag == s for s in range(1, LAG_MAX + 1)]
    weight = jnp.zeros((SUBS, dates), F32)
    for c in range(cpty_dev):
        weight = jnp.where(cpty[:, 0:dates] == c, weight_ref[c : c + 1, :], weight)
    zero = jnp.zeros((SUBS, LANES), F32)
    spent, slopes = zero, []
    for t in range(dates):
        before = zero
        for s in range(1, min(t, LAG_MAX) + 1):
            before = jnp.where(lags[s - 1], owed[t - s], before)
        excess = owed[t] - before
        square = excess * excess + SMOOTH * SMOOTH
        inverse = lax.rsqrt(square)
        due = weight[:, t : t + 1]
        spent = spent + due * (0.5 * (excess + square * inverse))
        slopes.append(due * (0.5 * (1.0 + excess * inverse)))
    grads = []
    for t in range(dates):
        after = zero
        for s in range(1, min(dates - 1 - t, LAG_MAX) + 1):
            after = jnp.where(lags[s - 1], slopes[t + s], after)
        grads.append(((slopes[t] - after) * (1.0 / path_total)).astype(BF16))

    dots = lax.dot_general(
        jnp.concatenate(grads, axis=1), val_ref[...], BOTH_LANES, preferred_element_type=F32
    )
    share = jnp.sum(jnp.where(hot & (row < AG_DEV), dots, 0.0), axis=0, keepdims=True)
    spent = jnp.sum(spent, axis=1, keepdims=True) * (1.0 / path_total)
    mine = (lane - room == cpty) & (iota((SUBS, LANES), 0) < AG_DEV)
    cva = jnp.sum(jnp.where(mine, spent, 0.0), axis=0, keepdims=True)
    block = lane // part
    count = plan.groups * plan.lines
    lines = jnp.concatenate([share[:, LANES * k : LANES * (k + 1)] for k in range(count)], axis=0)
    moved = [lines if m == 0 else pltpu.roll(lines, part * m, 1) for m in range(plan.per_line)]
    paths = out_ref.shape[0] // plan.owners
    for k in range(plan.lines):
        for s in range(plan.per_line):
            line = cva
            for g in range(plan.groups):
                n = g * plan.lines + k
                line = jnp.where(block == g, moved[(g - s) % plan.per_line][n : n + 1], line)
            for p in range(paths):
                out_ref[(k * plan.per_line + s) * paths + p] = line


def finish_kernel(plan, me_ref, place_ref, notional_ref, in_ref, alloc_ref, cva_ref):
    me = me_ref[0]
    rows = place_ref.shape[1]
    key = place_ref[0:1, :].astype(jnp.int32)
    rank = place_ref[1:2, :].astype(jnp.int32)
    lines = in_ref[...]
    count = lines.shape[0]
    paths = count // plan.owners
    hot = mask_bf16(iota((LANES, rows), 0) == rank)
    pieces = jnp.concatenate(split_bf16(lines, 3), axis=0)
    found = jnp.dot(pieces, hot, preferred_element_type=F32)
    wanted = lax.rem(iota(found.shape, 0), count) // paths == key
    share = jnp.sum(jnp.where(wanted, found, 0.0), axis=0, keepdims=True)
    alloc_ref[...] = share * in_a_row(notional_ref[...])
    own = iota(lines.shape, 0) // paths == me
    cva = jnp.sum(jnp.where(own, lines, 0.0), axis=0, keepdims=True)
    cva_ref[...] = cva[:, plan.room : plan.room + cva_ref.shape[1]]


def body(
    shocks,
    forward_start,
    loading,
    coefficient,
    notional,
    ns_of_trade,
    agr_of_ns,
    cpty_of_agr,
    margin_lag,
    default_weight,
):
    owners = lax.axis_size("trade")
    path_parts = lax.axis_size("path")
    tenors, dates, path_dev = shocks.shape
    path_total = float(path_dev * path_parts)
    rows = coefficient.shape[0]
    lines = rows // LANES
    plan = Plan(owners, rows, tenors, dates)
    cols = dates * path_dev
    me = lax.axis_index("trade").astype(jnp.int32).reshape(1)
    notional = notional.reshape(lines, LANES)

    place, outgoing = pl.pallas_call(
        functools.partial(pack_kernel, plan),
        out_shape=[
            jax.ShapeDtypeStruct((SUBS, rows), F32),
            jax.ShapeDtypeStruct((owners, plan.height, LANES), BF16),
        ],
        in_specs=[SMEM] + [HBM] * 3,
        out_specs=[VMEM, VMEM],
        scratch_shapes=[
            pltpu.VMEM((owners * lines, LANES), jnp.int32),
            pltpu.VMEM((2 * tenors, rows), BF16),
            pltpu.VMEM((lines, LANES), F32),
            pltpu.SemaphoreType.DMA((3,)),
        ],
        name="pack",
    )(me, ns_of_trade.reshape(owners * lines, LANES), coefficient.T, notional)
    incoming = lax.all_to_all(outgoing, "trade", split_axis=0, concat_axis=0, tiled=True)

    basis = pl.pallas_call(
        functools.partial(basis_kernel, plan),
        out_shape=jax.ShapeDtypeStruct((2 * LANES, cols), BF16),
        in_specs=[HBM] * 3,
        out_specs=VMEM,
        scratch_shapes=[
            pltpu.VMEM((tenors * dates, path_dev), BF16),
            pltpu.VMEM((1, tenors), F32),
            pltpu.VMEM((tenors, tenors), F32),
            pltpu.VMEM((tenors * dates, path_dev), F32),
            pltpu.SemaphoreType.DMA((3,)),
        ],
        name="basis",
        compiler_params=pltpu.CompilerParams(vmem_limit_bytes=16 << 20),
        cost_estimate=pl.CostEstimate(
            flops=2 * 400 * tenors * cols, bytes_accessed=4 << 20, transcendentals=3 * tenors * cols
        ),
    )(shocks.reshape(tenors * dates, path_dev), forward_start.reshape(1, tenors), loading)

    need = 2 * plan.trades * cols + 8 * plan.trades * plan.step + (8 << 20)
    lines_out = pl.pallas_call(
        functools.partial(main_kernel, plan, path_total),
        out_shape=jax.ShapeDtypeStruct((owners * path_parts, 1, LANES), F32),
        in_specs=[SMEM] * 4 + [VMEM] * 3,
        out_specs=VMEM,
        scratch_shapes=[pltpu.VMEM((plan.trades, cols), BF16)],
        name="value_and_allocate",
        compiler_params=pltpu.CompilerParams(vmem_limit_bytes=need),
    )(me, agr_of_ns, cpty_of_agr, margin_lag, default_weight, basis, incoming)

    lines_in = lax.all_to_all(lines_out, ("trade", "path"), split_axis=0, concat_axis=0, tiled=True)
    lines_in = lines_in.reshape(owners * path_parts, LANES)
    allocation, cva = pl.pallas_call(
        functools.partial(finish_kernel, plan),
        out_shape=[
            jax.ShapeDtypeStruct((1, rows), F32),
            jax.ShapeDtypeStruct((1, default_weight.shape[0]), F32),
        ],
        in_specs=[SMEM] + [VMEM] * 3,
        out_specs=[VMEM, VMEM],
        name="finish",
        compiler_params=pltpu.CompilerParams(vmem_limit_bytes=32 << 20),
    )(me, place, notional, lines_in)
    return (allocation.reshape(rows), cva.reshape(default_weight.shape[0]))


def solution(mesh):
    placed = (
        P(None, None, "path"),
        P(),
        P(),
        P("trade", None),
        P("trade"),
        P(),
        P("trade"),
        P("trade"),
        P("trade"),
        P("trade", None),
    )
    return jax.shard_map(
        body, mesh=mesh, in_specs=placed, out_specs=(P("trade"), P("trade")), check_vma=False
    )
```

```python
import functools

import jax
import jax.numpy as jnp
from jax import lax
from jax.experimental import pallas as pl
from jax.experimental.pallas import tpu as pltpu
from jax.sharding import PartitionSpec as P

NS_DEV = 8
AG_DEV = 4
LAG_MAX = 4
LANES = 128
SUBS = 8

RATE_UNIT = 0.03
STEP = 0.25
SMOOTH = 0.5

F32 = jnp.float32
BF16 = jnp.bfloat16
VMEM = pl.BlockSpec(memory_space=pltpu.VMEM)
SMEM = pl.BlockSpec(memory_space=pltpu.SMEM)
HBM = pl.BlockSpec(memory_space=pltpu.HBM)
BOTH_LANES = (((1,), (1,)), ((), ()))


def iota(shape, dim):
    return lax.broadcasted_iota(jnp.int32, shape, dim)


def mask_bf16(mask):
    return mask.astype(F32).astype(BF16)


def split_bf16(x, parts):
    pieces = []
    for _ in range(parts):
        piece = x.astype(BF16)
        pieces.append(piece)
        x = x - piece.astype(F32)
    return pieces


def fetch(sources, targets, sems):
    copies = [pltpu.make_async_copy(a, b, sems.at[n]) for n, (a, b) in enumerate(zip(sources, targets))]
    for copy in copies:
        copy.start()
    return copies


def in_a_row(x):
    return jnp.concatenate([x[r : r + 1] for r in range(x.shape[0])], axis=1)


class Plan:
    def __init__(self, owners, rows, tenors, dates):
        most = 3 * rows // (2 * owners)
        self.owners = owners
        self.groups = 3 if most % 48 == 0 else 1
        self.part = -(-most // (16 * self.groups)) * 16
        self.room = self.groups * self.part
        self.height = self.room + self.part
        self.extra = 2 * tenors - LANES
        self.per_line = LANES // self.part
        self.lines = owners * self.part // LANES
        self.trades = owners * self.room
        self.dates = dates
        self.width = 512
        self.step = 2048 if self.trades <= 1024 else 512


def pack_kernel(plan, me_ref, sets_hbm, coef_hbm, notional_hbm, place_ref, out_ref, *refs):
    sets_ref, coef_ref, notional_ref, sems = refs
    copies = fetch(
        [sets_hbm, notional_hbm, coef_hbm], [sets_ref, notional_ref, coef_ref], sems
    )
    me = me_ref[0]
    owners, part, room, extra = plan.owners, plan.part, plan.room, plan.extra
    lines = notional_ref.shape[0]
    rows = lines * LANES
    shared = SUBS // lines
    copies[0].wait()
    block = sets_ref[pl.ds(pl.multiple_of(me // shared * SUBS, SUBS), SUBS), :]
    own = block[0:lines]
    for b in range(1, shared):
        own = jnp.where(lax.rem(me, shared) == b, block[b * lines : (b + 1) * lines], own)
    sets = in_a_row(own)
    key = lax.shift_right_logical(sets, 3)
    local = sets - key * NS_DEV
    hot = iota((owners, rows), 0) == key
    before = mask_bf16(iota((rows, rows), 0) < iota((rows, rows), 1))
    count = jnp.dot(mask_bf16(hot), before, preferred_element_type=F32)
    rank = jnp.sum(jnp.where(hot, count, 0.0), axis=0, keepdims=True)
    place_ref[...] = jnp.concatenate(
        [key.astype(F32), rank, jnp.zeros((SUBS - 2, rows), F32)], axis=0
    )
    spot = key * room + rank.astype(jnp.int32)
    chosen = mask_bf16(iota((owners * room, rows), 0) == spot)
    copies[1].wait()
    notional = in_a_row(notional_ref[...])
    high = notional.astype(BF16).astype(F32)
    info = jnp.concatenate(
        [high, notional - high, local.astype(F32), jnp.zeros((13, rows), F32)], axis=0
    )
    copies[2].wait()
    table = jnp.concatenate([coef_ref[...], info.astype(BF16)], axis=0)
    moved = lax.dot_general(chosen, table, BOTH_LANES, preferred_element_type=F32)
    ids = LANES + extra
    for d in range(owners):
        message = out_ref.at[d]
        block = moved[d * room : (d + 1) * room]
        message[0:room, :] = block[:, 0:LANES].astype(BF16)
        split = [block[part * g : part * (g + 1)] for g in range(plan.groups)]
        lanes = [x[:, LANES:ids] for x in split]
        if plan.groups < 3:
            lanes.append(jnp.zeros((part, extra * (3 - plan.groups)), F32))
        lanes += [x[:, ids : ids + SUBS] for x in split]
        lanes.append(jnp.zeros((part, SUBS * (4 - plan.groups)), F32))
        message[room:, :] = jnp.concatenate(lanes, axis=1).astype(BF16)


def basis_kernel(plan, shocks_hbm, start_hbm, loading_hbm, out_ref, *refs):
    shocks_ref, start_ref, loading_ref, wide_ref, sems = refs
    copies = fetch(
        [loading_hbm, start_hbm, shocks_hbm], [loading_ref, start_ref, shocks_ref], sems
    )
    tenors = loading_ref.shape[0]
    dates = plan.dates
    copies[0].wait()
    copies[1].wait()
    loading_t = jnp.transpose(loading_ref[...])
    drift = 0.5 * STEP * jnp.sum(loading_t * loading_t, axis=1, keepdims=True)
    diag = iota((tenors, tenors), 0) == iota((tenors, tenors), 1)
    log_start = jnp.log(jnp.sum(jnp.where(diag, start_ref[...], 0.0), axis=1, keepdims=True))
    loads = jnp.concatenate(split_bf16((STEP**0.5) * loading_t, 3), axis=1)
    lower = mask_bf16(iota((tenors, tenors), 1) <= iota((tenors, tenors), 0))
    lower = jnp.concatenate([lower, lower], axis=1)
    log_fwd = jnp.broadcast_to(log_start, (tenors, LANES))
    drift = jnp.broadcast_to(drift, (tenors, LANES))
    head = LANES - tenors
    copies[2].wait()
    wide_ref[...] = shocks_ref[...].astype(F32)
    step = plan.width // LANES
    for c in range(dates // step):
        shock = jnp.concatenate(
            [
                wide_ref[pl.ds(c * step + j, tenors, stride=dates), :].astype(BF16)
                for j in range(step)
            ],
            axis=1,
        )
        change = jnp.dot(
            loads, jnp.concatenate([shock] * 3, axis=0), preferred_element_type=F32
        )
        logs = []
        for j in range(step):
            log_fwd = log_fwd + (change[:, LANES * j : LANES * (j + 1)] - drift)
            logs.append(log_fwd)
        fwd = jnp.exp(jnp.concatenate(logs, axis=1))
        growth = split_bf16(jnp.log(1.0 + STEP * fwd), 2)
        summed = jnp.dot(lower, jnp.concatenate(growth, axis=0), preferred_element_type=F32)
        bond = jnp.exp(-summed)
        cols = slice(c * plan.width, (c + 1) * plan.width)
        out_ref[0:tenors, cols] = (bond * fwd * (1.0 / RATE_UNIT)).astype(BF16)
        bond = bond.astype(BF16)
        out_ref[tenors:LANES, cols] = bond[0:head]
        for g in range(plan.groups):
            out_ref[LANES + plan.extra * g : LANES + plan.extra * (g + 1), cols] = bond[head:]
        used = LANES + plan.extra * plan.groups
        out_ref[used:, cols] = jnp.zeros((2 * LANES - used, plan.width), BF16)


def main_kernel(plan, path_total, me_ref, agr_ref, cpty_ref, lag_ref, weight_ref, basis_ref, *refs):
    in_ref, out_ref, val_ref = refs
    me = me_ref[0]
    part, room, dates = plan.part, plan.room, plan.dates
    cpty_dev = weight_ref.shape[0]

    def rows_of(first):
        return in_ref[:, first : first + part, :].reshape(plan.owners * part, LANES)

    rest = rows_of(room)
    lane = iota((1, LANES), 1)
    left, info = [], []
    for g in range(plan.groups):
        keep = mask_bf16((lane >= plan.extra * g) & (lane < plan.extra * (g + 1)))
        left.append(jnp.concatenate([rows_of(part * g), rest * keep], axis=1))
        pick = mask_bf16(iota((SUBS, LANES), 1) == 3 * plan.extra + SUBS * g + iota((SUBS, LANES), 0))
        info.append(lax.dot_general(pick, rest, BOTH_LANES, preferred_element_type=F32))
    left = jnp.concatenate(left, axis=0)
    info = jnp.concatenate(info, axis=1)
    local = info[2:3].astype(jnp.int32)
    agr = jnp.zeros_like(local)
    for n in range(NS_DEV):
        agr = jnp.where(local == n, agr_ref[n] - me * AG_DEV, agr)
    row = iota((SUBS, plan.trades), 0)
    hot = lax.rem(row, AG_DEV) == agr
    netting = jnp.where(hot, jnp.where(row < AG_DEV, info[0:1], info[1:2]), 0.0).astype(BF16)

    width = plan.step
    for c in range(dates * LANES // width):
        cols = slice(c * width, (c + 1) * width)
        under = jnp.dot(left, basis_ref[:, cols], preferred_element_type=F32)
        val_ref[:, cols] = jnp.maximum(under.astype(BF16), 0)
    both = jnp.dot(netting, val_ref[...], preferred_element_type=F32)
    both = both + pltpu.roll(both, AG_DEV, 0)
    owed = [both[:, LANES * t : LANES * (t + 1)] for t in range(dates)]

    member = lax.rem(iota((SUBS, LANES), 0), AG_DEV)
    lag = jnp.zeros((SUBS, LANES), jnp.int32)
    cpty = jnp.zeros((SUBS, LANES), jnp.int32)
    for a in range(AG_DEV):
        lag = jnp.where(member == a, lag_ref[a], lag)
        cpty = jnp.where(member == a, cpty_ref[a] - me * cpty_dev, cpty)
    lags = [lag == s for s in range(1, LAG_MAX + 1)]
    weight = jnp.zeros((SUBS, dates), F32)
    for c in range(cpty_dev):
        weight = jnp.where(cpty[:, 0:dates] == c, weight_ref[c : c + 1, :], weight)
    zero = jnp.zeros((SUBS, LANES), F32)
    spent, slopes = zero, []
    for t in range(dates):
        before = zero
        for s in range(1, min(t, LAG_MAX) + 1):
            before = jnp.where(lags[s - 1], owed[t - s], before)
        excess = owed[t] - before
        square = excess * excess + SMOOTH * SMOOTH
        inverse = lax.rsqrt(square)
        due = weight[:, t : t + 1]
        spent = spent + due * (0.5 * (excess + square * inverse))
        slopes.append(due * (0.5 * (1.0 + excess * inverse)))
    grads = []
    for t in range(dates):
        after = zero
        for s in range(1, min(dates - 1 - t, LAG_MAX) + 1):
            after = jnp.where(lags[s - 1], slopes[t + s], after)
        grads.append(((slopes[t] - after) * (1.0 / path_total)).astype(BF16))

    dots = lax.dot_general(
        jnp.concatenate(grads, axis=1), val_ref[...], BOTH_LANES, preferred_element_type=F32
    )
    share = jnp.sum(jnp.where(hot & (row < AG_DEV), dots, 0.0), axis=0, keepdims=True)
    spent = jnp.sum(spent, axis=1, keepdims=True) * (1.0 / path_total)
    mine = (lane - room == cpty) & (iota((SUBS, LANES), 0) < AG_DEV)
    cva = jnp.sum(jnp.where(mine, spent, 0.0), axis=0, keepdims=True)
    block = lane // part
    count = plan.groups * plan.lines
    lines = jnp.concatenate([share[:, LANES * k : LANES * (k + 1)] for k in range(count)], axis=0)
    moved = [lines if m == 0 else pltpu.roll(lines, part * m, 1) for m in range(plan.per_line)]
    paths = out_ref.shape[0] // plan.owners
    for k in range(plan.lines):
        for s in range(plan.per_line):
            line = cva
            for g in range(plan.groups):
                n = g * plan.lines + k
                line = jnp.where(block == g, moved[(g - s) % plan.per_line][n : n + 1], line)
            for p in range(paths):
                out_ref[(k * plan.per_line + s) * paths + p] = line


def finish_kernel(plan, me_ref, place_ref, notional_ref, in_ref, alloc_ref, cva_ref):
    me = me_ref[0]
    rows = place_ref.shape[1]
    key = place_ref[0:1, :].astype(jnp.int32)
    rank = place_ref[1:2, :].astype(jnp.int32)
    lines = in_ref[...]
    count = lines.shape[0]
    paths = count // plan.owners
    hot = mask_bf16(iota((LANES, rows), 0) == rank)
    pieces = jnp.concatenate(split_bf16(lines, 3), axis=0)
    found = jnp.dot(pieces, hot, preferred_element_type=F32)
    wanted = lax.rem(iota(found.shape, 0), count) // paths == key
    share = jnp.sum(jnp.where(wanted, found, 0.0), axis=0, keepdims=True)
    alloc_ref[...] = share * in_a_row(notional_ref[...])
    own = iota(lines.shape, 0) // paths == me
    cva = jnp.sum(jnp.where(own, lines, 0.0), axis=0, keepdims=True)
    cva_ref[...] = cva[:, plan.room : plan.room + cva_ref.shape[1]]


def body(
    shocks,
    forward_start,
    loading,
    coefficient,
    notional,
    ns_of_trade,
    agr_of_ns,
    cpty_of_agr,
    margin_lag,
    default_weight,
):
    owners = lax.axis_size("trade")
    path_parts = lax.axis_size("path")
    tenors, dates, path_dev = shocks.shape
    path_total = float(path_dev * path_parts)
    rows = coefficient.shape[0]
    lines = rows // LANES
    plan = Plan(owners, rows, tenors, dates)
    cols = dates * path_dev
    me = lax.axis_index("trade").astype(jnp.int32).reshape(1)
    notional = notional.reshape(lines, LANES)

    place, outgoing = pl.pallas_call(
        functools.partial(pack_kernel, plan),
        out_shape=[
            jax.ShapeDtypeStruct((SUBS, rows), F32),
            jax.ShapeDtypeStruct((owners, plan.height, LANES), BF16),
        ],
        in_specs=[SMEM] + [HBM] * 3,
        out_specs=[VMEM, VMEM],
        scratch_shapes=[
            pltpu.VMEM((owners * lines, LANES), jnp.int32),
            pltpu.VMEM((2 * tenors, rows), BF16),
            pltpu.VMEM((lines, LANES), F32),
            pltpu.SemaphoreType.DMA((3,)),
        ],
        name="pack",
        cost_estimate=pl.CostEstimate(flops=1 << 32, bytes_accessed=1 << 19, transcendentals=0),
    )(me, ns_of_trade.reshape(owners * lines, LANES), coefficient.T, notional)
    incoming = lax.all_to_all(outgoing, "trade", split_axis=0, concat_axis=0, tiled=True)

    basis = pl.pallas_call(
        functools.partial(basis_kernel, plan),
        out_shape=jax.ShapeDtypeStruct((2 * LANES, cols), BF16),
        in_specs=[HBM] * 3,
        out_specs=VMEM,
        scratch_shapes=[
            pltpu.VMEM((tenors * dates, path_dev), BF16),
            pltpu.VMEM((1, tenors), F32),
            pltpu.VMEM((tenors, tenors), F32),
            pltpu.VMEM((tenors * dates, path_dev), F32),
            pltpu.SemaphoreType.DMA((3,)),
        ],
        name="basis",
        compiler_params=pltpu.CompilerParams(vmem_limit_bytes=16 << 20),
        cost_estimate=pl.CostEstimate(
            flops=2 * 400 * tenors * cols, bytes_accessed=4 << 20, transcendentals=3 * tenors * cols
        ),
    )(shocks.reshape(tenors * dates, path_dev), forward_start.reshape(1, tenors), loading)

    need = 2 * plan.trades * cols + 8 * plan.trades * plan.step + (8 << 20)
    lines_out = pl.pallas_call(
        functools.partial(main_kernel, plan, path_total),
        out_shape=jax.ShapeDtypeStruct((owners * path_parts, 1, LANES), F32),
        in_specs=[SMEM] * 4 + [VMEM] * 3,
        out_specs=VMEM,
        scratch_shapes=[pltpu.VMEM((plan.trades, cols), BF16)],
        name="value_and_allocate",
        compiler_params=pltpu.CompilerParams(vmem_limit_bytes=need),
    )(me, agr_of_ns, cpty_of_agr, margin_lag, default_weight, basis, incoming)

    lines_in = lax.all_to_all(lines_out, ("trade", "path"), split_axis=0, concat_axis=0, tiled=True)
    lines_in = lines_in.reshape(owners * path_parts, LANES)
    allocation, cva = pl.pallas_call(
        functools.partial(finish_kernel, plan),
        out_shape=[
            jax.ShapeDtypeStruct((1, rows), F32),
            jax.ShapeDtypeStruct((1, default_weight.shape[0]), F32),
        ],
        in_specs=[SMEM] + [VMEM] * 3,
        out_specs=[VMEM, VMEM],
        name="finish",
        compiler_params=pltpu.CompilerParams(vmem_limit_bytes=32 << 20),
    )(me, place, notional, lines_in)
    return (allocation.reshape(rows), cva.reshape(default_weight.shape[0]))


def solution(mesh):
    placed = (
        P(None, None, "path"),
        P(),
        P(),
        P("trade", None),
        P("trade"),
        P(),
        P("trade"),
        P("trade"),
        P("trade"),
        P("trade", None),
    )
    return jax.shard_map(
        body, mesh=mesh, in_specs=placed, out_specs=(P("trade"), P("trade")), check_vma=False
    )
```

```python
import functools

import jax
import jax.numpy as jnp
from jax import lax
from jax.experimental import pallas as pl
from jax.experimental.pallas import tpu as pltpu
from jax.sharding import PartitionSpec as P

NS_DEV = 8
AG_DEV = 4
LAG_MAX = 4
LANES = 128
SUBS = 8

RATE_UNIT = 0.03
STEP = 0.25
SMOOTH = 0.5

F32 = jnp.float32
BF16 = jnp.bfloat16
VMEM = pl.BlockSpec(memory_space=pltpu.VMEM)
SMEM = pl.BlockSpec(memory_space=pltpu.SMEM)
HBM = pl.BlockSpec(memory_space=pltpu.HBM)
BOTH_LANES = (((1,), (1,)), ((), ()))


def iota(shape, dim):
    return lax.broadcasted_iota(jnp.int32, shape, dim)


def mask_bf16(mask):
    return mask.astype(F32).astype(BF16)


def split_bf16(x, parts):
    pieces = []
    for _ in range(parts):
        piece = x.astype(BF16)
        pieces.append(piece)
        x = x - piece.astype(F32)
    return pieces


def fetch(sources, targets, sems):
    copies = [pltpu.make_async_copy(a, b, sems.at[n]) for n, (a, b) in enumerate(zip(sources, targets))]
    for copy in copies:
        copy.start()
    return copies


def in_a_row(x):
    return jnp.concatenate([x[r : r + 1] for r in range(x.shape[0])], axis=1)


class Plan:
    def __init__(self, owners, rows, tenors, dates):
        most = 3 * rows // (2 * owners)
        self.owners = owners
        self.halves = 2 if most % 96 == 0 else 1
        most = most // self.halves
        self.groups = 3 if most % 48 == 0 else 1
        self.part = -(-most // (16 * self.groups)) * 16
        self.room = self.groups * self.part
        self.height = self.room + self.part
        self.extra = 2 * tenors - LANES
        self.per_line = LANES // self.part
        self.lines = owners * self.part // LANES
        self.slots = self.halves * self.room
        self.trades = owners * self.slots
        self.dates = dates
        self.width = 512
        self.step = 2048 if self.trades <= 1024 else 512


def pack_kernel(plan, me_ref, half_ref, sets_hbm, coef_hbm, notional_hbm, place_ref, out_ref, *refs):
    sets_ref, coef_ref, notional_ref, sems = refs
    copies = fetch(
        [sets_hbm, notional_hbm, coef_hbm], [sets_ref, notional_ref, coef_ref], sems
    )
    me = me_ref[0]
    owners, part, room, extra = plan.owners, plan.part, plan.room, plan.extra
    lines = notional_ref.shape[0]
    rows = lines * LANES
    shared = SUBS // lines
    copies[0].wait()
    block = sets_ref[pl.ds(pl.multiple_of(me // shared * SUBS, SUBS), SUBS), :]
    own = block[0:lines]
    for b in range(1, shared):
        own = jnp.where(lax.rem(me, shared) == b, block[b * lines : (b + 1) * lines], own)
    sets = in_a_row(own)
    key = lax.shift_right_logical(sets, 3)
    local = sets - key * NS_DEV
    hot = iota((owners, rows), 0) == key
    before = mask_bf16(iota((rows, rows), 0) < iota((rows, rows), 1))
    count = jnp.dot(mask_bf16(hot), before, preferred_element_type=F32)
    rank = jnp.sum(jnp.where(hot, count, 0.0), axis=0, keepdims=True)
    place_ref[...] = jnp.concatenate(
        [key.astype(F32), rank, jnp.zeros((SUBS - 2, rows), F32)], axis=0
    )
    mine = rank.astype(jnp.int32) - room * half_ref[0]
    spot = jnp.where((mine >= 0) & (mine < room), key * room + mine, -1)
    chosen = mask_bf16(iota((owners * room, rows), 0) == spot)
    copies[1].wait()
    notional = in_a_row(notional_ref[...])
    high = notional.astype(BF16).astype(F32)
    info = jnp.concatenate(
        [high, notional - high, local.astype(F32), jnp.zeros((13, rows), F32)], axis=0
    )
    copies[2].wait()
    table = jnp.concatenate([coef_ref[...], info.astype(BF16)], axis=0)
    moved = lax.dot_general(chosen, table, BOTH_LANES, preferred_element_type=F32)
    ids = LANES + extra
    for d in range(owners):
        message = out_ref.at[d]
        block = moved[d * room : (d + 1) * room]
        message[0:room, :] = block[:, 0:LANES].astype(BF16)
        split = [block[part * g : part * (g + 1)] for g in range(plan.groups)]
        lanes = [x[:, LANES:ids] for x in split]
        if plan.groups < 3:
            lanes.append(jnp.zeros((part, extra * (3 - plan.groups)), F32))
        lanes += [x[:, ids : ids + SUBS] for x in split]
        lanes.append(jnp.zeros((part, SUBS * (4 - plan.groups)), F32))
        message[room:, :] = jnp.concatenate(lanes, axis=1).astype(BF16)


def basis_kernel(plan, shocks_hbm, start_hbm, loading_hbm, out_ref, *refs):
    shocks_ref, start_ref, loading_ref, wide_ref, sems = refs
    copies = fetch(
        [loading_hbm, start_hbm, shocks_hbm], [loading_ref, start_ref, shocks_ref], sems
    )
    tenors = loading_ref.shape[0]
    dates = plan.dates
    copies[0].wait()
    copies[1].wait()
    loading_t = jnp.transpose(loading_ref[...])
    drift = 0.5 * STEP * jnp.sum(loading_t * loading_t, axis=1, keepdims=True)
    diag = iota((tenors, tenors), 0) == iota((tenors, tenors), 1)
    log_start = jnp.log(jnp.sum(jnp.where(diag, start_ref[...], 0.0), axis=1, keepdims=True))
    loads = jnp.concatenate(split_bf16((STEP**0.5) * loading_t, 3), axis=1)
    lower = mask_bf16(iota((tenors, tenors), 1) <= iota((tenors, tenors), 0))
    lower = jnp.concatenate([lower, lower], axis=1)
    log_fwd = jnp.broadcast_to(log_start, (tenors, LANES))
    drift = jnp.broadcast_to(drift, (tenors, LANES))
    head = LANES - tenors
    copies[2].wait()
    wide_ref[...] = shocks_ref[...].astype(F32)
    step = plan.width // LANES
    for c in range(dates // step):
        shock = jnp.concatenate(
            [
                wide_ref[pl.ds(c * step + j, tenors, stride=dates), :].astype(BF16)
                for j in range(step)
            ],
            axis=1,
        )
        change = jnp.dot(
            loads, jnp.concatenate([shock] * 3, axis=0), preferred_element_type=F32
        )
        logs = []
        for j in range(step):
            log_fwd = log_fwd + (change[:, LANES * j : LANES * (j + 1)] - drift)
            logs.append(log_fwd)
        fwd = jnp.exp(jnp.concatenate(logs, axis=1))
        growth = split_bf16(jnp.log(1.0 + STEP * fwd), 2)
        summed = jnp.dot(lower, jnp.concatenate(growth, axis=0), preferred_element_type=F32)
        bond = jnp.exp(-summed)
        cols = slice(c * plan.width, (c + 1) * plan.width)
        out_ref[0:tenors, cols] = (bond * fwd * (1.0 / RATE_UNIT)).astype(BF16)
        bond = bond.astype(BF16)
        out_ref[tenors:LANES, cols] = bond[0:head]
        for g in range(plan.groups):
            out_ref[LANES + plan.extra * g : LANES + plan.extra * (g + 1), cols] = bond[head:]
        used = LANES + plan.extra * plan.groups
        out_ref[used:, cols] = jnp.zeros((2 * LANES - used, plan.width), BF16)


def main_kernel(plan, path_total, me_ref, agr_ref, cpty_ref, lag_ref, weight_ref, basis_ref, *refs):
    *in_refs, out_ref, val_ref = refs
    me = me_ref[0]
    part, room, dates = plan.part, plan.room, plan.dates
    cpty_dev = weight_ref.shape[0]

    lane = iota((1, LANES), 1)
    left, info = [], []
    for in_ref in in_refs:
        rest = in_ref[:, room:, :].reshape(plan.owners * part, LANES)
        for g in range(plan.groups):
            main = in_ref[:, part * g : part * (g + 1), :].reshape(plan.owners * part, LANES)
            keep = mask_bf16((lane >= plan.extra * g) & (lane < plan.extra * (g + 1)))
            left.append(jnp.concatenate([main, rest * keep], axis=1))
            first = 3 * plan.extra + SUBS * g
            pick = mask_bf16(iota((SUBS, LANES), 1) == first + iota((SUBS, LANES), 0))
            info.append(lax.dot_general(pick, rest, BOTH_LANES, preferred_element_type=F32))
    left = jnp.concatenate(left, axis=0)
    info = jnp.concatenate(info, axis=1)
    local = info[2:3].astype(jnp.int32)
    agr = jnp.zeros_like(local)
    for n in range(NS_DEV):
        agr = jnp.where(local == n, agr_ref[n] - me * AG_DEV, agr)
    row = iota((SUBS, plan.trades), 0)
    hot = lax.rem(row, AG_DEV) == agr
    netting = jnp.where(hot, jnp.where(row < AG_DEV, info[0:1], info[1:2]), 0.0).astype(BF16)

    width = plan.step
    for c in range(dates * LANES // width):
        cols = slice(c * width, (c + 1) * width)
        under = jnp.dot(left, basis_ref[:, cols], preferred_element_type=F32)
        val_ref[:, cols] = jnp.maximum(under.astype(BF16), 0)
    both = jnp.dot(netting, val_ref[...], preferred_element_type=F32)
    both = both + pltpu.roll(both, AG_DEV, 0)
    owed = [both[:, LANES * t : LANES * (t + 1)] for t in range(dates)]

    member = lax.rem(iota((SUBS, LANES), 0), AG_DEV)
    lag = jnp.zeros((SUBS, LANES), jnp.int32)
    cpty = jnp.zeros((SUBS, LANES), jnp.int32)
    for a in range(AG_DEV):
        lag = jnp.where(member == a, lag_ref[a], lag)
        cpty = jnp.where(member == a, cpty_ref[a] - me * cpty_dev, cpty)
    lags = [lag == s for s in range(1, LAG_MAX + 1)]
    weight = jnp.zeros((SUBS, dates), F32)
    for c in range(cpty_dev):
        weight = jnp.where(cpty[:, 0:dates] == c, weight_ref[c : c + 1, :], weight)
    zero = jnp.zeros((SUBS, LANES), F32)
    spent, slopes = zero, []
    for t in range(dates):
        before = zero
        for s in range(1, min(t, LAG_MAX) + 1):
            before = jnp.where(lags[s - 1], owed[t - s], before)
        excess = owed[t] - before
        square = excess * excess + SMOOTH * SMOOTH
        inverse = lax.rsqrt(square)
        due = weight[:, t : t + 1]
        spent = spent + due * (0.5 * (excess + square * inverse))
        slopes.append(due * (0.5 * (1.0 + excess * inverse)))
    grads = []
    for t in range(dates):
        after = zero
        for s in range(1, min(dates - 1 - t, LAG_MAX) + 1):
            after = jnp.where(lags[s - 1], slopes[t + s], after)
        grads.append(((slopes[t] - after) * (1.0 / path_total)).astype(BF16))

    dots = lax.dot_general(
        jnp.concatenate(grads, axis=1), val_ref[...], BOTH_LANES, preferred_element_type=F32
    )
    share = jnp.sum(jnp.where(hot & (row < AG_DEV), dots, 0.0), axis=0, keepdims=True)
    spent = jnp.sum(spent, axis=1, keepdims=True) * (1.0 / path_total)
    mine = (lane - plan.slots == cpty) & (iota((SUBS, LANES), 0) < AG_DEV)
    cva = jnp.sum(jnp.where(mine, spent, 0.0), axis=0, keepdims=True)
    block = lane // part
    parts = plan.slots // part
    count = parts * plan.lines
    lines = jnp.concatenate([share[:, LANES * k : LANES * (k + 1)] for k in range(count)], axis=0)
    moved = [lines if m == 0 else pltpu.roll(lines, part * m, 1) for m in range(plan.per_line)]
    paths = out_ref.shape[0] // plan.owners
    for k in range(plan.lines):
        for s in range(plan.per_line):
            line = cva
            for g in range(parts):
                n = g * plan.lines + k
                line = jnp.where(block == g, moved[(g - s) % plan.per_line][n : n + 1], line)
            for p in range(paths):
                out_ref[(k * plan.per_line + s) * paths + p] = line


def finish_kernel(plan, me_ref, place_ref, notional_ref, in_ref, alloc_ref, cva_ref):
    me = me_ref[0]
    rows = place_ref.shape[1]
    key = place_ref[0:1, :].astype(jnp.int32)
    rank = place_ref[1:2, :].astype(jnp.int32)
    lines = in_ref[...]
    count = lines.shape[0]
    paths = count // plan.owners
    pieces = jnp.concatenate(split_bf16(lines, 3), axis=0)
    half = lax.rem(lax.rem(iota((pieces.shape[0], rows), 0), paths), plan.halves)
    found = jnp.zeros(half.shape, F32)
    for h in range(plan.halves):
        slot = lax.rem(rank + plan.room * h, plan.slots)
        hot = mask_bf16(iota((LANES, rows), 0) == slot)
        found = jnp.where(half == h, jnp.dot(pieces, hot, preferred_element_type=F32), found)
    wanted = lax.rem(iota(found.shape, 0), count) // paths == key
    share = jnp.sum(jnp.where(wanted, found, 0.0), axis=0, keepdims=True)
    alloc_ref[...] = share * in_a_row(notional_ref[...])
    own = iota(lines.shape, 0) // paths == me
    cva = jnp.sum(jnp.where(own, lines, 0.0), axis=0, keepdims=True)
    cva_ref[...] = cva[:, plan.slots : plan.slots + cva_ref.shape[1]]


def body(
    shocks,
    forward_start,
    loading,
    coefficient,
    notional,
    ns_of_trade,
    agr_of_ns,
    cpty_of_agr,
    margin_lag,
    default_weight,
):
    owners = lax.axis_size("trade")
    path_parts = lax.axis_size("path")
    tenors, dates, path_dev = shocks.shape
    path_total = float(path_dev * path_parts)
    rows = coefficient.shape[0]
    lines = rows // LANES
    plan = Plan(owners, rows, tenors, dates)
    cols = dates * path_dev
    me = lax.axis_index("trade").astype(jnp.int32).reshape(1)
    half = lax.rem(lax.axis_index("path").astype(jnp.int32), plan.halves).reshape(1)
    notional = notional.reshape(lines, LANES)

    place, outgoing = pl.pallas_call(
        functools.partial(pack_kernel, plan),
        out_shape=[
            jax.ShapeDtypeStruct((SUBS, rows), F32),
            jax.ShapeDtypeStruct((owners, plan.height, LANES), BF16),
        ],
        in_specs=[SMEM] * 2 + [HBM] * 3,
        out_specs=[VMEM, VMEM],
        scratch_shapes=[
            pltpu.VMEM((owners * lines, LANES), jnp.int32),
            pltpu.VMEM((2 * tenors, rows), BF16),
            pltpu.VMEM((lines, LANES), F32),
            pltpu.SemaphoreType.DMA((3,)),
        ],
        name="pack",
        cost_estimate=pl.CostEstimate(flops=1 << 32, bytes_accessed=1 << 19, transcendentals=0),
    )(me, half, ns_of_trade.reshape(owners * lines, LANES), coefficient.T, notional)
    incoming = [lax.all_to_all(outgoing, "trade", split_axis=0, concat_axis=0, tiled=True)]
    if plan.halves == 2:
        pairs = [(p, p ^ 1) for p in range(path_parts)]
        incoming.append(lax.ppermute(incoming[0], "path", pairs))

    basis = pl.pallas_call(
        functools.partial(basis_kernel, plan),
        out_shape=jax.ShapeDtypeStruct((2 * LANES, cols), BF16),
        in_specs=[HBM] * 3,
        out_specs=VMEM,
        scratch_shapes=[
            pltpu.VMEM((tenors * dates, path_dev), BF16),
            pltpu.VMEM((1, tenors), F32),
            pltpu.VMEM((tenors, tenors), F32),
            pltpu.VMEM((tenors * dates, path_dev), F32),
            pltpu.SemaphoreType.DMA((3,)),
        ],
        name="basis",
        compiler_params=pltpu.CompilerParams(vmem_limit_bytes=16 << 20),
        cost_estimate=pl.CostEstimate(
            flops=2 * 400 * tenors * cols, bytes_accessed=4 << 20, transcendentals=3 * tenors * cols
        ),
    )(shocks.reshape(tenors * dates, path_dev), forward_start.reshape(1, tenors), loading)

    need = 2 * plan.trades * cols + 8 * plan.trades * plan.step + (8 << 20)
    lines_out = pl.pallas_call(
        functools.partial(main_kernel, plan, path_total),
        out_shape=jax.ShapeDtypeStruct((owners * path_parts, 1, LANES), F32),
        in_specs=[SMEM] * 4 + [VMEM] * (2 + len(incoming)),
        out_specs=VMEM,
        scratch_shapes=[pltpu.VMEM((plan.trades, cols), BF16)],
        name="value_and_allocate",
        compiler_params=pltpu.CompilerParams(vmem_limit_bytes=need),
    )(me, agr_of_ns, cpty_of_agr, margin_lag, default_weight, basis, *incoming)

    lines_in = lax.all_to_all(lines_out, ("trade", "path"), split_axis=0, concat_axis=0, tiled=True)
    lines_in = lines_in.reshape(owners * path_parts, LANES)
    allocation, cva = pl.pallas_call(
        functools.partial(finish_kernel, plan),
        out_shape=[
            jax.ShapeDtypeStruct((1, rows), F32),
            jax.ShapeDtypeStruct((1, default_weight.shape[0]), F32),
        ],
        in_specs=[SMEM] + [VMEM] * 3,
        out_specs=[VMEM, VMEM],
        name="finish",
        compiler_params=pltpu.CompilerParams(vmem_limit_bytes=32 << 20),
    )(me, place, notional, lines_in)
    return (allocation.reshape(rows), cva.reshape(default_weight.shape[0]))


def solution(mesh):
    placed = (
        P(None, None, "path"),
        P(),
        P(),
        P("trade", None),
        P("trade"),
        P(),
        P("trade"),
        P("trade"),
        P("trade"),
        P("trade", None),
    )
    return jax.shard_map(
        body, mesh=mesh, in_specs=placed, out_specs=(P("trade"), P("trade")), check_vma=False
    )
```

```python
import functools

import jax
import jax.numpy as jnp
from jax import lax
from jax.experimental import pallas as pl
from jax.experimental.pallas import tpu as pltpu
from jax.sharding import PartitionSpec as P

NS_DEV = 8
AG_DEV = 4
LAG_MAX = 4
LANES = 128
SUBS = 8

RATE_UNIT = 0.03
STEP = 0.25
SMOOTH = 0.5

F32 = jnp.float32
BF16 = jnp.bfloat16
VMEM = pl.BlockSpec(memory_space=pltpu.VMEM)
SMEM = pl.BlockSpec(memory_space=pltpu.SMEM)
HBM = pl.BlockSpec(memory_space=pltpu.HBM)
BOTH_LANES = (((1,), (1,)), ((), ()))


def iota(shape, dim):
    return lax.broadcasted_iota(jnp.int32, shape, dim)


def mask_bf16(mask):
    return mask.astype(F32).astype(BF16)


def split_bf16(x, parts):
    pieces = []
    for _ in range(parts):
        piece = x.astype(BF16)
        pieces.append(piece)
        x = x - piece.astype(F32)
    return pieces


def fetch(sources, targets, sems):
    copies = [pltpu.make_async_copy(a, b, sems.at[n]) for n, (a, b) in enumerate(zip(sources, targets))]
    for copy in copies:
        copy.start()
    return copies


def in_a_row(x):
    return jnp.concatenate([x[r : r + 1] for r in range(x.shape[0])], axis=1)


class Plan:
    def __init__(self, owners, rows, tenors, dates):
        most = 3 * rows // (2 * owners)
        self.owners = owners
        self.halves = 2 if most % 96 == 0 else 1
        most = most // self.halves
        self.groups = 3 if most % 48 == 0 else 1
        self.part = -(-most // (16 * self.groups)) * 16
        self.room = self.groups * self.part
        self.height = self.room + self.part
        self.extra = 2 * tenors - LANES
        self.per_line = LANES // self.part
        self.lines = owners * self.part // LANES
        self.slots = self.halves * self.room
        self.trades = owners * self.slots
        self.dates = dates
        self.width = 512
        self.step = 2048 if self.trades <= 1024 else 512


def pack_kernel(plan, me_ref, half_ref, sets_hbm, coef_hbm, notional_hbm, place_ref, out_ref, *refs):
    sets_ref, coef_ref, notional_ref, sems = refs
    copies = fetch(
        [sets_hbm, notional_hbm, coef_hbm], [sets_ref, notional_ref, coef_ref], sems
    )
    me = me_ref[0]
    owners, part, room, extra = plan.owners, plan.part, plan.room, plan.extra
    lines = notional_ref.shape[0]
    rows = lines * LANES
    shared = SUBS // lines
    copies[0].wait()
    block = sets_ref[pl.ds(pl.multiple_of(me // shared * SUBS, SUBS), SUBS), :]
    own = block[0:lines]
    for b in range(1, shared):
        own = jnp.where(lax.rem(me, shared) == b, block[b * lines : (b + 1) * lines], own)
    sets = in_a_row(own)
    key = lax.shift_right_logical(sets, 3)
    local = sets - key * NS_DEV
    hot = iota((owners, rows), 0) == key
    before = mask_bf16(iota((rows, rows), 0) < iota((rows, rows), 1))
    count = jnp.dot(mask_bf16(hot), before, preferred_element_type=F32)
    rank = jnp.sum(jnp.where(hot, count, 0.0), axis=0, keepdims=True)
    place_ref[...] = jnp.concatenate(
        [key.astype(F32), rank, jnp.zeros((SUBS - 2, rows), F32)], axis=0
    )
    mine = rank.astype(jnp.int32) - room * half_ref[0]
    spot = jnp.where((mine >= 0) & (mine < room), key * room + mine, -1)
    chosen = mask_bf16(iota((owners * room, rows), 0) == spot)
    copies[1].wait()
    notional = in_a_row(notional_ref[...])
    high = notional.astype(BF16).astype(F32)
    info = jnp.concatenate(
        [high, notional - high, local.astype(F32), jnp.zeros((13, rows), F32)], axis=0
    )
    copies[2].wait()
    table = jnp.concatenate([coef_ref[...], info.astype(BF16)], axis=0)
    moved = lax.dot_general(chosen, table, BOTH_LANES, preferred_element_type=F32)
    ids = LANES + extra
    for d in range(owners):
        message = out_ref.at[d]
        block = moved[d * room : (d + 1) * room]
        message[0:room, :] = block[:, 0:LANES].astype(BF16)
        split = [block[part * g : part * (g + 1)] for g in range(plan.groups)]
        lanes = [x[:, LANES:ids] for x in split]
        if plan.groups < 3:
            lanes.append(jnp.zeros((part, extra * (3 - plan.groups)), F32))
        lanes += [x[:, ids : ids + SUBS] for x in split]
        lanes.append(jnp.zeros((part, SUBS * (4 - plan.groups)), F32))
        message[room:, :] = jnp.concatenate(lanes, axis=1).astype(BF16)


def basis_kernel(plan, shocks_hbm, start_hbm, loading_hbm, out_ref, *refs):
    shocks_ref, start_ref, loading_ref, wide_ref, sems = refs
    copies = fetch(
        [loading_hbm, start_hbm, shocks_hbm], [loading_ref, start_ref, shocks_ref], sems
    )
    tenors = loading_ref.shape[0]
    dates = plan.dates
    copies[0].wait()
    copies[1].wait()
    loading_t = jnp.transpose(loading_ref[...])
    drift = 0.5 * STEP * jnp.sum(loading_t * loading_t, axis=1, keepdims=True)
    diag = iota((tenors, tenors), 0) == iota((tenors, tenors), 1)
    log_start = jnp.log(jnp.sum(jnp.where(diag, start_ref[...], 0.0), axis=1, keepdims=True))
    loads = jnp.concatenate(split_bf16((STEP**0.5) * loading_t, 3), axis=1)
    lower = mask_bf16(iota((tenors, tenors), 1) <= iota((tenors, tenors), 0))
    lower = jnp.concatenate([lower, lower], axis=1)
    log_fwd = jnp.broadcast_to(log_start, (tenors, LANES))
    drift = jnp.broadcast_to(drift, (tenors, LANES))
    head = LANES - tenors
    copies[2].wait()
    wide_ref[...] = shocks_ref[...].astype(F32)
    step = plan.width // LANES
    for c in range(dates // step):
        shock = jnp.concatenate(
            [
                wide_ref[pl.ds(c * step + j, tenors, stride=dates), :].astype(BF16)
                for j in range(step)
            ],
            axis=1,
        )
        change = jnp.dot(
            loads, jnp.concatenate([shock] * 3, axis=0), preferred_element_type=F32
        )
        logs = []
        for j in range(step):
            log_fwd = log_fwd + (change[:, LANES * j : LANES * (j + 1)] - drift)
            logs.append(log_fwd)
        fwd = jnp.exp(jnp.concatenate(logs, axis=1))
        growth = split_bf16(jnp.log(1.0 + STEP * fwd), 2)
        summed = jnp.dot(lower, jnp.concatenate(growth, axis=0), preferred_element_type=F32)
        bond = jnp.exp(-summed)
        cols = slice(c * plan.width, (c + 1) * plan.width)
        out_ref[0:tenors, cols] = (bond * fwd * (1.0 / RATE_UNIT)).astype(BF16)
        bond = bond.astype(BF16)
        out_ref[tenors:LANES, cols] = bond[0:head]
        for g in range(plan.groups):
            out_ref[LANES + plan.extra * g : LANES + plan.extra * (g + 1), cols] = bond[head:]
        used = LANES + plan.extra * plan.groups
        out_ref[used:, cols] = jnp.zeros((2 * LANES - used, plan.width), BF16)


def main_kernel(plan, path_total, me_ref, agr_ref, cpty_ref, lag_ref, weight_ref, basis_ref, *refs):
    *in_refs, out_ref, val_ref = refs
    me = me_ref[0]
    part, room, dates = plan.part, plan.room, plan.dates
    cpty_dev = weight_ref.shape[0]

    lane = iota((1, LANES), 1)
    left, info = [], []
    for in_ref in in_refs:
        rest = in_ref[:, room:, :].reshape(plan.owners * part, LANES)
        for g in range(plan.groups):
            main = in_ref[:, part * g : part * (g + 1), :].reshape(plan.owners * part, LANES)
            keep = mask_bf16((lane >= plan.extra * g) & (lane < plan.extra * (g + 1)))
            left.append(jnp.concatenate([main, rest * keep], axis=1))
            first = 3 * plan.extra + SUBS * g
            pick = mask_bf16(iota((SUBS, LANES), 1) == first + iota((SUBS, LANES), 0))
            info.append(lax.dot_general(pick, rest, BOTH_LANES, preferred_element_type=F32))
    left = jnp.concatenate(left, axis=0)
    info = jnp.concatenate(info, axis=1)
    local = info[2:3].astype(jnp.int32)
    agr = jnp.zeros_like(local)
    for n in range(NS_DEV):
        agr = jnp.where(local == n, agr_ref[n] - me * AG_DEV, agr)
    row = iota((SUBS, plan.trades), 0)
    hot = lax.rem(row, AG_DEV) == agr
    netting = jnp.where(hot, jnp.where(row < AG_DEV, info[0:1], info[1:2]), 0.0).astype(BF16)

    width = plan.step
    for c in range(dates * LANES // width):
        cols = slice(c * width, (c + 1) * width)
        under = jnp.dot(left, basis_ref[:, cols], preferred_element_type=F32)
        val_ref[:, cols] = jnp.maximum(under.astype(BF16), 0)
    both = jnp.dot(netting, val_ref[...], preferred_element_type=F32)
    both = both + pltpu.roll(both, AG_DEV, 0)
    owed = [both[:, LANES * t : LANES * (t + 1)] for t in range(dates)]

    member = lax.rem(iota((SUBS, LANES), 0), AG_DEV)
    lag = jnp.zeros((SUBS, LANES), jnp.int32)
    cpty = jnp.zeros((SUBS, LANES), jnp.int32)
    for a in range(AG_DEV):
        lag = jnp.where(member == a, lag_ref[a], lag)
        cpty = jnp.where(member == a, cpty_ref[a] - me * cpty_dev, cpty)
    lags = [lag == s for s in range(1, LAG_MAX + 1)]
    weight = jnp.zeros((SUBS, dates), F32)
    for c in range(cpty_dev):
        weight = jnp.where(cpty[:, 0:dates] == c, weight_ref[c : c + 1, :], weight)
    zero = jnp.zeros((SUBS, LANES), F32)
    spent, slopes = zero, []
    for t in range(dates):
        before = zero
        for s in range(1, min(t, LAG_MAX) + 1):
            before = jnp.where(lags[s - 1], owed[t - s], before)
        excess = owed[t] - before
        square = excess * excess + SMOOTH * SMOOTH
        inverse = lax.rsqrt(square)
        due = weight[:, t : t + 1]
        spent = spent + due * (0.5 * (excess + square * inverse))
        slopes.append(due * (0.5 * (1.0 + excess * inverse)))
    grads = []
    for t in range(dates):
        after = zero
        for s in range(1, min(dates - 1 - t, LAG_MAX) + 1):
            after = jnp.where(lags[s - 1], slopes[t + s], after)
        grads.append(((slopes[t] - after) * (1.0 / path_total)).astype(BF16))

    dots = lax.dot_general(
        jnp.concatenate(grads, axis=1), val_ref[...], BOTH_LANES, preferred_element_type=F32
    )
    share = jnp.sum(jnp.where(hot & (row < AG_DEV), dots, 0.0), axis=0, keepdims=True)
    spent = jnp.sum(spent, axis=1, keepdims=True) * (1.0 / path_total)
    mine = (lane - plan.slots == cpty) & (iota((SUBS, LANES), 0) < AG_DEV)
    cva = jnp.sum(jnp.where(mine, spent, 0.0), axis=0, keepdims=True)
    block = lane // part
    parts = plan.slots // part
    count = parts * plan.lines
    lines = jnp.concatenate([share[:, LANES * k : LANES * (k + 1)] for k in range(count)], axis=0)
    moved = [lines if m == 0 else pltpu.roll(lines, part * m, 1) for m in range(plan.per_line)]
    paths = out_ref.shape[0] // plan.owners
    for k in range(plan.lines):
        for s in range(plan.per_line):
            line = cva
            for g in range(parts):
                n = g * plan.lines + k
                line = jnp.where(block == g, moved[(g - s) % plan.per_line][n : n + 1], line)
            for p in range(paths):
                out_ref[(k * plan.per_line + s) * paths + p] = line


def finish_kernel(plan, me_ref, place_ref, notional_ref, in_ref, alloc_ref, cva_ref):
    me = me_ref[0]
    rows = place_ref.shape[1]
    key = place_ref[0:1, :].astype(jnp.int32)
    rank = place_ref[1:2, :].astype(jnp.int32)
    lines = in_ref[...]
    count = lines.shape[0]
    paths = count // plan.owners
    pieces = jnp.concatenate(split_bf16(lines, 3), axis=0)
    half = lax.rem(lax.rem(iota((pieces.shape[0], rows), 0), paths), plan.halves)
    found = jnp.zeros(half.shape, F32)
    for h in range(plan.halves):
        slot = lax.rem(rank + plan.room * h, plan.slots)
        hot = mask_bf16(iota((LANES, rows), 0) == slot)
        found = jnp.where(half == h, jnp.dot(pieces, hot, preferred_element_type=F32), found)
    wanted = lax.rem(iota(found.shape, 0), count) // paths == key
    share = jnp.sum(jnp.where(wanted, found, 0.0), axis=0, keepdims=True)
    alloc_ref[...] = share * in_a_row(notional_ref[...])
    own = iota(lines.shape, 0) // paths == me
    cva = jnp.sum(jnp.where(own, lines, 0.0), axis=0, keepdims=True)
    cva_ref[...] = cva[:, plan.slots : plan.slots + cva_ref.shape[1]]


def body(
    shocks,
    forward_start,
    loading,
    coefficient,
    notional,
    ns_of_trade,
    agr_of_ns,
    cpty_of_agr,
    margin_lag,
    default_weight,
):
    owners = lax.axis_size("trade")
    path_parts = lax.axis_size("path")
    tenors, dates, path_dev = shocks.shape
    path_total = float(path_dev * path_parts)
    rows = coefficient.shape[0]
    lines = rows // LANES
    plan = Plan(owners, rows, tenors, dates)
    cols = dates * path_dev
    me = lax.axis_index("trade").astype(jnp.int32).reshape(1)
    half = lax.rem(lax.axis_index("path").astype(jnp.int32), plan.halves).reshape(1)
    notional = notional.reshape(lines, LANES)

    place, outgoing = pl.pallas_call(
        functools.partial(pack_kernel, plan),
        out_shape=[
            jax.ShapeDtypeStruct((SUBS, rows), F32),
            jax.ShapeDtypeStruct((owners, plan.height, LANES), BF16),
        ],
        in_specs=[SMEM] * 2 + [HBM] * 3,
        out_specs=[VMEM, VMEM],
        scratch_shapes=[
            pltpu.VMEM((owners * lines, LANES), jnp.int32),
            pltpu.VMEM((2 * tenors, rows), BF16),
            pltpu.VMEM((lines, LANES), F32),
            pltpu.SemaphoreType.DMA((3,)),
        ],
        name="pack",
        cost_estimate=pl.CostEstimate(flops=1 << 32, bytes_accessed=1 << 19, transcendentals=0),
    )(me, half, ns_of_trade.reshape(owners * lines, LANES), coefficient.T, notional)
    incoming = [lax.all_to_all(outgoing, "trade", split_axis=0, concat_axis=0, tiled=True)]
    basis = pl.pallas_call(
        functools.partial(basis_kernel, plan),
        out_shape=jax.ShapeDtypeStruct((2 * LANES, cols), BF16),
        in_specs=[HBM] * 3,
        out_specs=VMEM,
        scratch_shapes=[
            pltpu.VMEM((tenors * dates, path_dev), BF16),
            pltpu.VMEM((1, tenors), F32),
            pltpu.VMEM((tenors, tenors), F32),
            pltpu.VMEM((tenors * dates, path_dev), F32),
            pltpu.SemaphoreType.DMA((3,)),
        ],
        name="basis",
        compiler_params=pltpu.CompilerParams(vmem_limit_bytes=16 << 20),
        cost_estimate=pl.CostEstimate(
            flops=2 * 400 * tenors * cols, bytes_accessed=4 << 20, transcendentals=3 * tenors * cols
        ),
    )(shocks.reshape(tenors * dates, path_dev), forward_start.reshape(1, tenors), loading)

    if plan.halves == 2:
        incoming[0], basis = lax.optimization_barrier((incoming[0], basis))
        pairs = [(p, p ^ 1) for p in range(path_parts)]
        incoming.append(lax.ppermute(incoming[0], "path", pairs))

    need = 2 * plan.trades * cols + 8 * plan.trades * plan.step + (8 << 20)
    lines_out = pl.pallas_call(
        functools.partial(main_kernel, plan, path_total),
        out_shape=jax.ShapeDtypeStruct((owners * path_parts, 1, LANES), F32),
        in_specs=[SMEM] * 4 + [VMEM] * (2 + len(incoming)),
        out_specs=VMEM,
        scratch_shapes=[pltpu.VMEM((plan.trades, cols), BF16)],
        name="value_and_allocate",
        compiler_params=pltpu.CompilerParams(vmem_limit_bytes=need),
    )(me, agr_of_ns, cpty_of_agr, margin_lag, default_weight, basis, *incoming)

    lines_in = lax.all_to_all(lines_out, ("trade", "path"), split_axis=0, concat_axis=0, tiled=True)
    lines_in = lines_in.reshape(owners * path_parts, LANES)
    allocation, cva = pl.pallas_call(
        functools.partial(finish_kernel, plan),
        out_shape=[
            jax.ShapeDtypeStruct((1, rows), F32),
            jax.ShapeDtypeStruct((1, default_weight.shape[0]), F32),
        ],
        in_specs=[SMEM] + [VMEM] * 3,
        out_specs=[VMEM, VMEM],
        name="finish",
        compiler_params=pltpu.CompilerParams(vmem_limit_bytes=32 << 20),
    )(me, place, notional, lines_in)
    return (allocation.reshape(rows), cva.reshape(default_weight.shape[0]))


def solution(mesh):
    placed = (
        P(None, None, "path"),
        P(),
        P(),
        P("trade", None),
        P("trade"),
        P(),
        P("trade"),
        P("trade"),
        P("trade"),
        P("trade", None),
    )
    return jax.shard_map(
        body, mesh=mesh, in_specs=placed, out_specs=(P("trade"), P("trade")), check_vma=False
    )
```

```python
import functools

import jax
import jax.numpy as jnp
from jax import lax
from jax.experimental import pallas as pl
from jax.experimental.pallas import tpu as pltpu
from jax.sharding import PartitionSpec as P

NS_DEV = 8
AG_DEV = 4
LAG_MAX = 4
LANES = 128
SUBS = 8

RATE_UNIT = 0.03
STEP = 0.25
SMOOTH = 0.5

F32 = jnp.float32
BF16 = jnp.bfloat16
VMEM = pl.BlockSpec(memory_space=pltpu.VMEM)
SMEM = pl.BlockSpec(memory_space=pltpu.SMEM)
HBM = pl.BlockSpec(memory_space=pltpu.HBM)
BOTH_LANES = (((1,), (1,)), ((), ()))


def iota(shape, dim):
    return lax.broadcasted_iota(jnp.int32, shape, dim)


def mask_bf16(mask):
    return mask.astype(F32).astype(BF16)


def split_bf16(x, parts):
    pieces = []
    for _ in range(parts):
        piece = x.astype(BF16)
        pieces.append(piece)
        x = x - piece.astype(F32)
    return pieces


def fetch(sources, targets, sems):
    copies = [pltpu.make_async_copy(a, b, sems.at[n]) for n, (a, b) in enumerate(zip(sources, targets))]
    for copy in copies:
        copy.start()
    return copies


def in_a_row(x):
    return jnp.concatenate([x[r : r + 1] for r in range(x.shape[0])], axis=1)


class Plan:
    def __init__(self, owners, rows, tenors, dates):
        most = 3 * rows // (2 * owners)
        self.owners = owners
        self.halves = 2 if most % 96 == 0 else 1
        most = most // self.halves
        self.groups = 3 if most % 48 == 0 else 1
        self.part = -(-most // (16 * self.groups)) * 16
        self.room = self.groups * self.part
        self.height = self.room + self.part
        self.extra = 2 * tenors - LANES
        self.per_line = LANES // self.part
        self.lines = owners * self.part // LANES
        self.slots = self.halves * self.room
        self.trades = owners * self.slots
        self.dates = dates
        self.width = 512
        self.step = 2048 if self.trades <= 1024 else 512


def pack_kernel(plan, me_ref, half_ref, sets_hbm, coef_hbm, notional_hbm, place_ref, out_ref, *refs):
    sets_ref, coef_ref, notional_ref, sems = refs
    copies = fetch(
        [sets_hbm, notional_hbm, coef_hbm], [sets_ref, notional_ref, coef_ref], sems
    )
    me = me_ref[0]
    owners, part, room, extra = plan.owners, plan.part, plan.room, plan.extra
    lines = notional_ref.shape[0]
    rows = lines * LANES
    shared = SUBS // lines
    copies[0].wait()
    block = sets_ref[pl.ds(pl.multiple_of(me // shared * SUBS, SUBS), SUBS), :]
    own = block[0:lines]
    for b in range(1, shared):
        own = jnp.where(lax.rem(me, shared) == b, block[b * lines : (b + 1) * lines], own)
    sets = in_a_row(own)
    key = lax.shift_right_logical(sets, 3)
    local = sets - key * NS_DEV
    hot = iota((owners, rows), 0) == key
    before = mask_bf16(iota((rows, rows), 0) < iota((rows, rows), 1))
    count = jnp.dot(mask_bf16(hot), before, preferred_element_type=F32)
    rank = jnp.sum(jnp.where(hot, count, 0.0), axis=0, keepdims=True)
    place_ref[...] = jnp.concatenate(
        [key.astype(F32), rank, jnp.zeros((SUBS - 2, rows), F32)], axis=0
    )
    mine = rank.astype(jnp.int32) - room * half_ref[0]
    spot = jnp.where((mine >= 0) & (mine < room), key * room + mine, -1)
    chosen = mask_bf16(iota((owners * room, rows), 0) == spot)
    copies[1].wait()
    notional = in_a_row(notional_ref[...])
    high = notional.astype(BF16).astype(F32)
    info = jnp.concatenate(
        [high, notional - high, local.astype(F32), jnp.zeros((13, rows), F32)], axis=0
    )
    copies[2].wait()
    table = jnp.concatenate([coef_ref[...], info.astype(BF16)], axis=0)
    moved = lax.dot_general(chosen, table, BOTH_LANES, preferred_element_type=F32)
    ids = LANES + extra
    for d in range(owners):
        message = out_ref.at[d]
        block = moved[d * room : (d + 1) * room]
        message[0:room, :] = block[:, 0:LANES].astype(BF16)
        split = [block[part * g : part * (g + 1)] for g in range(plan.groups)]
        lanes = [x[:, LANES:ids] for x in split]
        if plan.groups < 3:
            lanes.append(jnp.zeros((part, extra * (3 - plan.groups)), F32))
        lanes += [x[:, ids : ids + SUBS] for x in split]
        lanes.append(jnp.zeros((part, SUBS * (4 - plan.groups)), F32))
        message[room:, :] = jnp.concatenate(lanes, axis=1).astype(BF16)


def basis_kernel(plan, shocks_hbm, start_hbm, loading_hbm, out_ref, *refs):
    shocks_ref, start_ref, loading_ref, wide_ref, sems = refs
    copies = fetch(
        [loading_hbm, start_hbm, shocks_hbm], [loading_ref, start_ref, shocks_ref], sems
    )
    tenors = loading_ref.shape[0]
    dates = plan.dates
    copies[0].wait()
    copies[1].wait()
    loading_t = jnp.transpose(loading_ref[...])
    drift = 0.5 * STEP * jnp.sum(loading_t * loading_t, axis=1, keepdims=True)
    diag = iota((tenors, tenors), 0) == iota((tenors, tenors), 1)
    log_start = jnp.log(jnp.sum(jnp.where(diag, start_ref[...], 0.0), axis=1, keepdims=True))
    loads = jnp.concatenate(split_bf16((STEP**0.5) * loading_t, 3), axis=1)
    lower = mask_bf16(iota((tenors, tenors), 1) <= iota((tenors, tenors), 0))
    lower = jnp.concatenate([lower, lower], axis=1)
    log_fwd = jnp.broadcast_to(log_start, (tenors, LANES))
    drift = jnp.broadcast_to(drift, (tenors, LANES))
    head = LANES - tenors
    copies[2].wait()
    wide_ref[...] = shocks_ref[...].astype(F32)
    step = plan.width // LANES
    for c in range(dates // step):
        shock = jnp.concatenate(
            [
                wide_ref[pl.ds(c * step + j, tenors, stride=dates), :].astype(BF16)
                for j in range(step)
            ],
            axis=1,
        )
        change = jnp.dot(
            loads, jnp.concatenate([shock] * 3, axis=0), preferred_element_type=F32
        )
        logs = []
        for j in range(step):
            log_fwd = log_fwd + (change[:, LANES * j : LANES * (j + 1)] - drift)
            logs.append(log_fwd)
        fwd = jnp.exp(jnp.concatenate(logs, axis=1))
        growth = split_bf16(jnp.log(1.0 + STEP * fwd), 2)
        summed = jnp.dot(lower, jnp.concatenate(growth, axis=0), preferred_element_type=F32)
        bond = jnp.exp(-summed)
        cols = slice(c * plan.width, (c + 1) * plan.width)
        out_ref[0:tenors, cols] = (bond * fwd * (1.0 / RATE_UNIT)).astype(BF16)
        bond = bond.astype(BF16)
        out_ref[tenors:LANES, cols] = bond[0:head]
        for g in range(plan.groups):
            out_ref[LANES + plan.extra * g : LANES + plan.extra * (g + 1), cols] = bond[head:]
        used = LANES + plan.extra * plan.groups
        out_ref[used:, cols] = jnp.zeros((2 * LANES - used, plan.width), BF16)


def left_side(plan, in_ref):
    part, extra = plan.part, plan.extra
    rest = in_ref[:, plan.room :, :].reshape(plan.owners * part, LANES)
    lane = iota((1, LANES), 1)
    left = []
    for g in range(plan.groups):
        main = in_ref[:, part * g : part * (g + 1), :].reshape(plan.owners * part, LANES)
        keep = mask_bf16((lane >= extra * g) & (lane < extra * (g + 1)))
        left.append(jnp.concatenate([main, rest * keep], axis=1))
    return jnp.concatenate(left, axis=0), rest


def price(plan, left, basis_ref, val_ref):
    width = plan.step
    for c in range(basis_ref.shape[1] // width):
        cols = slice(c * width, (c + 1) * width)
        under = jnp.dot(left, basis_ref[:, cols], preferred_element_type=F32)
        val_ref[:, cols] = jnp.maximum(under.astype(BF16), 0)


def price_kernel(plan, basis_ref, in_ref, val_ref):
    price(plan, left_side(plan, in_ref)[0], basis_ref, val_ref)


def main_kernel(plan, path_total, me_ref, agr_ref, cpty_ref, lag_ref, weight_ref, basis_ref, *refs):
    *in_refs, out_ref, val_ref = refs
    val_refs = [val_ref]
    if plan.halves == 2:
        val_refs = [in_refs.pop(), val_ref]
    me = me_ref[0]
    part, room, dates = plan.part, plan.room, plan.dates
    cpty_dev = weight_ref.shape[0]

    lane = iota((1, LANES), 1)
    info = []
    for in_ref in in_refs:
        left, rest = left_side(plan, in_ref)
        for g in range(plan.groups):
            first = 3 * plan.extra + SUBS * g
            pick = mask_bf16(iota((SUBS, LANES), 1) == first + iota((SUBS, LANES), 0))
            info.append(lax.dot_general(pick, rest, BOTH_LANES, preferred_element_type=F32))
    info = jnp.concatenate(info, axis=1)
    local = info[2:3].astype(jnp.int32)
    agr = jnp.zeros_like(local)
    for n in range(NS_DEV):
        agr = jnp.where(local == n, agr_ref[n] - me * AG_DEV, agr)
    row = iota((SUBS, plan.trades), 0)
    hot = lax.rem(row, AG_DEV) == agr
    netting = jnp.where(hot, jnp.where(row < AG_DEV, info[0:1], info[1:2]), 0.0).astype(BF16)

    price(plan, left, basis_ref, val_ref)
    size = val_ref.shape[0]
    both = jnp.zeros((SUBS, val_ref.shape[1]), F32)
    for h, values in enumerate(val_refs):
        both = both + jnp.dot(
            netting[:, size * h : size * (h + 1)], values[...], preferred_element_type=F32
        )
    both = both + pltpu.roll(both, AG_DEV, 0)
    owed = [both[:, LANES * t : LANES * (t + 1)] for t in range(dates)]

    member = lax.rem(iota((SUBS, LANES), 0), AG_DEV)
    lag = jnp.zeros((SUBS, LANES), jnp.int32)
    cpty = jnp.zeros((SUBS, LANES), jnp.int32)
    for a in range(AG_DEV):
        lag = jnp.where(member == a, lag_ref[a], lag)
        cpty = jnp.where(member == a, cpty_ref[a] - me * cpty_dev, cpty)
    lags = [lag == s for s in range(1, LAG_MAX + 1)]
    weight = jnp.zeros((SUBS, dates), F32)
    for c in range(cpty_dev):
        weight = jnp.where(cpty[:, 0:dates] == c, weight_ref[c : c + 1, :], weight)
    zero = jnp.zeros((SUBS, LANES), F32)
    spent, slopes = zero, []
    for t in range(dates):
        before = zero
        for s in range(1, min(t, LAG_MAX) + 1):
            before = jnp.where(lags[s - 1], owed[t - s], before)
        excess = owed[t] - before
        square = excess * excess + SMOOTH * SMOOTH
        inverse = lax.rsqrt(square)
        due = weight[:, t : t + 1]
        spent = spent + due * (0.5 * (excess + square * inverse))
        slopes.append(due * (0.5 * (1.0 + excess * inverse)))
    grads = []
    for t in range(dates):
        after = zero
        for s in range(1, min(dates - 1 - t, LAG_MAX) + 1):
            after = jnp.where(lags[s - 1], slopes[t + s], after)
        grads.append(((slopes[t] - after) * (1.0 / path_total)).astype(BF16))

    grads = jnp.concatenate(grads, axis=1)
    dots = [
        lax.dot_general(grads, values[...], BOTH_LANES, preferred_element_type=F32)
        for values in val_refs
    ]
    dots = jnp.concatenate(dots, axis=1)
    share = jnp.sum(jnp.where(hot & (row < AG_DEV), dots, 0.0), axis=0, keepdims=True)
    spent = jnp.sum(spent, axis=1, keepdims=True) * (1.0 / path_total)
    mine = (lane - plan.slots == cpty) & (iota((SUBS, LANES), 0) < AG_DEV)
    cva = jnp.sum(jnp.where(mine, spent, 0.0), axis=0, keepdims=True)
    block = lane // part
    parts = plan.slots // part
    count = parts * plan.lines
    lines = jnp.concatenate([share[:, LANES * k : LANES * (k + 1)] for k in range(count)], axis=0)
    moved = [lines if m == 0 else pltpu.roll(lines, part * m, 1) for m in range(plan.per_line)]
    paths = out_ref.shape[0] // plan.owners
    for k in range(plan.lines):
        for s in range(plan.per_line):
            line = cva
            for g in range(parts):
                n = g * plan.lines + k
                line = jnp.where(block == g, moved[(g - s) % plan.per_line][n : n + 1], line)
            for p in range(paths):
                out_ref[(k * plan.per_line + s) * paths + p] = line


def finish_kernel(plan, me_ref, place_ref, notional_ref, in_ref, alloc_ref, cva_ref):
    me = me_ref[0]
    rows = place_ref.shape[1]
    key = place_ref[0:1, :].astype(jnp.int32)
    rank = place_ref[1:2, :].astype(jnp.int32)
    lines = in_ref[...]
    count = lines.shape[0]
    paths = count // plan.owners
    pieces = jnp.concatenate(split_bf16(lines, 3), axis=0)
    half = lax.rem(lax.rem(iota((pieces.shape[0], rows), 0), paths), plan.halves)
    found = jnp.zeros(half.shape, F32)
    for h in range(plan.halves):
        slot = lax.rem(rank + plan.room * h, plan.slots)
        hot = mask_bf16(iota((LANES, rows), 0) == slot)
        found = jnp.where(half == h, jnp.dot(pieces, hot, preferred_element_type=F32), found)
    wanted = lax.rem(iota(found.shape, 0), count) // paths == key
    share = jnp.sum(jnp.where(wanted, found, 0.0), axis=0, keepdims=True)
    alloc_ref[...] = share * in_a_row(notional_ref[...])
    own = iota(lines.shape, 0) // paths == me
    cva = jnp.sum(jnp.where(own, lines, 0.0), axis=0, keepdims=True)
    cva_ref[...] = cva[:, plan.slots : plan.slots + cva_ref.shape[1]]


def body(
    shocks,
    forward_start,
    loading,
    coefficient,
    notional,
    ns_of_trade,
    agr_of_ns,
    cpty_of_agr,
    margin_lag,
    default_weight,
):
    owners = lax.axis_size("trade")
    path_parts = lax.axis_size("path")
    tenors, dates, path_dev = shocks.shape
    path_total = float(path_dev * path_parts)
    rows = coefficient.shape[0]
    lines = rows // LANES
    plan = Plan(owners, rows, tenors, dates)
    cols = dates * path_dev
    me = lax.axis_index("trade").astype(jnp.int32).reshape(1)
    half = lax.rem(lax.axis_index("path").astype(jnp.int32), plan.halves).reshape(1)
    notional = notional.reshape(lines, LANES)

    place, outgoing = pl.pallas_call(
        functools.partial(pack_kernel, plan),
        out_shape=[
            jax.ShapeDtypeStruct((SUBS, rows), F32),
            jax.ShapeDtypeStruct((owners, plan.height, LANES), BF16),
        ],
        in_specs=[SMEM] * 2 + [HBM] * 3,
        out_specs=[VMEM, VMEM],
        scratch_shapes=[
            pltpu.VMEM((owners * lines, LANES), jnp.int32),
            pltpu.VMEM((2 * tenors, rows), BF16),
            pltpu.VMEM((lines, LANES), F32),
            pltpu.SemaphoreType.DMA((3,)),
        ],
        name="pack",
        cost_estimate=pl.CostEstimate(flops=1 << 32, bytes_accessed=1 << 19, transcendentals=0),
    )(me, half, ns_of_trade.reshape(owners * lines, LANES), coefficient.T, notional)
    incoming = [lax.all_to_all(outgoing, "trade", split_axis=0, concat_axis=0, tiled=True)]
    basis = pl.pallas_call(
        functools.partial(basis_kernel, plan),
        out_shape=jax.ShapeDtypeStruct((2 * LANES, cols), BF16),
        in_specs=[HBM] * 3,
        out_specs=VMEM,
        scratch_shapes=[
            pltpu.VMEM((tenors * dates, path_dev), BF16),
            pltpu.VMEM((1, tenors), F32),
            pltpu.VMEM((tenors, tenors), F32),
            pltpu.VMEM((tenors * dates, path_dev), F32),
            pltpu.SemaphoreType.DMA((3,)),
        ],
        name="basis",
        compiler_params=pltpu.CompilerParams(vmem_limit_bytes=16 << 20),
        cost_estimate=pl.CostEstimate(
            flops=2 * 400 * tenors * cols, bytes_accessed=4 << 20, transcendentals=3 * tenors * cols
        ),
    )(shocks.reshape(tenors * dates, path_dev), forward_start.reshape(1, tenors), loading)

    half_trades = plan.trades // plan.halves
    if plan.halves == 2:
        incoming[0], basis = lax.optimization_barrier((incoming[0], basis))
        pairs = [(p, p ^ 1) for p in range(path_parts)]
        incoming.append(lax.ppermute(incoming[0], "path", pairs))
        incoming.append(
            pl.pallas_call(
                functools.partial(price_kernel, plan),
                out_shape=jax.ShapeDtypeStruct((half_trades, cols), BF16),
                in_specs=[VMEM] * 2,
                out_specs=VMEM,
                name="price_own_half",
                compiler_params=pltpu.CompilerParams(vmem_limit_bytes=24 << 20),
                cost_estimate=pl.CostEstimate(
                    flops=4 * half_trades * LANES * cols, bytes_accessed=6 << 20, transcendentals=0
                ),
            )(basis, incoming[0])
        )

    need = 2 * plan.trades * cols + 8 * plan.trades * plan.step + (8 << 20)
    lines_out = pl.pallas_call(
        functools.partial(main_kernel, plan, path_total),
        out_shape=jax.ShapeDtypeStruct((owners * path_parts, 1, LANES), F32),
        in_specs=[SMEM] * 4 + [VMEM] * (2 + len(incoming)),
        out_specs=VMEM,
        scratch_shapes=[pltpu.VMEM((half_trades, cols), BF16)],
        name="value_and_allocate",
        compiler_params=pltpu.CompilerParams(vmem_limit_bytes=need),
    )(me, agr_of_ns, cpty_of_agr, margin_lag, default_weight, basis, *incoming)

    lines_in = lax.all_to_all(lines_out, ("trade", "path"), split_axis=0, concat_axis=0, tiled=True)
    lines_in = lines_in.reshape(owners * path_parts, LANES)
    allocation, cva = pl.pallas_call(
        functools.partial(finish_kernel, plan),
        out_shape=[
            jax.ShapeDtypeStruct((1, rows), F32),
            jax.ShapeDtypeStruct((1, default_weight.shape[0]), F32),
        ],
        in_specs=[SMEM] + [VMEM] * 3,
        out_specs=[VMEM, VMEM],
        name="finish",
        compiler_params=pltpu.CompilerParams(vmem_limit_bytes=32 << 20),
    )(me, place, notional, lines_in)
    return (allocation.reshape(rows), cva.reshape(default_weight.shape[0]))


def solution(mesh):
    placed = (
        P(None, None, "path"),
        P(),
        P(),
        P("trade", None),
        P("trade"),
        P(),
        P("trade"),
        P("trade"),
        P("trade"),
        P("trade", None),
    )
    return jax.shard_map(
        body, mesh=mesh, in_specs=placed, out_specs=(P("trade"), P("trade")), check_vma=False
    )
```

```python
import functools

import jax
import jax.numpy as jnp
from jax import lax
from jax.experimental import pallas as pl
from jax.experimental.pallas import tpu as pltpu
from jax.sharding import PartitionSpec as P

NS_DEV = 8
AG_DEV = 4
LAG_MAX = 4
LANES = 128
SUBS = 8

RATE_UNIT = 0.03
STEP = 0.25
SMOOTH = 0.5

F32 = jnp.float32
BF16 = jnp.bfloat16
VMEM = pl.BlockSpec(memory_space=pltpu.VMEM)
SMEM = pl.BlockSpec(memory_space=pltpu.SMEM)
HBM = pl.BlockSpec(memory_space=pltpu.HBM)
BOTH_LANES = (((1,), (1,)), ((), ()))


def iota(shape, dim):
    return lax.broadcasted_iota(jnp.int32, shape, dim)


def mask_bf16(mask):
    return mask.astype(F32).astype(BF16)


def split_bf16(x, parts):
    pieces = []
    for _ in range(parts):
        piece = x.astype(BF16)
        pieces.append(piece)
        x = x - piece.astype(F32)
    return pieces


def fetch(sources, targets, sems):
    copies = [pltpu.make_async_copy(a, b, sems.at[n]) for n, (a, b) in enumerate(zip(sources, targets))]
    for copy in copies:
        copy.start()
    return copies


def in_a_row(x):
    return jnp.concatenate([x[r : r + 1] for r in range(x.shape[0])], axis=1)


class Plan:
    def __init__(self, owners, rows, tenors, dates):
        most = 3 * rows // (2 * owners)
        self.owners = owners
        self.halves = 2 if most % 96 == 0 else 1
        most = most // self.halves
        self.groups = 3 if most % 48 == 0 else 1
        self.part = -(-most // (16 * self.groups)) * 16
        self.room = self.groups * self.part
        self.height = self.room + self.part
        self.extra = 2 * tenors - LANES
        self.per_line = LANES // self.part
        self.lines = owners * self.part // LANES
        self.slots = self.halves * self.room
        self.trades = owners * self.slots
        self.dates = dates
        self.width = 512
        self.step = 2048 if self.trades <= 1024 else 512


def pack_kernel(plan, me_ref, half_ref, sets_hbm, coef_hbm, notional_hbm, place_ref, out_ref, *refs):
    sets_ref, coef_ref, notional_ref, sems = refs
    copies = fetch(
        [sets_hbm, notional_hbm, coef_hbm], [sets_ref, notional_ref, coef_ref], sems
    )
    me = me_ref[0]
    owners, part, room, extra = plan.owners, plan.part, plan.room, plan.extra
    lines = notional_ref.shape[0]
    rows = lines * LANES
    shared = SUBS // lines
    copies[0].wait()
    block = sets_ref[pl.ds(pl.multiple_of(me // shared * SUBS, SUBS), SUBS), :]
    own = block[0:lines]
    for b in range(1, shared):
        own = jnp.where(lax.rem(me, shared) == b, block[b * lines : (b + 1) * lines], own)
    sets = in_a_row(own)
    key = lax.shift_right_logical(sets, 3)
    local = sets - key * NS_DEV
    hot = iota((owners, rows), 0) == key
    before = mask_bf16(iota((rows, rows), 0) < iota((rows, rows), 1))
    count = jnp.dot(mask_bf16(hot), before, preferred_element_type=F32)
    rank = jnp.sum(jnp.where(hot, count, 0.0), axis=0, keepdims=True)
    place_ref[...] = jnp.concatenate(
        [key.astype(F32), rank, jnp.zeros((SUBS - 2, rows), F32)], axis=0
    )
    mine = rank.astype(jnp.int32) - room * half_ref[0]
    spot = jnp.where((mine >= 0) & (mine < room), key * room + mine, -1)
    chosen = mask_bf16(iota((owners * room, rows), 0) == spot)
    copies[1].wait()
    notional = in_a_row(notional_ref[...])
    high = notional.astype(BF16).astype(F32)
    info = jnp.concatenate(
        [high, notional - high, local.astype(F32), jnp.zeros((13, rows), F32)], axis=0
    )
    copies[2].wait()
    table = jnp.concatenate([coef_ref[...], info.astype(BF16)], axis=0)
    moved = lax.dot_general(chosen, table, BOTH_LANES, preferred_element_type=F32)
    ids = LANES + extra
    for d in range(owners):
        message = out_ref.at[d]
        block = moved[d * room : (d + 1) * room]
        message[0:room, :] = block[:, 0:LANES].astype(BF16)
        split = [block[part * g : part * (g + 1)] for g in range(plan.groups)]
        lanes = [x[:, LANES:ids] for x in split]
        if plan.groups < 3:
            lanes.append(jnp.zeros((part, extra * (3 - plan.groups)), F32))
        lanes += [x[:, ids : ids + SUBS] for x in split]
        lanes.append(jnp.zeros((part, SUBS * (4 - plan.groups)), F32))
        message[room:, :] = jnp.concatenate(lanes, axis=1).astype(BF16)


def basis_kernel(plan, shocks_hbm, start_hbm, loading_hbm, out_ref, *refs):
    shocks_ref, start_ref, loading_ref, wide_ref, sems = refs
    copies = fetch(
        [loading_hbm, start_hbm, shocks_hbm], [loading_ref, start_ref, shocks_ref], sems
    )
    tenors = loading_ref.shape[0]
    dates = plan.dates
    copies[0].wait()
    copies[1].wait()
    loading_t = jnp.transpose(loading_ref[...])
    drift = 0.5 * STEP * jnp.sum(loading_t * loading_t, axis=1, keepdims=True)
    diag = iota((tenors, tenors), 0) == iota((tenors, tenors), 1)
    log_start = jnp.log(jnp.sum(jnp.where(diag, start_ref[...], 0.0), axis=1, keepdims=True))
    loads = jnp.concatenate(split_bf16((STEP**0.5) * loading_t, 3), axis=1)
    lower = mask_bf16(iota((tenors, tenors), 1) <= iota((tenors, tenors), 0))
    lower = jnp.concatenate([lower, lower], axis=1)
    log_fwd = jnp.broadcast_to(log_start, (tenors, LANES))
    drift = jnp.broadcast_to(drift, (tenors, LANES))
    head = LANES - tenors
    copies[2].wait()
    wide_ref[...] = shocks_ref[...].astype(F32)
    step = plan.width // LANES
    for c in range(dates // step):
        shock = jnp.concatenate(
            [
                wide_ref[pl.ds(c * step + j, tenors, stride=dates), :].astype(BF16)
                for j in range(step)
            ],
            axis=1,
        )
        change = jnp.dot(
            loads, jnp.concatenate([shock] * 3, axis=0), preferred_element_type=F32
        )
        logs = []
        for j in range(step):
            log_fwd = log_fwd + (change[:, LANES * j : LANES * (j + 1)] - drift)
            logs.append(log_fwd)
        fwd = jnp.exp(jnp.concatenate(logs, axis=1))
        growth = split_bf16(jnp.log(1.0 + STEP * fwd), 2)
        summed = jnp.dot(lower, jnp.concatenate(growth, axis=0), preferred_element_type=F32)
        bond = jnp.exp(-summed)
        cols = slice(c * plan.width, (c + 1) * plan.width)
        out_ref[0:tenors, cols] = (bond * fwd * (1.0 / RATE_UNIT)).astype(BF16)
        bond = bond.astype(BF16)
        out_ref[tenors:LANES, cols] = bond[0:head]
        for g in range(plan.groups):
            out_ref[LANES + plan.extra * g : LANES + plan.extra * (g + 1), cols] = bond[head:]
        used = LANES + plan.extra * plan.groups
        out_ref[used:, cols] = jnp.zeros((2 * LANES - used, plan.width), BF16)


def left_side(plan, in_ref):
    part, extra = plan.part, plan.extra
    rest = in_ref[:, plan.room :, :].reshape(plan.owners * part, LANES)
    lane = iota((1, LANES), 1)
    left = []
    for g in range(plan.groups):
        main = in_ref[:, part * g : part * (g + 1), :].reshape(plan.owners * part, LANES)
        keep = mask_bf16((lane >= extra * g) & (lane < extra * (g + 1)))
        left.append(jnp.concatenate([main, rest * keep], axis=1))
    return jnp.concatenate(left, axis=0), rest


def price(plan, left, basis_ref, val_ref):
    width = plan.step
    for c in range(basis_ref.shape[1] // width):
        cols = slice(c * width, (c + 1) * width)
        under = jnp.dot(left, basis_ref[:, cols], preferred_element_type=F32)
        val_ref[:, cols] = jnp.maximum(under.astype(BF16), 0)


def price_kernel(plan, basis_ref, in_ref, val_ref):
    price(plan, left_side(plan, in_ref)[0], basis_ref, val_ref)


def main_kernel(plan, path_total, me_ref, agr_ref, cpty_ref, lag_ref, weight_ref, basis_ref, *refs):
    *in_refs, out_ref, val_ref = refs
    val_refs = [val_ref]
    if plan.halves == 2:
        val_refs = [in_refs.pop(), val_ref]
    me = me_ref[0]
    part, room, dates = plan.part, plan.room, plan.dates
    cpty_dev = weight_ref.shape[0]

    lane = iota((1, LANES), 1)
    info = []
    for in_ref in in_refs:
        left, rest = left_side(plan, in_ref)
        for g in range(plan.groups):
            first = 3 * plan.extra + SUBS * g
            pick = mask_bf16(iota((SUBS, LANES), 1) == first + iota((SUBS, LANES), 0))
            info.append(lax.dot_general(pick, rest, BOTH_LANES, preferred_element_type=F32))
    info = jnp.concatenate(info, axis=1)
    local = info[2:3].astype(jnp.int32)
    agr = jnp.zeros_like(local)
    for n in range(NS_DEV):
        agr = jnp.where(local == n, agr_ref[n] - me * AG_DEV, agr)
    row = iota((SUBS, plan.trades), 0)
    hot = lax.rem(row, AG_DEV) == agr
    netting = jnp.where(hot, jnp.where(row < AG_DEV, info[0:1], info[1:2]), 0.0).astype(BF16)

    price(plan, left, basis_ref, val_ref)
    size = val_ref.shape[0]
    both = jnp.zeros((SUBS, val_ref.shape[1]), F32)
    for h, values in enumerate(val_refs):
        both = both + jnp.dot(
            netting[:, size * h : size * (h + 1)], values[...], preferred_element_type=F32
        )
    both = both + pltpu.roll(both, AG_DEV, 0)
    owed = [both[:, LANES * t : LANES * (t + 1)] for t in range(dates)]

    member = lax.rem(iota((SUBS, LANES), 0), AG_DEV)
    lag = jnp.zeros((SUBS, LANES), jnp.int32)
    cpty = jnp.zeros((SUBS, LANES), jnp.int32)
    for a in range(AG_DEV):
        lag = jnp.where(member == a, lag_ref[a], lag)
        cpty = jnp.where(member == a, cpty_ref[a] - me * cpty_dev, cpty)
    lags = [lag == s for s in range(1, LAG_MAX + 1)]
    weight = jnp.zeros((SUBS, dates), F32)
    for c in range(cpty_dev):
        weight = jnp.where(cpty[:, 0:dates] == c, weight_ref[c : c + 1, :], weight)
    zero = jnp.zeros((SUBS, LANES), F32)
    spent, slopes = zero, []
    for t in range(dates):
        before = zero
        for s in range(1, min(t, LAG_MAX) + 1):
            before = jnp.where(lags[s - 1], owed[t - s], before)
        excess = owed[t] - before
        square = excess * excess + SMOOTH * SMOOTH
        inverse = lax.rsqrt(square)
        due = weight[:, t : t + 1]
        spent = spent + due * (0.5 * (excess + square * inverse))
        slopes.append(due * (0.5 * (1.0 + excess * inverse)))
    grads = []
    for t in range(dates):
        after = zero
        for s in range(1, min(dates - 1 - t, LAG_MAX) + 1):
            after = jnp.where(lags[s - 1], slopes[t + s], after)
        grads.append(((slopes[t] - after) * (1.0 / path_total)).astype(BF16))

    grads = jnp.concatenate(grads, axis=1)
    dots = [
        jnp.transpose(
            lax.dot_general(values[...], grads, BOTH_LANES, preferred_element_type=F32)
        )
        for values in val_refs
    ]
    dots = jnp.concatenate(dots, axis=1)
    share = jnp.sum(jnp.where(hot & (row < AG_DEV), dots, 0.0), axis=0, keepdims=True)
    spent = jnp.sum(spent, axis=1, keepdims=True) * (1.0 / path_total)
    mine = (lane - plan.slots == cpty) & (iota((SUBS, LANES), 0) < AG_DEV)
    cva = jnp.sum(jnp.where(mine, spent, 0.0), axis=0, keepdims=True)
    block = lane // part
    parts = plan.slots // part
    count = parts * plan.lines
    lines = jnp.concatenate([share[:, LANES * k : LANES * (k + 1)] for k in range(count)], axis=0)
    moved = [lines if m == 0 else pltpu.roll(lines, part * m, 1) for m in range(plan.per_line)]
    paths = out_ref.shape[0] // plan.owners
    for k in range(plan.lines):
        for s in range(plan.per_line):
            line = cva
            for g in range(parts):
                n = g * plan.lines + k
                line = jnp.where(block == g, moved[(g - s) % plan.per_line][n : n + 1], line)
            for p in range(paths):
                out_ref[(k * plan.per_line + s) * paths + p] = line


def finish_kernel(plan, me_ref, place_ref, notional_ref, in_ref, alloc_ref, cva_ref):
    me = me_ref[0]
    rows = place_ref.shape[1]
    key = place_ref[0:1, :].astype(jnp.int32)
    rank = place_ref[1:2, :].astype(jnp.int32)
    lines = in_ref[...]
    count = lines.shape[0]
    paths = count // plan.owners
    pieces = jnp.concatenate(split_bf16(lines, 3), axis=0)
    half = lax.rem(lax.rem(iota((pieces.shape[0], rows), 0), paths), plan.halves)
    found = jnp.zeros(half.shape, F32)
    for h in range(plan.halves):
        slot = lax.rem(rank + plan.room * h, plan.slots)
        hot = mask_bf16(iota((LANES, rows), 0) == slot)
        found = jnp.where(half == h, jnp.dot(pieces, hot, preferred_element_type=F32), found)
    wanted = lax.rem(iota(found.shape, 0), count) // paths == key
    share = jnp.sum(jnp.where(wanted, found, 0.0), axis=0, keepdims=True)
    alloc_ref[...] = share * in_a_row(notional_ref[...])
    own = iota(lines.shape, 0) // paths == me
    cva = jnp.sum(jnp.where(own, lines, 0.0), axis=0, keepdims=True)
    cva_ref[...] = cva[:, plan.slots : plan.slots + cva_ref.shape[1]]


def body(
    shocks,
    forward_start,
    loading,
    coefficient,
    notional,
    ns_of_trade,
    agr_of_ns,
    cpty_of_agr,
    margin_lag,
    default_weight,
):
    owners = lax.axis_size("trade")
    path_parts = lax.axis_size("path")
    tenors, dates, path_dev = shocks.shape
    path_total = float(path_dev * path_parts)
    rows = coefficient.shape[0]
    lines = rows // LANES
    plan = Plan(owners, rows, tenors, dates)
    cols = dates * path_dev
    me = lax.axis_index("trade").astype(jnp.int32).reshape(1)
    half = lax.rem(lax.axis_index("path").astype(jnp.int32), plan.halves).reshape(1)
    notional = notional.reshape(lines, LANES)

    place, outgoing = pl.pallas_call(
        functools.partial(pack_kernel, plan),
        out_shape=[
            jax.ShapeDtypeStruct((SUBS, rows), F32),
            jax.ShapeDtypeStruct((owners, plan.height, LANES), BF16),
        ],
        in_specs=[SMEM] * 2 + [HBM] * 3,
        out_specs=[VMEM, VMEM],
        scratch_shapes=[
            pltpu.VMEM((owners * lines, LANES), jnp.int32),
            pltpu.VMEM((2 * tenors, rows), BF16),
            pltpu.VMEM((lines, LANES), F32),
            pltpu.SemaphoreType.DMA((3,)),
        ],
        name="pack",
        cost_estimate=pl.CostEstimate(flops=1 << 32, bytes_accessed=1 << 19, transcendentals=0),
    )(me, half, ns_of_trade.reshape(owners * lines, LANES), coefficient.T, notional)
    incoming = [lax.all_to_all(outgoing, "trade", split_axis=0, concat_axis=0, tiled=True)]
    basis = pl.pallas_call(
        functools.partial(basis_kernel, plan),
        out_shape=jax.ShapeDtypeStruct((2 * LANES, cols), BF16),
        in_specs=[HBM] * 3,
        out_specs=VMEM,
        scratch_shapes=[
            pltpu.VMEM((tenors * dates, path_dev), BF16),
            pltpu.VMEM((1, tenors), F32),
            pltpu.VMEM((tenors, tenors), F32),
            pltpu.VMEM((tenors * dates, path_dev), F32),
            pltpu.SemaphoreType.DMA((3,)),
        ],
        name="basis",
        compiler_params=pltpu.CompilerParams(vmem_limit_bytes=16 << 20),
        cost_estimate=pl.CostEstimate(
            flops=2 * 400 * tenors * cols, bytes_accessed=4 << 20, transcendentals=3 * tenors * cols
        ),
    )(shocks.reshape(tenors * dates, path_dev), forward_start.reshape(1, tenors), loading)

    half_trades = plan.trades // plan.halves
    if plan.halves == 2:
        incoming[0], basis = lax.optimization_barrier((incoming[0], basis))
        pairs = [(p, p ^ 1) for p in range(path_parts)]
        incoming.append(lax.ppermute(incoming[0], "path", pairs))
        incoming.append(
            pl.pallas_call(
                functools.partial(price_kernel, plan),
                out_shape=jax.ShapeDtypeStruct((half_trades, cols), BF16),
                in_specs=[VMEM] * 2,
                out_specs=VMEM,
                name="price_own_half",
                compiler_params=pltpu.CompilerParams(vmem_limit_bytes=24 << 20),
                cost_estimate=pl.CostEstimate(
                    flops=4 * half_trades * LANES * cols, bytes_accessed=6 << 20, transcendentals=0
                ),
            )(basis, incoming[0])
        )

    need = 2 * plan.trades * cols + 8 * plan.trades * plan.step + (8 << 20)
    lines_out = pl.pallas_call(
        functools.partial(main_kernel, plan, path_total),
        out_shape=jax.ShapeDtypeStruct((owners * path_parts, 1, LANES), F32),
        in_specs=[SMEM] * 4 + [VMEM] * (2 + len(incoming)),
        out_specs=VMEM,
        scratch_shapes=[pltpu.VMEM((half_trades, cols), BF16)],
        name="value_and_allocate",
        compiler_params=pltpu.CompilerParams(vmem_limit_bytes=need),
    )(me, agr_of_ns, cpty_of_agr, margin_lag, default_weight, basis, *incoming)

    lines_in = lax.all_to_all(lines_out, ("trade", "path"), split_axis=0, concat_axis=0, tiled=True)
    lines_in = lines_in.reshape(owners * path_parts, LANES)
    allocation, cva = pl.pallas_call(
        functools.partial(finish_kernel, plan),
        out_shape=[
            jax.ShapeDtypeStruct((1, rows), F32),
            jax.ShapeDtypeStruct((1, default_weight.shape[0]), F32),
        ],
        in_specs=[SMEM] + [VMEM] * 3,
        out_specs=[VMEM, VMEM],
        name="finish",
        compiler_params=pltpu.CompilerParams(vmem_limit_bytes=32 << 20),
    )(me, place, notional, lines_in)
    return (allocation.reshape(rows), cva.reshape(default_weight.shape[0]))


def solution(mesh):
    placed = (
        P(None, None, "path"),
        P(),
        P(),
        P("trade", None),
        P("trade"),
        P(),
        P("trade"),
        P("trade"),
        P("trade"),
        P("trade", None),
    )
    return jax.shard_map(
        body, mesh=mesh, in_specs=placed, out_specs=(P("trade"), P("trade")), check_vma=False
    )
```

```python
import functools

import jax
import jax.numpy as jnp
from jax import lax
from jax.experimental import pallas as pl
from jax.experimental.pallas import tpu as pltpu
from jax.sharding import PartitionSpec as P

NS_DEV = 8
AG_DEV = 4
LAG_MAX = 4
LANES = 128
SUBS = 8

RATE_UNIT = 0.03
STEP = 0.25
SMOOTH = 0.5

F32 = jnp.float32
BF16 = jnp.bfloat16
VMEM = pl.BlockSpec(memory_space=pltpu.VMEM)
SMEM = pl.BlockSpec(memory_space=pltpu.SMEM)
HBM = pl.BlockSpec(memory_space=pltpu.HBM)
BOTH_LANES = (((1,), (1,)), ((), ()))


def iota(shape, dim):
    return lax.broadcasted_iota(jnp.int32, shape, dim)


def mask_bf16(mask):
    return mask.astype(F32).astype(BF16)


def split_bf16(x, parts):
    pieces = []
    for _ in range(parts):
        piece = x.astype(BF16)
        pieces.append(piece)
        x = x - piece.astype(F32)
    return pieces


def fetch(sources, targets, sems):
    copies = [pltpu.make_async_copy(a, b, sems.at[n]) for n, (a, b) in enumerate(zip(sources, targets))]
    for copy in copies:
        copy.start()
    return copies


def in_a_row(x):
    return jnp.concatenate([x[r : r + 1] for r in range(x.shape[0])], axis=1)


class Plan:
    def __init__(self, owners, rows, tenors, dates):
        most = 3 * rows // (2 * owners)
        self.owners = owners
        self.halves = 2 if most % 96 == 0 else 1
        most = most // self.halves
        self.groups = 3 if most % 48 == 0 else 1
        self.part = -(-most // (16 * self.groups)) * 16
        self.room = self.groups * self.part
        self.height = self.room + self.part
        self.extra = 2 * tenors - LANES
        self.per_line = LANES // self.part
        self.lines = owners * self.part // LANES
        self.slots = self.halves * self.room
        self.trades = owners * self.slots
        self.dates = dates
        self.width = 512
        self.step = 4096 if self.trades <= 1024 else 512


def pack_kernel(plan, me_ref, half_ref, sets_hbm, coef_hbm, notional_hbm, place_ref, out_ref, *refs):
    sets_ref, coef_ref, notional_ref, sems = refs
    copies = fetch(
        [sets_hbm, notional_hbm, coef_hbm], [sets_ref, notional_ref, coef_ref], sems
    )
    me = me_ref[0]
    owners, part, room, extra = plan.owners, plan.part, plan.room, plan.extra
    lines = notional_ref.shape[0]
    rows = lines * LANES
    shared = SUBS // lines
    copies[0].wait()
    block = sets_ref[pl.ds(pl.multiple_of(me // shared * SUBS, SUBS), SUBS), :]
    own = block[0:lines]
    for b in range(1, shared):
        own = jnp.where(lax.rem(me, shared) == b, block[b * lines : (b + 1) * lines], own)
    sets = in_a_row(own)
    key = lax.shift_right_logical(sets, 3)
    local = sets - key * NS_DEV
    hot = iota((owners, rows), 0) == key
    before = mask_bf16(iota((rows, rows), 0) < iota((rows, rows), 1))
    count = jnp.dot(mask_bf16(hot), before, preferred_element_type=F32)
    rank = jnp.sum(jnp.where(hot, count, 0.0), axis=0, keepdims=True)
    place_ref[...] = jnp.concatenate(
        [key.astype(F32), rank, jnp.zeros((SUBS - 2, rows), F32)], axis=0
    )
    mine = rank.astype(jnp.int32) - room * half_ref[0]
    spot = jnp.where((mine >= 0) & (mine < room), key * room + mine, -1)
    chosen = mask_bf16(iota((owners * room, rows), 0) == spot)
    copies[1].wait()
    notional = in_a_row(notional_ref[...])
    high = notional.astype(BF16).astype(F32)
    info = jnp.concatenate(
        [high, notional - high, local.astype(F32), jnp.zeros((13, rows), F32)], axis=0
    )
    copies[2].wait()
    table = jnp.concatenate([coef_ref[...], info.astype(BF16)], axis=0)
    moved = lax.dot_general(chosen, table, BOTH_LANES, preferred_element_type=F32)
    ids = LANES + extra
    for d in range(owners):
        message = out_ref.at[d]
        block = moved[d * room : (d + 1) * room]
        message[0:room, :] = block[:, 0:LANES].astype(BF16)
        split = [block[part * g : part * (g + 1)] for g in range(plan.groups)]
        lanes = [x[:, LANES:ids] for x in split]
        if plan.groups < 3:
            lanes.append(jnp.zeros((part, extra * (3 - plan.groups)), F32))
        lanes += [x[:, ids : ids + SUBS] for x in split]
        lanes.append(jnp.zeros((part, SUBS * (4 - plan.groups)), F32))
        message[room:, :] = jnp.concatenate(lanes, axis=1).astype(BF16)


def basis_kernel(plan, shocks_hbm, start_hbm, loading_hbm, out_ref, *refs):
    shocks_ref, start_ref, loading_ref, wide_ref, sems = refs
    copies = fetch(
        [loading_hbm, start_hbm, shocks_hbm], [loading_ref, start_ref, shocks_ref], sems
    )
    tenors = loading_ref.shape[0]
    dates = plan.dates
    copies[0].wait()
    copies[1].wait()
    loading_t = jnp.transpose(loading_ref[...])
    drift = 0.5 * STEP * jnp.sum(loading_t * loading_t, axis=1, keepdims=True)
    diag = iota((tenors, tenors), 0) == iota((tenors, tenors), 1)
    log_start = jnp.log(jnp.sum(jnp.where(diag, start_ref[...], 0.0), axis=1, keepdims=True))
    loads = jnp.concatenate(split_bf16((STEP**0.5) * loading_t, 3), axis=1)
    lower = mask_bf16(iota((tenors, tenors), 1) <= iota((tenors, tenors), 0))
    lower = jnp.concatenate([lower, lower], axis=1)
    log_fwd = jnp.broadcast_to(log_start, (tenors, LANES))
    drift = jnp.broadcast_to(drift, (tenors, LANES))
    head = LANES - tenors
    copies[2].wait()
    wide_ref[...] = shocks_ref[...].astype(F32)
    step = plan.width // LANES
    for c in range(dates // step):
        shock = jnp.concatenate(
            [
                wide_ref[pl.ds(c * step + j, tenors, stride=dates), :].astype(BF16)
                for j in range(step)
            ],
            axis=1,
        )
        change = jnp.dot(
            loads, jnp.concatenate([shock] * 3, axis=0), preferred_element_type=F32
        )
        logs = []
        for j in range(step):
            log_fwd = log_fwd + (change[:, LANES * j : LANES * (j + 1)] - drift)
            logs.append(log_fwd)
        fwd = jnp.exp(jnp.concatenate(logs, axis=1))
        growth = split_bf16(jnp.log(1.0 + STEP * fwd), 2)
        summed = jnp.dot(lower, jnp.concatenate(growth, axis=0), preferred_element_type=F32)
        bond = jnp.exp(-summed)
        cols = slice(c * plan.width, (c + 1) * plan.width)
        out_ref[0:tenors, cols] = (bond * fwd * (1.0 / RATE_UNIT)).astype(BF16)
        bond = bond.astype(BF16)
        out_ref[tenors:LANES, cols] = bond[0:head]
        for g in range(plan.groups):
            out_ref[LANES + plan.extra * g : LANES + plan.extra * (g + 1), cols] = bond[head:]
        used = LANES + plan.extra * plan.groups
        out_ref[used:, cols] = jnp.zeros((2 * LANES - used, plan.width), BF16)


def left_side(plan, in_ref):
    part, extra = plan.part, plan.extra
    rest = in_ref[:, plan.room :, :].reshape(plan.owners * part, LANES)
    lane = iota((1, LANES), 1)
    left = []
    for g in range(plan.groups):
        main = in_ref[:, part * g : part * (g + 1), :].reshape(plan.owners * part, LANES)
        keep = mask_bf16((lane >= extra * g) & (lane < extra * (g + 1)))
        left.append(jnp.concatenate([main, rest * keep], axis=1))
    return jnp.concatenate(left, axis=0), rest


def price(plan, left, basis_ref, val_ref):
    width = plan.step
    for c in range(basis_ref.shape[1] // width):
        cols = slice(c * width, (c + 1) * width)
        under = jnp.dot(left, basis_ref[:, cols], preferred_element_type=F32)
        val_ref[:, cols] = jnp.maximum(under.astype(BF16), 0)


def price_kernel(plan, basis_ref, in_ref, val_ref):
    price(plan, left_side(plan, in_ref)[0], basis_ref, val_ref)


def main_kernel(plan, path_total, me_ref, agr_ref, cpty_ref, lag_ref, weight_ref, basis_ref, *refs):
    *in_refs, out_ref, val_ref = refs
    val_refs = [val_ref]
    if plan.halves == 2:
        val_refs = [in_refs.pop(), val_ref]
    me = me_ref[0]
    part, room, dates = plan.part, plan.room, plan.dates
    cpty_dev = weight_ref.shape[0]

    lane = iota((1, LANES), 1)
    info = []
    for in_ref in in_refs:
        left, rest = left_side(plan, in_ref)
        for g in range(plan.groups):
            first = 3 * plan.extra + SUBS * g
            pick = mask_bf16(iota((SUBS, LANES), 1) == first + iota((SUBS, LANES), 0))
            info.append(lax.dot_general(pick, rest, BOTH_LANES, preferred_element_type=F32))
    info = jnp.concatenate(info, axis=1)
    local = info[2:3].astype(jnp.int32)
    agr = jnp.zeros_like(local)
    for n in range(NS_DEV):
        agr = jnp.where(local == n, agr_ref[n] - me * AG_DEV, agr)
    row = iota((SUBS, plan.trades), 0)
    hot = (row & (AG_DEV - 1)) == agr
    netting = jnp.where(hot, jnp.where(row < AG_DEV, info[0:1], info[1:2]), 0.0).astype(BF16)

    price(plan, left, basis_ref, val_ref)
    size = val_ref.shape[0]
    both = jnp.zeros((SUBS, val_ref.shape[1]), F32)
    for h, values in enumerate(val_refs):
        both = both + jnp.dot(
            netting[:, size * h : size * (h + 1)], values[...], preferred_element_type=F32
        )
    both = both + pltpu.roll(both, AG_DEV, 0)
    owed = [both[:, LANES * t : LANES * (t + 1)] for t in range(dates)]

    member = iota((SUBS, LANES), 0) & (AG_DEV - 1)
    lag = jnp.zeros((SUBS, LANES), jnp.int32)
    cpty = jnp.zeros((SUBS, LANES), jnp.int32)
    for a in range(AG_DEV):
        lag = jnp.where(member == a, lag_ref[a], lag)
        cpty = jnp.where(member == a, cpty_ref[a] - me * cpty_dev, cpty)
    lags = [lag == s for s in range(1, LAG_MAX + 1)]
    weight = jnp.zeros((SUBS, dates), F32)
    for c in range(cpty_dev):
        weight = jnp.where(cpty[:, 0:dates] == c, weight_ref[c : c + 1, :], weight)
    zero = jnp.zeros((SUBS, LANES), F32)
    spent, slopes = zero, []
    for t in range(dates):
        before = zero
        for s in range(1, min(t, LAG_MAX) + 1):
            before = jnp.where(lags[s - 1], owed[t - s], before)
        excess = owed[t] - before
        square = excess * excess + SMOOTH * SMOOTH
        inverse = lax.rsqrt(square)
        due = weight[:, t : t + 1]
        spent = spent + due * (0.5 * (excess + square * inverse))
        slopes.append(due * (0.5 * (1.0 + excess * inverse)))
    grads = []
    for t in range(dates):
        after = zero
        for s in range(1, min(dates - 1 - t, LAG_MAX) + 1):
            after = jnp.where(lags[s - 1], slopes[t + s], after)
        grads.append(((slopes[t] - after) * (1.0 / path_total)).astype(BF16))

    grads = jnp.concatenate(grads, axis=1)
    dots = [
        lax.dot_general(grads, values[...], BOTH_LANES, preferred_element_type=F32)
        for values in val_refs
    ]
    dots = jnp.concatenate(dots, axis=1)
    share = jnp.sum(jnp.where(hot & (row < AG_DEV), dots, 0.0), axis=0, keepdims=True)
    spent = jnp.sum(spent, axis=1, keepdims=True) * (1.0 / path_total)
    mine = (lane - plan.slots == cpty) & (iota((SUBS, LANES), 0) < AG_DEV)
    cva = jnp.sum(jnp.where(mine, spent, 0.0), axis=0, keepdims=True)
    block = lane // part
    parts = plan.slots // part
    count = parts * plan.lines
    lines = jnp.concatenate([share[:, LANES * k : LANES * (k + 1)] for k in range(count)], axis=0)
    moved = [lines if m == 0 else pltpu.roll(lines, part * m, 1) for m in range(plan.per_line)]
    paths = out_ref.shape[0] // plan.owners
    for k in range(plan.lines):
        for s in range(plan.per_line):
            line = cva
            for g in range(parts):
                n = g * plan.lines + k
                line = jnp.where(block == g, moved[(g - s) % plan.per_line][n : n + 1], line)
            for p in range(paths):
                out_ref[(k * plan.per_line + s) * paths + p] = line


def finish_kernel(plan, me_ref, place_ref, notional_ref, in_ref, alloc_ref, cva_ref):
    me = me_ref[0]
    rows = place_ref.shape[1]
    key = place_ref[0:1, :].astype(jnp.int32)
    rank = place_ref[1:2, :].astype(jnp.int32)
    lines = in_ref[...]
    count = lines.shape[0]
    paths = count // plan.owners
    pieces = jnp.concatenate(split_bf16(lines, 3), axis=0)
    row = iota((pieces.shape[0], 1), 0) & (count - 1)
    shift = paths.bit_length() - 1
    half = row & (plan.halves - 1)
    found = jnp.zeros((pieces.shape[0], rows), F32)
    for h in range(plan.halves):
        slot = rank + plan.room * h
        slot = jnp.where(slot >= plan.slots, slot - plan.slots, slot)
        hot = mask_bf16(iota((LANES, rows), 0) == slot)
        found = jnp.where(half == h, jnp.dot(pieces, hot, preferred_element_type=F32), found)
    wanted = lax.shift_right_logical(row, shift) == key
    share = jnp.sum(jnp.where(wanted, found, 0.0), axis=0, keepdims=True)
    alloc_ref[...] = share * in_a_row(notional_ref[...])
    own = lax.shift_right_logical(iota((count, 1), 0), shift) == me
    cva = jnp.sum(jnp.where(own, lines, 0.0), axis=0, keepdims=True)
    cva_ref[...] = cva[:, plan.slots : plan.slots + cva_ref.shape[1]]


def body(
    shocks,
    forward_start,
    loading,
    coefficient,
    notional,
    ns_of_trade,
    agr_of_ns,
    cpty_of_agr,
    margin_lag,
    default_weight,
):
    owners = lax.axis_size("trade")
    path_parts = lax.axis_size("path")
    tenors, dates, path_dev = shocks.shape
    path_total = float(path_dev * path_parts)
    rows = coefficient.shape[0]
    lines = rows // LANES
    plan = Plan(owners, rows, tenors, dates)
    cols = dates * path_dev
    me = lax.axis_index("trade").astype(jnp.int32).reshape(1)
    half = lax.rem(lax.axis_index("path").astype(jnp.int32), plan.halves).reshape(1)
    notional = notional.reshape(lines, LANES)

    place, outgoing = pl.pallas_call(
        functools.partial(pack_kernel, plan),
        out_shape=[
            jax.ShapeDtypeStruct((SUBS, rows), F32),
            jax.ShapeDtypeStruct((owners, plan.height, LANES), BF16),
        ],
        in_specs=[SMEM] * 2 + [HBM] * 3,
        out_specs=[VMEM, VMEM],
        scratch_shapes=[
            pltpu.VMEM((owners * lines, LANES), jnp.int32),
            pltpu.VMEM((2 * tenors, rows), BF16),
            pltpu.VMEM((lines, LANES), F32),
            pltpu.SemaphoreType.DMA((3,)),
        ],
        name="pack",
        cost_estimate=pl.CostEstimate(flops=1 << 32, bytes_accessed=1 << 19, transcendentals=0),
    )(me, half, ns_of_trade.reshape(owners * lines, LANES), coefficient.T, notional)
    incoming = [lax.all_to_all(outgoing, "trade", split_axis=0, concat_axis=0, tiled=True)]
    basis = pl.pallas_call(
        functools.partial(basis_kernel, plan),
        out_shape=jax.ShapeDtypeStruct((2 * LANES, cols), BF16),
        in_specs=[HBM] * 3,
        out_specs=VMEM,
        scratch_shapes=[
            pltpu.VMEM((tenors * dates, path_dev), BF16),
            pltpu.VMEM((1, tenors), F32),
            pltpu.VMEM((tenors, tenors), F32),
            pltpu.VMEM((tenors * dates, path_dev), F32),
            pltpu.SemaphoreType.DMA((3,)),
        ],
        name="basis",
        compiler_params=pltpu.CompilerParams(vmem_limit_bytes=16 << 20),
        cost_estimate=pl.CostEstimate(
            flops=2 * 400 * tenors * cols, bytes_accessed=4 << 20, transcendentals=3 * tenors * cols
        ),
    )(shocks.reshape(tenors * dates, path_dev), forward_start.reshape(1, tenors), loading)

    half_trades = plan.trades // plan.halves
    if plan.halves == 2:
        incoming[0], basis = lax.optimization_barrier((incoming[0], basis))
        pairs = [(p, p ^ 1) for p in range(path_parts)]
        incoming.append(lax.ppermute(incoming[0], "path", pairs))
        incoming.append(
            pl.pallas_call(
                functools.partial(price_kernel, plan),
                out_shape=jax.ShapeDtypeStruct((half_trades, cols), BF16),
                in_specs=[VMEM] * 2,
                out_specs=VMEM,
                name="price_own_half",
                compiler_params=pltpu.CompilerParams(vmem_limit_bytes=24 << 20),
                cost_estimate=pl.CostEstimate(
                    flops=4 * half_trades * LANES * cols, bytes_accessed=6 << 20, transcendentals=0
                ),
            )(basis, incoming[0])
        )

    need = 2 * plan.trades * cols + 8 * plan.trades * plan.step + (8 << 20)
    lines_out = pl.pallas_call(
        functools.partial(main_kernel, plan, path_total),
        out_shape=jax.ShapeDtypeStruct((owners * path_parts, 1, LANES), F32),
        in_specs=[SMEM] * 4 + [VMEM] * (2 + len(incoming)),
        out_specs=VMEM,
        scratch_shapes=[pltpu.VMEM((half_trades, cols), BF16)],
        name="value_and_allocate",
        compiler_params=pltpu.CompilerParams(vmem_limit_bytes=need),
    )(me, agr_of_ns, cpty_of_agr, margin_lag, default_weight, basis, *incoming)

    lines_in = lax.all_to_all(lines_out, ("trade", "path"), split_axis=0, concat_axis=0, tiled=True)
    lines_in = lines_in.reshape(owners * path_parts, LANES)
    allocation, cva = pl.pallas_call(
        functools.partial(finish_kernel, plan),
        out_shape=[
            jax.ShapeDtypeStruct((1, rows), F32),
            jax.ShapeDtypeStruct((1, default_weight.shape[0]), F32),
        ],
        in_specs=[SMEM] + [VMEM] * 3,
        out_specs=[VMEM, VMEM],
        name="finish",
        compiler_params=pltpu.CompilerParams(vmem_limit_bytes=32 << 20),
    )(me, place, notional, lines_in)
    return (allocation.reshape(rows), cva.reshape(default_weight.shape[0]))


def solution(mesh):
    placed = (
        P(None, None, "path"),
        P(),
        P(),
        P("trade", None),
        P("trade"),
        P(),
        P("trade"),
        P("trade"),
        P("trade"),
        P("trade", None),
    )
    return jax.shard_map(
        body, mesh=mesh, in_specs=placed, out_specs=(P("trade"), P("trade")), check_vma=False
    )
```

```python
import functools

import jax
import jax.numpy as jnp
from jax import lax
from jax.experimental import pallas as pl
from jax.experimental.pallas import tpu as pltpu
from jax.sharding import PartitionSpec as P

NS_DEV = 8
AG_DEV = 4
LAG_MAX = 4
LANES = 128
SUBS = 8

RATE_UNIT = 0.03
STEP = 0.25
SMOOTH = 0.5

F32 = jnp.float32
BF16 = jnp.bfloat16
VMEM = pl.BlockSpec(memory_space=pltpu.VMEM)
SMEM = pl.BlockSpec(memory_space=pltpu.SMEM)
HBM = pl.BlockSpec(memory_space=pltpu.HBM)
BOTH_LANES = (((1,), (1,)), ((), ()))


def iota(shape, dim):
    return lax.broadcasted_iota(jnp.int32, shape, dim)


def mask_bf16(mask):
    return mask.astype(F32).astype(BF16)


def split_bf16(x, parts):
    pieces = []
    for _ in range(parts):
        piece = x.astype(BF16)
        pieces.append(piece)
        x = x - piece.astype(F32)
    return pieces


def fetch(sources, targets, sems):
    copies = [pltpu.make_async_copy(a, b, sems.at[n]) for n, (a, b) in enumerate(zip(sources, targets))]
    for copy in copies:
        copy.start()
    return copies


def in_a_row(x):
    return jnp.concatenate([x[r : r + 1] for r in range(x.shape[0])], axis=1)


class Plan:
    def __init__(self, owners, rows, tenors, dates):
        most = 3 * rows // (2 * owners)
        self.owners = owners
        self.halves = 2 if most % 96 == 0 else 1
        most = most // self.halves
        self.groups = 3 if most % 48 == 0 else 1
        self.part = -(-most // (16 * self.groups)) * 16
        self.room = self.groups * self.part
        self.height = self.room + self.part
        self.extra = 2 * tenors - LANES
        self.per_line = LANES // self.part
        self.lines = owners * self.part // LANES
        self.slots = self.halves * self.room
        self.trades = owners * self.slots
        self.dates = dates
        self.width = 1024
        self.step = 2048 if self.trades <= 1024 else 512


def pack_kernel(plan, me_ref, half_ref, sets_hbm, coef_hbm, notional_hbm, place_ref, out_ref, *refs):
    sets_ref, coef_ref, notional_ref, sems = refs
    copies = fetch(
        [sets_hbm, notional_hbm, coef_hbm], [sets_ref, notional_ref, coef_ref], sems
    )
    me = me_ref[0]
    owners, part, room, extra = plan.owners, plan.part, plan.room, plan.extra
    lines = notional_ref.shape[0]
    rows = lines * LANES
    shared = SUBS // lines
    copies[0].wait()
    block = sets_ref[pl.ds(pl.multiple_of(me // shared * SUBS, SUBS), SUBS), :]
    own = block[0:lines]
    for b in range(1, shared):
        own = jnp.where(lax.rem(me, shared) == b, block[b * lines : (b + 1) * lines], own)
    sets = in_a_row(own)
    key = lax.shift_right_logical(sets, 3)
    local = sets - key * NS_DEV
    hot = iota((owners, rows), 0) == key
    before = mask_bf16(iota((rows, rows), 0) < iota((rows, rows), 1))
    count = jnp.dot(mask_bf16(hot), before, preferred_element_type=F32)
    rank = jnp.sum(jnp.where(hot, count, 0.0), axis=0, keepdims=True)
    place_ref[...] = jnp.concatenate(
        [key.astype(F32), rank, jnp.zeros((SUBS - 2, rows), F32)], axis=0
    )
    mine = rank.astype(jnp.int32) - room * half_ref[0]
    spot = jnp.where((mine >= 0) & (mine < room), key * room + mine, -1)
    chosen = mask_bf16(iota((owners * room, rows), 0) == spot)
    copies[1].wait()
    notional = in_a_row(notional_ref[...])
    high = notional.astype(BF16).astype(F32)
    info = jnp.concatenate(
        [high, notional - high, local.astype(F32), jnp.zeros((13, rows), F32)], axis=0
    )
    copies[2].wait()
    table = jnp.concatenate([coef_ref[...], info.astype(BF16)], axis=0)
    moved = lax.dot_general(chosen, table, BOTH_LANES, preferred_element_type=F32)
    ids = LANES + extra
    for d in range(owners):
        message = out_ref.at[d]
        block = moved[d * room : (d + 1) * room]
        message[0:room, :] = block[:, 0:LANES].astype(BF16)
        split = [block[part * g : part * (g + 1)] for g in range(plan.groups)]
        lanes = [x[:, LANES:ids] for x in split]
        if plan.groups < 3:
            lanes.append(jnp.zeros((part, extra * (3 - plan.groups)), F32))
        lanes += [x[:, ids : ids + SUBS] for x in split]
        lanes.append(jnp.zeros((part, SUBS * (4 - plan.groups)), F32))
        message[room:, :] = jnp.concatenate(lanes, axis=1).astype(BF16)


def basis_kernel(plan, shocks_hbm, start_hbm, loading_hbm, out_ref, *refs):
    shocks_ref, start_ref, loading_ref, wide_ref, sems = refs
    copies = fetch(
        [loading_hbm, start_hbm, shocks_hbm], [loading_ref, start_ref, shocks_ref], sems
    )
    tenors = loading_ref.shape[0]
    dates = plan.dates
    copies[0].wait()
    copies[1].wait()
    loading_t = jnp.transpose(loading_ref[...])
    drift = 0.5 * STEP * jnp.sum(loading_t * loading_t, axis=1, keepdims=True)
    diag = iota((tenors, tenors), 0) == iota((tenors, tenors), 1)
    log_start = jnp.log(jnp.sum(jnp.where(diag, start_ref[...], 0.0), axis=1, keepdims=True))
    loads = jnp.concatenate(split_bf16((STEP**0.5) * loading_t, 3), axis=1)
    lower = mask_bf16(iota((tenors, tenors), 1) <= iota((tenors, tenors), 0))
    lower = jnp.concatenate([lower, lower], axis=1)
    log_fwd = jnp.broadcast_to(log_start, (tenors, LANES))
    drift = jnp.broadcast_to(drift, (tenors, LANES))
    head = LANES - tenors
    copies[2].wait()
    wide_ref[...] = shocks_ref[...].astype(F32)
    step = plan.width // LANES
    for c in range(dates // step):
        shock = jnp.concatenate(
            [
                wide_ref[pl.ds(c * step + j, tenors, stride=dates), :].astype(BF16)
                for j in range(step)
            ],
            axis=1,
        )
        change = jnp.dot(
            loads, jnp.concatenate([shock] * 3, axis=0), preferred_element_type=F32
        )
        logs = []
        for j in range(step):
            log_fwd = log_fwd + (change[:, LANES * j : LANES * (j + 1)] - drift)
            logs.append(log_fwd)
        fwd = jnp.exp(jnp.concatenate(logs, axis=1))
        growth = split_bf16(jnp.log(1.0 + STEP * fwd), 2)
        summed = jnp.dot(lower, jnp.concatenate(growth, axis=0), preferred_element_type=F32)
        bond = jnp.exp(-summed)
        cols = slice(c * plan.width, (c + 1) * plan.width)
        out_ref[0:tenors, cols] = (bond * fwd * (1.0 / RATE_UNIT)).astype(BF16)
        bond = bond.astype(BF16)
        out_ref[tenors:LANES, cols] = bond[0:head]
        for g in range(plan.groups):
            out_ref[LANES + plan.extra * g : LANES + plan.extra * (g + 1), cols] = bond[head:]
        used = LANES + plan.extra * plan.groups
        out_ref[used:, cols] = jnp.zeros((2 * LANES - used, plan.width), BF16)


def left_side(plan, in_ref):
    part, extra = plan.part, plan.extra
    rest = in_ref[:, plan.room :, :].reshape(plan.owners * part, LANES)
    lane = iota((1, LANES), 1)
    left = []
    for g in range(plan.groups):
        main = in_ref[:, part * g : part * (g + 1), :].reshape(plan.owners * part, LANES)
        keep = mask_bf16((lane >= extra * g) & (lane < extra * (g + 1)))
        left.append(jnp.concatenate([main, rest * keep], axis=1))
    return jnp.concatenate(left, axis=0), rest


def price(plan, left, basis_ref, val_ref):
    width = plan.step
    for c in range(basis_ref.shape[1] // width):
        cols = slice(c * width, (c + 1) * width)
        under = jnp.dot(left, basis_ref[:, cols], preferred_element_type=F32)
        val_ref[:, cols] = jnp.maximum(under.astype(BF16), 0)


def price_kernel(plan, basis_ref, in_ref, val_ref):
    price(plan, left_side(plan, in_ref)[0], basis_ref, val_ref)


def main_kernel(plan, path_total, me_ref, agr_ref, cpty_ref, lag_ref, weight_ref, basis_ref, *refs):
    *in_refs, out_ref, val_ref = refs
    val_refs = [val_ref]
    if plan.halves == 2:
        val_refs = [in_refs.pop(), val_ref]
    me = me_ref[0]
    part, room, dates = plan.part, plan.room, plan.dates
    cpty_dev = weight_ref.shape[0]

    lane = iota((1, LANES), 1)
    info = []
    for in_ref in in_refs:
        left, rest = left_side(plan, in_ref)
        for g in range(plan.groups):
            first = 3 * plan.extra + SUBS * g
            pick = mask_bf16(iota((SUBS, LANES), 1) == first + iota((SUBS, LANES), 0))
            info.append(lax.dot_general(pick, rest, BOTH_LANES, preferred_element_type=F32))
    info = jnp.concatenate(info, axis=1)
    local = info[2:3].astype(jnp.int32)
    agr = jnp.zeros_like(local)
    for n in range(NS_DEV):
        agr = jnp.where(local == n, agr_ref[n] - me * AG_DEV, agr)
    row = iota((SUBS, plan.trades), 0)
    hot = (row & (AG_DEV - 1)) == agr
    netting = jnp.where(hot, jnp.where(row < AG_DEV, info[0:1], info[1:2]), 0.0).astype(BF16)

    price(plan, left, basis_ref, val_ref)
    size = val_ref.shape[0]
    both = jnp.zeros((SUBS, val_ref.shape[1]), F32)
    for h, values in enumerate(val_refs):
        both = both + jnp.dot(
            netting[:, size * h : size * (h + 1)], values[...], preferred_element_type=F32
        )
    both = both + pltpu.roll(both, AG_DEV, 0)
    owed = [both[:, LANES * t : LANES * (t + 1)] for t in range(dates)]

    member = iota((SUBS, LANES), 0) & (AG_DEV - 1)
    lag = jnp.zeros((SUBS, LANES), jnp.int32)
    cpty = jnp.zeros((SUBS, LANES), jnp.int32)
    for a in range(AG_DEV):
        lag = jnp.where(member == a, lag_ref[a], lag)
        cpty = jnp.where(member == a, cpty_ref[a] - me * cpty_dev, cpty)
    lags = [lag == s for s in range(1, LAG_MAX + 1)]
    weight = jnp.zeros((SUBS, dates), F32)
    for c in range(cpty_dev):
        weight = jnp.where(cpty[:, 0:dates] == c, weight_ref[c : c + 1, :], weight)
    zero = jnp.zeros((SUBS, LANES), F32)
    spent, slopes = zero, []
    for t in range(dates):
        before = zero
        for s in range(1, min(t, LAG_MAX) + 1):
            before = jnp.where(lags[s - 1], owed[t - s], before)
        excess = owed[t] - before
        square = excess * excess + SMOOTH * SMOOTH
        inverse = lax.rsqrt(square)
        due = weight[:, t : t + 1]
        spent = spent + due * (0.5 * (excess + square * inverse))
        slopes.append(due * (0.5 * (1.0 + excess * inverse)))
    grads = []
    for t in range(dates):
        after = zero
        for s in range(1, min(dates - 1 - t, LAG_MAX) + 1):
            after = jnp.where(lags[s - 1], slopes[t + s], after)
        grads.append(((slopes[t] - after) * (1.0 / path_total)).astype(BF16))

    grads = jnp.concatenate(grads, axis=1)
    dots = [
        lax.dot_general(grads, values[...], BOTH_LANES, preferred_element_type=F32)
        for values in val_refs
    ]
    dots = jnp.concatenate(dots, axis=1)
    share = jnp.sum(jnp.where(hot & (row < AG_DEV), dots, 0.0), axis=0, keepdims=True)
    spent = jnp.sum(spent, axis=1, keepdims=True) * (1.0 / path_total)
    mine = (lane - plan.slots == cpty) & (iota((SUBS, LANES), 0) < AG_DEV)
    cva = jnp.sum(jnp.where(mine, spent, 0.0), axis=0, keepdims=True)
    block = lane // part
    parts = plan.slots // part
    count = parts * plan.lines
    lines = jnp.concatenate([share[:, LANES * k : LANES * (k + 1)] for k in range(count)], axis=0)
    moved = [lines if m == 0 else pltpu.roll(lines, part * m, 1) for m in range(plan.per_line)]
    paths = out_ref.shape[0] // plan.owners
    for k in range(plan.lines):
        for s in range(plan.per_line):
            line = cva
            for g in range(parts):
                n = g * plan.lines + k
                line = jnp.where(block == g, moved[(g - s) % plan.per_line][n : n + 1], line)
            for p in range(paths):
                out_ref[(k * plan.per_line + s) * paths + p] = line


def finish_kernel(plan, me_ref, place_ref, notional_ref, in_ref, alloc_ref, cva_ref):
    me = me_ref[0]
    rows = place_ref.shape[1]
    key = place_ref[0:1, :].astype(jnp.int32)
    rank = place_ref[1:2, :].astype(jnp.int32)
    lines = in_ref[...]
    count = lines.shape[0]
    paths = count // plan.owners
    pieces = jnp.concatenate(split_bf16(lines, 3), axis=0)
    row = iota((pieces.shape[0], 1), 0) & (count - 1)
    shift = paths.bit_length() - 1
    half = row & (plan.halves - 1)
    found = jnp.zeros((pieces.shape[0], rows), F32)
    for h in range(plan.halves):
        slot = rank + plan.room * h
        slot = jnp.where(slot >= plan.slots, slot - plan.slots, slot)
        hot = mask_bf16(iota((LANES, rows), 0) == slot)
        found = jnp.where(half == h, jnp.dot(pieces, hot, preferred_element_type=F32), found)
    wanted = lax.shift_right_logical(row, shift) == key
    share = jnp.sum(jnp.where(wanted, found, 0.0), axis=0, keepdims=True)
    alloc_ref[...] = share * in_a_row(notional_ref[...])
    own = lax.shift_right_logical(iota((count, 1), 0), shift) == me
    cva = jnp.sum(jnp.where(own, lines, 0.0), axis=0, keepdims=True)
    cva_ref[...] = cva[:, plan.slots : plan.slots + cva_ref.shape[1]]


def body(
    shocks,
    forward_start,
    loading,
    coefficient,
    notional,
    ns_of_trade,
    agr_of_ns,
    cpty_of_agr,
    margin_lag,
    default_weight,
):
    owners = lax.axis_size("trade")
    path_parts = lax.axis_size("path")
    tenors, dates, path_dev = shocks.shape
    path_total = float(path_dev * path_parts)
    rows = coefficient.shape[0]
    lines = rows // LANES
    plan = Plan(owners, rows, tenors, dates)
    cols = dates * path_dev
    me = lax.axis_index("trade").astype(jnp.int32).reshape(1)
    half = lax.rem(lax.axis_index("path").astype(jnp.int32), plan.halves).reshape(1)
    notional = notional.reshape(lines, LANES)

    place, outgoing = pl.pallas_call(
        functools.partial(pack_kernel, plan),
        out_shape=[
            jax.ShapeDtypeStruct((SUBS, rows), F32),
            jax.ShapeDtypeStruct((owners, plan.height, LANES), BF16),
        ],
        in_specs=[SMEM] * 2 + [HBM] * 3,
        out_specs=[VMEM, VMEM],
        scratch_shapes=[
            pltpu.VMEM((owners * lines, LANES), jnp.int32),
            pltpu.VMEM((2 * tenors, rows), BF16),
            pltpu.VMEM((lines, LANES), F32),
            pltpu.SemaphoreType.DMA((3,)),
        ],
        name="pack",
        cost_estimate=pl.CostEstimate(flops=1 << 32, bytes_accessed=1 << 19, transcendentals=0),
    )(me, half, ns_of_trade.reshape(owners * lines, LANES), coefficient.T, notional)
    incoming = [lax.all_to_all(outgoing, "trade", split_axis=0, concat_axis=0, tiled=True)]
    basis = pl.pallas_call(
        functools.partial(basis_kernel, plan),
        out_shape=jax.ShapeDtypeStruct((2 * LANES, cols), BF16),
        in_specs=[HBM] * 3,
        out_specs=VMEM,
        scratch_shapes=[
            pltpu.VMEM((tenors * dates, path_dev), BF16),
            pltpu.VMEM((1, tenors), F32),
            pltpu.VMEM((tenors, tenors), F32),
            pltpu.VMEM((tenors * dates, path_dev), F32),
            pltpu.SemaphoreType.DMA((3,)),
        ],
        name="basis",
        compiler_params=pltpu.CompilerParams(vmem_limit_bytes=16 << 20),
        cost_estimate=pl.CostEstimate(
            flops=2 * 400 * tenors * cols, bytes_accessed=4 << 20, transcendentals=3 * tenors * cols
        ),
    )(shocks.reshape(tenors * dates, path_dev), forward_start.reshape(1, tenors), loading)

    half_trades = plan.trades // plan.halves
    if plan.halves == 2:
        incoming[0], basis = lax.optimization_barrier((incoming[0], basis))
        pairs = [(p, p ^ 1) for p in range(path_parts)]
        incoming.append(lax.ppermute(incoming[0], "path", pairs))
        incoming.append(
            pl.pallas_call(
                functools.partial(price_kernel, plan),
                out_shape=jax.ShapeDtypeStruct((half_trades, cols), BF16),
                in_specs=[VMEM] * 2,
                out_specs=VMEM,
                name="price_own_half",
                compiler_params=pltpu.CompilerParams(vmem_limit_bytes=24 << 20),
                cost_estimate=pl.CostEstimate(
                    flops=4 * half_trades * LANES * cols, bytes_accessed=6 << 20, transcendentals=0
                ),
            )(basis, incoming[0])
        )

    need = 2 * plan.trades * cols + 8 * plan.trades * plan.step + (8 << 20)
    lines_out = pl.pallas_call(
        functools.partial(main_kernel, plan, path_total),
        out_shape=jax.ShapeDtypeStruct((owners * path_parts, 1, LANES), F32),
        in_specs=[SMEM] * 4 + [VMEM] * (2 + len(incoming)),
        out_specs=VMEM,
        scratch_shapes=[pltpu.VMEM((half_trades, cols), BF16)],
        name="value_and_allocate",
        compiler_params=pltpu.CompilerParams(vmem_limit_bytes=need),
    )(me, agr_of_ns, cpty_of_agr, margin_lag, default_weight, basis, *incoming)

    lines_in = lax.all_to_all(lines_out, ("trade", "path"), split_axis=0, concat_axis=0, tiled=True)
    lines_in = lines_in.reshape(owners * path_parts, LANES)
    allocation, cva = pl.pallas_call(
        functools.partial(finish_kernel, plan),
        out_shape=[
            jax.ShapeDtypeStruct((1, rows), F32),
            jax.ShapeDtypeStruct((1, default_weight.shape[0]), F32),
        ],
        in_specs=[SMEM] + [VMEM] * 3,
        out_specs=[VMEM, VMEM],
        name="finish",
        compiler_params=pltpu.CompilerParams(vmem_limit_bytes=32 << 20),
    )(me, place, notional, lines_in)
    return (allocation.reshape(rows), cva.reshape(default_weight.shape[0]))


def solution(mesh):
    placed = (
        P(None, None, "path"),
        P(),
        P(),
        P("trade", None),
        P("trade"),
        P(),
        P("trade"),
        P("trade"),
        P("trade"),
        P("trade", None),
    )
    return jax.shard_map(
        body, mesh=mesh, in_specs=placed, out_specs=(P("trade"), P("trade")), check_vma=False
    )
```

```python
import functools

import jax
import jax.numpy as jnp
from jax import lax
from jax.experimental import pallas as pl
from jax.experimental.pallas import tpu as pltpu
from jax.sharding import PartitionSpec as P

NS_DEV = 8
AG_DEV = 4
LAG_MAX = 4
LANES = 128
SUBS = 8

RATE_UNIT = 0.03
STEP = 0.25
SMOOTH = 0.5

F32 = jnp.float32
BF16 = jnp.bfloat16
VMEM = pl.BlockSpec(memory_space=pltpu.VMEM)
SMEM = pl.BlockSpec(memory_space=pltpu.SMEM)
HBM = pl.BlockSpec(memory_space=pltpu.HBM)
BOTH_LANES = (((1,), (1,)), ((), ()))


def iota(shape, dim):
    return lax.broadcasted_iota(jnp.int32, shape, dim)


def mask_bf16(mask):
    return mask.astype(F32).astype(BF16)


def split_bf16(x, parts):
    pieces = []
    for _ in range(parts):
        piece = x.astype(BF16)
        pieces.append(piece)
        x = x - piece.astype(F32)
    return pieces


def fetch(sources, targets, sems):
    copies = [pltpu.make_async_copy(a, b, sems.at[n]) for n, (a, b) in enumerate(zip(sources, targets))]
    for copy in copies:
        copy.start()
    return copies


def in_a_row(x):
    return jnp.concatenate([x[r : r + 1] for r in range(x.shape[0])], axis=1)


class Plan:
    def __init__(self, owners, rows, tenors, dates):
        most = 3 * rows // (2 * owners)
        self.owners = owners
        self.halves = 2 if most % 96 == 0 else 1
        most = most // self.halves
        self.groups = 3 if most % 48 == 0 else 1
        self.part = -(-most // (16 * self.groups)) * 16
        self.room = self.groups * self.part
        self.height = self.room + self.part
        self.extra = 2 * tenors - LANES
        self.per_line = LANES // self.part
        self.lines = owners * self.part // LANES
        self.slots = self.halves * self.room
        self.trades = owners * self.slots
        self.dates = dates
        self.width = 1024
        self.step = 2048 if self.trades <= 1024 else 512


def pack_kernel(plan, me_ref, half_ref, sets_hbm, coef_hbm, notional_hbm, place_ref, out_ref, *refs):
    sets_ref, coef_ref, notional_ref, sems = refs
    copies = fetch(
        [sets_hbm, notional_hbm, coef_hbm], [sets_ref, notional_ref, coef_ref], sems
    )
    me = me_ref[0]
    owners, part, room, extra = plan.owners, plan.part, plan.room, plan.extra
    lines = notional_ref.shape[0]
    rows = lines * LANES
    shared = SUBS // lines
    before = mask_bf16(iota((rows, rows), 0) < iota((rows, rows), 1))
    copies[0].wait()
    block = sets_ref[pl.ds(pl.multiple_of(me // shared * SUBS, SUBS), SUBS), :]
    own = block[0:lines]
    for b in range(1, shared):
        own = jnp.where(lax.rem(me, shared) == b, block[b * lines : (b + 1) * lines], own)
    sets = in_a_row(own)
    key = lax.shift_right_logical(sets, 3)
    local = sets - key * NS_DEV
    copies[1].wait()
    notional = in_a_row(notional_ref[...])
    high = notional.astype(BF16).astype(F32)
    info = jnp.concatenate(
        [high, notional - high, local.astype(F32), jnp.zeros((13, rows), F32)], axis=0
    )
    copies[2].wait()
    table = jnp.concatenate([coef_ref[...], info.astype(BF16)], axis=0)
    hot = iota((owners, rows), 0) == key
    count = jnp.dot(mask_bf16(hot), before, preferred_element_type=F32)
    rank = jnp.sum(jnp.where(hot, count, 0.0), axis=0, keepdims=True)
    place_ref[...] = jnp.concatenate(
        [key.astype(F32), rank, jnp.zeros((SUBS - 2, rows), F32)], axis=0
    )
    mine = rank.astype(jnp.int32) - room * half_ref[0]
    spot = jnp.where((mine >= 0) & (mine < room), key * room + mine, -1)
    chosen = mask_bf16(iota((owners * room, rows), 0) == spot)
    moved = lax.dot_general(chosen, table, BOTH_LANES, preferred_element_type=F32)
    ids = LANES + extra
    for d in range(owners):
        message = out_ref.at[d]
        block = moved[d * room : (d + 1) * room]
        message[0:room, :] = block[:, 0:LANES].astype(BF16)
        split = [block[part * g : part * (g + 1)] for g in range(plan.groups)]
        lanes = [x[:, LANES:ids] for x in split]
        if plan.groups < 3:
            lanes.append(jnp.zeros((part, extra * (3 - plan.groups)), F32))
        lanes += [x[:, ids : ids + SUBS] for x in split]
        lanes.append(jnp.zeros((part, SUBS * (4 - plan.groups)), F32))
        message[room:, :] = jnp.concatenate(lanes, axis=1).astype(BF16)


def basis_kernel(plan, shocks_hbm, start_hbm, loading_hbm, out_ref, *refs):
    shocks_ref, start_ref, loading_ref, wide_ref, sems = refs
    copies = fetch(
        [loading_hbm, start_hbm, shocks_hbm], [loading_ref, start_ref, shocks_ref], sems
    )
    tenors = loading_ref.shape[0]
    dates = plan.dates
    copies[0].wait()
    copies[1].wait()
    loading_t = jnp.transpose(loading_ref[...])
    drift = 0.5 * STEP * jnp.sum(loading_t * loading_t, axis=1, keepdims=True)
    diag = iota((tenors, tenors), 0) == iota((tenors, tenors), 1)
    log_start = jnp.log(jnp.sum(jnp.where(diag, start_ref[...], 0.0), axis=1, keepdims=True))
    loads = jnp.concatenate(split_bf16((STEP**0.5) * loading_t, 3), axis=1)
    lower = mask_bf16(iota((tenors, tenors), 1) <= iota((tenors, tenors), 0))
    lower = jnp.concatenate([lower, lower], axis=1)
    log_fwd = jnp.broadcast_to(log_start, (tenors, LANES))
    drift = jnp.broadcast_to(drift, (tenors, LANES))
    head = LANES - tenors
    copies[2].wait()
    wide_ref[...] = shocks_ref[...].astype(F32)
    step = plan.width // LANES
    for c in range(dates // step):
        shock = jnp.concatenate(
            [
                wide_ref[pl.ds(c * step + j, tenors, stride=dates), :].astype(BF16)
                for j in range(step)
            ],
            axis=1,
        )
        change = jnp.dot(
            loads, jnp.concatenate([shock] * 3, axis=0), preferred_element_type=F32
        )
        logs = []
        for j in range(step):
            log_fwd = log_fwd + (change[:, LANES * j : LANES * (j + 1)] - drift)
            logs.append(log_fwd)
        fwd = jnp.exp(jnp.concatenate(logs, axis=1))
        growth = split_bf16(jnp.log(1.0 + STEP * fwd), 2)
        summed = jnp.dot(lower, jnp.concatenate(growth, axis=0), preferred_element_type=F32)
        bond = jnp.exp(-summed)
        cols = slice(c * plan.width, (c + 1) * plan.width)
        out_ref[0:tenors, cols] = (bond * fwd * (1.0 / RATE_UNIT)).astype(BF16)
        bond = bond.astype(BF16)
        out_ref[tenors:LANES, cols] = bond[0:head]
        for g in range(plan.groups):
            out_ref[LANES + plan.extra * g : LANES + plan.extra * (g + 1), cols] = bond[head:]
        used = LANES + plan.extra * plan.groups
        out_ref[used:, cols] = jnp.zeros((2 * LANES - used, plan.width), BF16)


def left_side(plan, in_ref):
    part, extra = plan.part, plan.extra
    rest = in_ref[:, plan.room :, :].reshape(plan.owners * part, LANES)
    lane = iota((1, LANES), 1)
    left = []
    for g in range(plan.groups):
        main = in_ref[:, part * g : part * (g + 1), :].reshape(plan.owners * part, LANES)
        keep = mask_bf16((lane >= extra * g) & (lane < extra * (g + 1)))
        left.append(jnp.concatenate([main, rest * keep], axis=1))
    return jnp.concatenate(left, axis=0), rest


def price(plan, left, basis_ref, val_ref):
    width = plan.step
    for c in range(basis_ref.shape[1] // width):
        cols = slice(c * width, (c + 1) * width)
        under = jnp.dot(left, basis_ref[:, cols], preferred_element_type=F32)
        val_ref[:, cols] = jnp.maximum(under.astype(BF16), 0)


def price_kernel(plan, basis_ref, in_ref, val_ref):
    price(plan, left_side(plan, in_ref)[0], basis_ref, val_ref)


def main_kernel(plan, path_total, me_ref, agr_ref, cpty_ref, lag_ref, weight_ref, basis_ref, *refs):
    *in_refs, out_ref, val_ref = refs
    val_refs = [val_ref]
    if plan.halves == 2:
        val_refs = [in_refs.pop(), val_ref]
    me = me_ref[0]
    part, room, dates = plan.part, plan.room, plan.dates
    cpty_dev = weight_ref.shape[0]

    lane = iota((1, LANES), 1)
    info = []
    for in_ref in in_refs:
        left, rest = left_side(plan, in_ref)
        for g in range(plan.groups):
            first = 3 * plan.extra + SUBS * g
            pick = mask_bf16(iota((SUBS, LANES), 1) == first + iota((SUBS, LANES), 0))
            info.append(lax.dot_general(pick, rest, BOTH_LANES, preferred_element_type=F32))
    info = jnp.concatenate(info, axis=1)
    local = info[2:3].astype(jnp.int32)
    agr = jnp.zeros_like(local)
    for n in range(NS_DEV):
        agr = jnp.where(local == n, agr_ref[n] - me * AG_DEV, agr)
    row = iota((SUBS, plan.trades), 0)
    hot = (row & (AG_DEV - 1)) == agr
    netting = jnp.where(hot, jnp.where(row < AG_DEV, info[0:1], info[1:2]), 0.0).astype(BF16)

    price(plan, left, basis_ref, val_ref)
    size = val_ref.shape[0]
    both = jnp.zeros((SUBS, val_ref.shape[1]), F32)
    for h, values in enumerate(val_refs):
        both = both + jnp.dot(
            netting[:, size * h : size * (h + 1)], values[...], preferred_element_type=F32
        )
    both = both + pltpu.roll(both, AG_DEV, 0)
    owed = [both[:, LANES * t : LANES * (t + 1)] for t in range(dates)]

    member = iota((SUBS, LANES), 0) & (AG_DEV - 1)
    lag = jnp.zeros((SUBS, LANES), jnp.int32)
    cpty = jnp.zeros((SUBS, LANES), jnp.int32)
    for a in range(AG_DEV):
        lag = jnp.where(member == a, lag_ref[a], lag)
        cpty = jnp.where(member == a, cpty_ref[a] - me * cpty_dev, cpty)
    lags = [lag == s for s in range(1, LAG_MAX + 1)]
    weight = jnp.zeros((SUBS, dates), F32)
    for c in range(cpty_dev):
        weight = jnp.where(cpty[:, 0:dates] == c, weight_ref[c : c + 1, :], weight)
    zero = jnp.zeros((SUBS, LANES), F32)
    spent, slopes = zero, []
    for t in range(dates):
        before = zero
        for s in range(1, min(t, LAG_MAX) + 1):
            before = jnp.where(lags[s - 1], owed[t - s], before)
        excess = owed[t] - before
        square = excess * excess + SMOOTH * SMOOTH
        inverse = lax.rsqrt(square)
        due = weight[:, t : t + 1]
        spent = spent + due * (0.5 * (excess + square * inverse))
        slopes.append(due * (0.5 * (1.0 + excess * inverse)))
    grads = []
    for t in range(dates):
        after = zero
        for s in range(1, min(dates - 1 - t, LAG_MAX) + 1):
            after = jnp.where(lags[s - 1], slopes[t + s], after)
        grads.append(((slopes[t] - after) * (1.0 / path_total)).astype(BF16))

    grads = jnp.concatenate(grads, axis=1)
    dots = [
        lax.dot_general(grads, values[...], BOTH_LANES, preferred_element_type=F32)
        for values in val_refs
    ]
    dots = jnp.concatenate(dots, axis=1)
    share = jnp.sum(jnp.where(hot & (row < AG_DEV), dots, 0.0), axis=0, keepdims=True)
    spent = jnp.sum(spent, axis=1, keepdims=True) * (1.0 / path_total)
    mine = (lane - plan.slots == cpty) & (iota((SUBS, LANES), 0) < AG_DEV)
    cva = jnp.sum(jnp.where(mine, spent, 0.0), axis=0, keepdims=True)
    block = lane // part
    parts = plan.slots // part
    count = parts * plan.lines
    lines = jnp.concatenate([share[:, LANES * k : LANES * (k + 1)] for k in range(count)], axis=0)
    moved = [lines if m == 0 else pltpu.roll(lines, part * m, 1) for m in range(plan.per_line)]
    paths = out_ref.shape[0] // plan.owners
    for k in range(plan.lines):
        for s in range(plan.per_line):
            line = cva
            for g in range(parts):
                n = g * plan.lines + k
                line = jnp.where(block == g, moved[(g - s) % plan.per_line][n : n + 1], line)
            for p in range(paths):
                out_ref[(k * plan.per_line + s) * paths + p] = line


def finish_kernel(plan, me_ref, place_ref, notional_ref, in_ref, alloc_ref, cva_ref):
    me = me_ref[0]
    rows = place_ref.shape[1]
    key = place_ref[0:1, :].astype(jnp.int32)
    rank = place_ref[1:2, :].astype(jnp.int32)
    lines = in_ref[...]
    count = lines.shape[0]
    paths = count // plan.owners
    pieces = jnp.concatenate(split_bf16(lines, 3), axis=0)
    row = iota((pieces.shape[0], 1), 0) & (count - 1)
    shift = paths.bit_length() - 1
    half = row & (plan.halves - 1)
    found = jnp.zeros((pieces.shape[0], rows), F32)
    for h in range(plan.halves):
        slot = rank + plan.room * h
        slot = jnp.where(slot >= plan.slots, slot - plan.slots, slot)
        hot = mask_bf16(iota((LANES, rows), 0) == slot)
        found = jnp.where(half == h, jnp.dot(pieces, hot, preferred_element_type=F32), found)
    wanted = lax.shift_right_logical(row, shift) == key
    share = jnp.sum(jnp.where(wanted, found, 0.0), axis=0, keepdims=True)
    alloc_ref[...] = share * in_a_row(notional_ref[...])
    own = lax.shift_right_logical(iota((count, 1), 0), shift) == me
    cva = jnp.sum(jnp.where(own, lines, 0.0), axis=0, keepdims=True)
    cva_ref[...] = cva[:, plan.slots : plan.slots + cva_ref.shape[1]]


def body(
    shocks,
    forward_start,
    loading,
    coefficient,
    notional,
    ns_of_trade,
    agr_of_ns,
    cpty_of_agr,
    margin_lag,
    default_weight,
):
    owners = lax.axis_size("trade")
    path_parts = lax.axis_size("path")
    tenors, dates, path_dev = shocks.shape
    path_total = float(path_dev * path_parts)
    rows = coefficient.shape[0]
    lines = rows // LANES
    plan = Plan(owners, rows, tenors, dates)
    cols = dates * path_dev
    me = lax.axis_index("trade").astype(jnp.int32).reshape(1)
    half = lax.rem(lax.axis_index("path").astype(jnp.int32), plan.halves).reshape(1)
    notional = notional.reshape(lines, LANES)

    place, outgoing = pl.pallas_call(
        functools.partial(pack_kernel, plan),
        out_shape=[
            jax.ShapeDtypeStruct((SUBS, rows), F32),
            jax.ShapeDtypeStruct((owners, plan.height, LANES), BF16),
        ],
        in_specs=[SMEM] * 2 + [HBM] * 3,
        out_specs=[VMEM, VMEM],
        scratch_shapes=[
            pltpu.VMEM((owners * lines, LANES), jnp.int32),
            pltpu.VMEM((2 * tenors, rows), BF16),
            pltpu.VMEM((lines, LANES), F32),
            pltpu.SemaphoreType.DMA((3,)),
        ],
        name="pack",
        cost_estimate=pl.CostEstimate(flops=1 << 32, bytes_accessed=1 << 19, transcendentals=0),
    )(me, half, ns_of_trade.reshape(owners * lines, LANES), coefficient.T, notional)
    incoming = [lax.all_to_all(outgoing, "trade", split_axis=0, concat_axis=0, tiled=True)]
    basis = pl.pallas_call(
        functools.partial(basis_kernel, plan),
        out_shape=jax.ShapeDtypeStruct((2 * LANES, cols), BF16),
        in_specs=[HBM] * 3,
        out_specs=VMEM,
        scratch_shapes=[
            pltpu.VMEM((tenors * dates, path_dev), BF16),
            pltpu.VMEM((1, tenors), F32),
            pltpu.VMEM((tenors, tenors), F32),
            pltpu.VMEM((tenors * dates, path_dev), F32),
            pltpu.SemaphoreType.DMA((3,)),
        ],
        name="basis",
        compiler_params=pltpu.CompilerParams(vmem_limit_bytes=16 << 20),
        cost_estimate=pl.CostEstimate(
            flops=2 * 400 * tenors * cols, bytes_accessed=4 << 20, transcendentals=3 * tenors * cols
        ),
    )(shocks.reshape(tenors * dates, path_dev), forward_start.reshape(1, tenors), loading)

    half_trades = plan.trades // plan.halves
    if plan.halves == 2:
        incoming[0], basis = lax.optimization_barrier((incoming[0], basis))
        pairs = [(p, p ^ 1) for p in range(path_parts)]
        incoming.append(lax.ppermute(incoming[0], "path", pairs))
        incoming.append(
            pl.pallas_call(
                functools.partial(price_kernel, plan),
                out_shape=jax.ShapeDtypeStruct((half_trades, cols), BF16),
                in_specs=[VMEM] * 2,
                out_specs=VMEM,
                name="price_own_half",
                compiler_params=pltpu.CompilerParams(vmem_limit_bytes=24 << 20),
                cost_estimate=pl.CostEstimate(
                    flops=4 * half_trades * LANES * cols, bytes_accessed=6 << 20, transcendentals=0
                ),
            )(basis, incoming[0])
        )

    need = 2 * plan.trades * cols + 8 * plan.trades * plan.step + (8 << 20)
    lines_out = pl.pallas_call(
        functools.partial(main_kernel, plan, path_total),
        out_shape=jax.ShapeDtypeStruct((owners * path_parts, 1, LANES), F32),
        in_specs=[SMEM] * 4 + [VMEM] * (2 + len(incoming)),
        out_specs=VMEM,
        scratch_shapes=[pltpu.VMEM((half_trades, cols), BF16)],
        name="value_and_allocate",
        compiler_params=pltpu.CompilerParams(vmem_limit_bytes=need),
    )(me, agr_of_ns, cpty_of_agr, margin_lag, default_weight, basis, *incoming)

    lines_in = lax.all_to_all(lines_out, ("trade", "path"), split_axis=0, concat_axis=0, tiled=True)
    lines_in = lines_in.reshape(owners * path_parts, LANES)
    allocation, cva = pl.pallas_call(
        functools.partial(finish_kernel, plan),
        out_shape=[
            jax.ShapeDtypeStruct((1, rows), F32),
            jax.ShapeDtypeStruct((1, default_weight.shape[0]), F32),
        ],
        in_specs=[SMEM] + [VMEM] * 3,
        out_specs=[VMEM, VMEM],
        name="finish",
        compiler_params=pltpu.CompilerParams(vmem_limit_bytes=32 << 20),
    )(me, place, notional, lines_in)
    return (allocation.reshape(rows), cva.reshape(default_weight.shape[0]))


def solution(mesh):
    placed = (
        P(None, None, "path"),
        P(),
        P(),
        P("trade", None),
        P("trade"),
        P(),
        P("trade"),
        P("trade"),
        P("trade"),
        P("trade", None),
    )
    return jax.shard_map(
        body, mesh=mesh, in_specs=placed, out_specs=(P("trade"), P("trade")), check_vma=False
    )
```

```python
import functools

import jax
import jax.numpy as jnp
from jax import lax
from jax.experimental import pallas as pl
from jax.experimental.pallas import tpu as pltpu
from jax.sharding import PartitionSpec as P

NS_DEV = 8
AG_DEV = 4
LAG_MAX = 4
LANES = 128
SUBS = 8

RATE_UNIT = 0.03
STEP = 0.25
SMOOTH = 0.5

F32 = jnp.float32
BF16 = jnp.bfloat16
VMEM = pl.BlockSpec(memory_space=pltpu.VMEM)
SMEM = pl.BlockSpec(memory_space=pltpu.SMEM)
HBM = pl.BlockSpec(memory_space=pltpu.HBM)
BOTH_LANES = (((1,), (1,)), ((), ()))


def iota(shape, dim):
    return lax.broadcasted_iota(jnp.int32, shape, dim)


def mask_bf16(mask):
    return mask.astype(F32).astype(BF16)


def split_bf16(x, parts):
    pieces = []
    for _ in range(parts):
        piece = x.astype(BF16)
        pieces.append(piece)
        x = x - piece.astype(F32)
    return pieces


def fetch(sources, targets, sems):
    copies = [pltpu.make_async_copy(a, b, sems.at[n]) for n, (a, b) in enumerate(zip(sources, targets))]
    for copy in copies:
        copy.start()
    return copies


def in_a_row(x):
    return jnp.concatenate([x[r : r + 1] for r in range(x.shape[0])], axis=1)


class Plan:
    def __init__(self, owners, rows, tenors, dates):
        most = 3 * rows // (2 * owners)
        self.owners = owners
        self.halves = 2 if most % 96 == 0 else 1
        most = most // self.halves
        self.groups = 3 if most % 48 == 0 else 1
        self.part = -(-most // (16 * self.groups)) * 16
        self.room = self.groups * self.part
        self.height = self.room + self.part
        self.extra = 2 * tenors - LANES
        self.per_line = LANES // self.part
        self.lines = owners * self.part // LANES
        self.slots = self.halves * self.room
        self.trades = owners * self.slots
        self.dates = dates
        self.width = 1024
        self.step = 2048 if self.trades <= 1024 else 512


def pack_kernel(plan, me_ref, half_ref, sets_ref, coef_ref, notional_ref, place_ref, out_ref):
    me = me_ref[0]
    owners, part, room, extra = plan.owners, plan.part, plan.room, plan.extra
    lines = notional_ref.shape[0]
    rows = lines * LANES
    shared = SUBS // lines
    block = sets_ref[pl.ds(pl.multiple_of(me // shared * SUBS, SUBS), SUBS), :]
    own = block[0:lines]
    for b in range(1, shared):
        own = jnp.where(lax.rem(me, shared) == b, block[b * lines : (b + 1) * lines], own)
    sets = in_a_row(own)
    key = lax.shift_right_logical(sets, 3)
    local = sets - key * NS_DEV
    hot = iota((owners, rows), 0) == key
    before = mask_bf16(iota((rows, rows), 0) < iota((rows, rows), 1))
    count = jnp.dot(mask_bf16(hot), before, preferred_element_type=F32)
    rank = jnp.sum(jnp.where(hot, count, 0.0), axis=0, keepdims=True)
    place_ref[...] = jnp.concatenate(
        [key.astype(F32), rank, jnp.zeros((SUBS - 2, rows), F32)], axis=0
    )
    mine = rank.astype(jnp.int32) - room * half_ref[0]
    spot = jnp.where((mine >= 0) & (mine < room), key * room + mine, -1)
    chosen = mask_bf16(iota((owners * room, rows), 0) == spot)
    notional = in_a_row(notional_ref[...])
    high = notional.astype(BF16).astype(F32)
    info = jnp.concatenate(
        [high, notional - high, local.astype(F32), jnp.zeros((13, rows), F32)], axis=0
    )
    table = jnp.concatenate([coef_ref[...], info.astype(BF16)], axis=0)
    moved = lax.dot_general(chosen, table, BOTH_LANES, preferred_element_type=F32)
    ids = LANES + extra
    for d in range(owners):
        message = out_ref.at[d]
        block = moved[d * room : (d + 1) * room]
        message[0:room, :] = block[:, 0:LANES].astype(BF16)
        split = [block[part * g : part * (g + 1)] for g in range(plan.groups)]
        lanes = [x[:, LANES:ids] for x in split]
        if plan.groups < 3:
            lanes.append(jnp.zeros((part, extra * (3 - plan.groups)), F32))
        lanes += [x[:, ids : ids + SUBS] for x in split]
        lanes.append(jnp.zeros((part, SUBS * (4 - plan.groups)), F32))
        message[room:, :] = jnp.concatenate(lanes, axis=1).astype(BF16)


def basis_kernel(plan, shocks_hbm, start_hbm, loading_hbm, out_ref, *refs):
    shocks_ref, start_ref, loading_ref, wide_ref, sems = refs
    copies = fetch(
        [loading_hbm, start_hbm, shocks_hbm], [loading_ref, start_ref, shocks_ref], sems
    )
    tenors = loading_ref.shape[0]
    dates = plan.dates
    copies[0].wait()
    copies[1].wait()
    loading_t = jnp.transpose(loading_ref[...])
    drift = 0.5 * STEP * jnp.sum(loading_t * loading_t, axis=1, keepdims=True)
    diag = iota((tenors, tenors), 0) == iota((tenors, tenors), 1)
    log_start = jnp.log(jnp.sum(jnp.where(diag, start_ref[...], 0.0), axis=1, keepdims=True))
    loads = jnp.concatenate(split_bf16((STEP**0.5) * loading_t, 3), axis=1)
    lower = mask_bf16(iota((tenors, tenors), 1) <= iota((tenors, tenors), 0))
    lower = jnp.concatenate([lower, lower], axis=1)
    log_fwd = jnp.broadcast_to(log_start, (tenors, LANES))
    drift = jnp.broadcast_to(drift, (tenors, LANES))
    head = LANES - tenors
    copies[2].wait()
    wide_ref[...] = shocks_ref[...].astype(F32)
    step = plan.width // LANES
    for c in range(dates // step):
        shock = jnp.concatenate(
            [
                wide_ref[pl.ds(c * step + j, tenors, stride=dates), :].astype(BF16)
                for j in range(step)
            ],
            axis=1,
        )
        change = jnp.dot(
            loads, jnp.concatenate([shock] * 3, axis=0), preferred_element_type=F32
        )
        logs = []
        for j in range(step):
            log_fwd = log_fwd + (change[:, LANES * j : LANES * (j + 1)] - drift)
            logs.append(log_fwd)
        fwd = jnp.exp(jnp.concatenate(logs, axis=1))
        growth = split_bf16(jnp.log(1.0 + STEP * fwd), 2)
        summed = jnp.dot(lower, jnp.concatenate(growth, axis=0), preferred_element_type=F32)
        bond = jnp.exp(-summed)
        cols = slice(c * plan.width, (c + 1) * plan.width)
        out_ref[0:tenors, cols] = (bond * fwd * (1.0 / RATE_UNIT)).astype(BF16)
        bond = bond.astype(BF16)
        out_ref[tenors:LANES, cols] = bond[0:head]
        for g in range(plan.groups):
            out_ref[LANES + plan.extra * g : LANES + plan.extra * (g + 1), cols] = bond[head:]
        used = LANES + plan.extra * plan.groups
        out_ref[used:, cols] = jnp.zeros((2 * LANES - used, plan.width), BF16)


def left_side(plan, in_ref):
    part, extra = plan.part, plan.extra
    rest = in_ref[:, plan.room :, :].reshape(plan.owners * part, LANES)
    lane = iota((1, LANES), 1)
    left = []
    for g in range(plan.groups):
        main = in_ref[:, part * g : part * (g + 1), :].reshape(plan.owners * part, LANES)
        keep = mask_bf16((lane >= extra * g) & (lane < extra * (g + 1)))
        left.append(jnp.concatenate([main, rest * keep], axis=1))
    return jnp.concatenate(left, axis=0), rest


def price(plan, left, basis_ref, val_ref):
    width = plan.step
    for c in range(basis_ref.shape[1] // width):
        cols = slice(c * width, (c + 1) * width)
        under = jnp.dot(left, basis_ref[:, cols], preferred_element_type=F32)
        val_ref[:, cols] = jnp.maximum(under.astype(BF16), 0)


def price_kernel(plan, basis_ref, in_ref, val_ref):
    price(plan, left_side(plan, in_ref)[0], basis_ref, val_ref)


def main_kernel(plan, path_total, me_ref, agr_ref, cpty_ref, lag_ref, weight_ref, basis_ref, *refs):
    *in_refs, out_ref, val_ref = refs
    val_refs = [val_ref]
    if plan.halves == 2:
        val_refs = [in_refs.pop(), val_ref]
    me = me_ref[0]
    part, room, dates = plan.part, plan.room, plan.dates
    cpty_dev = weight_ref.shape[0]

    lane = iota((1, LANES), 1)
    info = []
    for in_ref in in_refs:
        left, rest = left_side(plan, in_ref)
        for g in range(plan.groups):
            first = 3 * plan.extra + SUBS * g
            pick = mask_bf16(iota((SUBS, LANES), 1) == first + iota((SUBS, LANES), 0))
            info.append(lax.dot_general(pick, rest, BOTH_LANES, preferred_element_type=F32))
    info = jnp.concatenate(info, axis=1)
    local = info[2:3].astype(jnp.int32)
    agr = jnp.zeros_like(local)
    for n in range(NS_DEV):
        agr = jnp.where(local == n, agr_ref[n] - me * AG_DEV, agr)
    row = iota((SUBS, plan.trades), 0)
    hot = (row & (AG_DEV - 1)) == agr
    netting = jnp.where(hot, jnp.where(row < AG_DEV, info[0:1], info[1:2]), 0.0).astype(BF16)

    price(plan, left, basis_ref, val_ref)
    values = jnp.concatenate([ref[...] for ref in val_refs], axis=0)
    both = jnp.dot(netting, values, preferred_element_type=F32)
    both = both + pltpu.roll(both, AG_DEV, 0)
    owed = [both[:, LANES * t : LANES * (t + 1)] for t in range(dates)]

    member = iota((SUBS, LANES), 0) & (AG_DEV - 1)
    lag = jnp.zeros((SUBS, LANES), jnp.int32)
    cpty = jnp.zeros((SUBS, LANES), jnp.int32)
    for a in range(AG_DEV):
        lag = jnp.where(member == a, lag_ref[a], lag)
        cpty = jnp.where(member == a, cpty_ref[a] - me * cpty_dev, cpty)
    lags = [lag == s for s in range(1, LAG_MAX + 1)]
    weight = jnp.zeros((SUBS, dates), F32)
    for c in range(cpty_dev):
        weight = jnp.where(cpty[:, 0:dates] == c, weight_ref[c : c + 1, :], weight)
    zero = jnp.zeros((SUBS, LANES), F32)
    spent, slopes = zero, []
    for t in range(dates):
        before = zero
        for s in range(1, min(t, LAG_MAX) + 1):
            before = jnp.where(lags[s - 1], owed[t - s], before)
        excess = owed[t] - before
        square = excess * excess + SMOOTH * SMOOTH
        inverse = lax.rsqrt(square)
        due = weight[:, t : t + 1]
        spent = spent + due * (0.5 * (excess + square * inverse))
        slopes.append(due * (0.5 * (1.0 + excess * inverse)))
    grads = []
    for t in range(dates):
        after = zero
        for s in range(1, min(dates - 1 - t, LAG_MAX) + 1):
            after = jnp.where(lags[s - 1], slopes[t + s], after)
        grads.append(((slopes[t] - after) * (1.0 / path_total)).astype(BF16))

    grads = jnp.concatenate(grads, axis=1)
    values = jnp.concatenate([ref[...] for ref in val_refs], axis=0)
    dots = lax.dot_general(grads, values, BOTH_LANES, preferred_element_type=F32)
    share = jnp.sum(jnp.where(hot & (row < AG_DEV), dots, 0.0), axis=0, keepdims=True)
    spent = jnp.sum(spent, axis=1, keepdims=True) * (1.0 / path_total)
    mine = (lane - plan.slots == cpty) & (iota((SUBS, LANES), 0) < AG_DEV)
    cva = jnp.sum(jnp.where(mine, spent, 0.0), axis=0, keepdims=True)
    block = lane // part
    parts = plan.slots // part
    count = parts * plan.lines
    lines = jnp.concatenate([share[:, LANES * k : LANES * (k + 1)] for k in range(count)], axis=0)
    moved = [lines if m == 0 else pltpu.roll(lines, part * m, 1) for m in range(plan.per_line)]
    paths = out_ref.shape[0] // plan.owners
    for k in range(plan.lines):
        for s in range(plan.per_line):
            line = cva
            for g in range(parts):
                n = g * plan.lines + k
                line = jnp.where(block == g, moved[(g - s) % plan.per_line][n : n + 1], line)
            for p in range(paths):
                out_ref[(k * plan.per_line + s) * paths + p] = line


def finish_kernel(plan, me_ref, place_ref, notional_ref, in_ref, alloc_ref, cva_ref):
    me = me_ref[0]
    rows = place_ref.shape[1]
    key = place_ref[0:1, :].astype(jnp.int32)
    rank = place_ref[1:2, :].astype(jnp.int32)
    lines = in_ref[...]
    count = lines.shape[0]
    paths = count // plan.owners
    pieces = jnp.concatenate(split_bf16(lines, 3), axis=0)
    row = iota((pieces.shape[0], 1), 0) & (count - 1)
    shift = paths.bit_length() - 1
    half = row & (plan.halves - 1)
    found = jnp.zeros((pieces.shape[0], rows), F32)
    for h in range(plan.halves):
        slot = rank + plan.room * h
        slot = jnp.where(slot >= plan.slots, slot - plan.slots, slot)
        hot = mask_bf16(iota((LANES, rows), 0) == slot)
        found = jnp.where(half == h, jnp.dot(pieces, hot, preferred_element_type=F32), found)
    wanted = lax.shift_right_logical(row, shift) == key
    share = jnp.sum(jnp.where(wanted, found, 0.0), axis=0, keepdims=True)
    alloc_ref[...] = share * in_a_row(notional_ref[...])
    own = lax.shift_right_logical(iota((count, 1), 0), shift) == me
    cva = jnp.sum(jnp.where(own, lines, 0.0), axis=0, keepdims=True)
    cva_ref[...] = cva[:, plan.slots : plan.slots + cva_ref.shape[1]]


def body(
    shocks,
    forward_start,
    loading,
    coefficient,
    notional,
    ns_of_trade,
    agr_of_ns,
    cpty_of_agr,
    margin_lag,
    default_weight,
):
    owners = lax.axis_size("trade")
    path_parts = lax.axis_size("path")
    tenors, dates, path_dev = shocks.shape
    path_total = float(path_dev * path_parts)
    rows = coefficient.shape[0]
    lines = rows // LANES
    plan = Plan(owners, rows, tenors, dates)
    cols = dates * path_dev
    me = lax.axis_index("trade").astype(jnp.int32).reshape(1)
    half = lax.rem(lax.axis_index("path").astype(jnp.int32), plan.halves).reshape(1)
    notional = notional.reshape(lines, LANES)

    place, outgoing = pl.pallas_call(
        functools.partial(pack_kernel, plan),
        out_shape=[
            jax.ShapeDtypeStruct((SUBS, rows), F32),
            jax.ShapeDtypeStruct((owners, plan.height, LANES), BF16),
        ],
        in_specs=[SMEM] * 2 + [VMEM] * 3,
        out_specs=[VMEM, VMEM],
        name="pack",
        cost_estimate=pl.CostEstimate(flops=1 << 32, bytes_accessed=1 << 19, transcendentals=0),
    )(me, half, ns_of_trade.reshape(owners * lines, LANES), coefficient.T, notional)
    incoming = [lax.all_to_all(outgoing, "trade", split_axis=0, concat_axis=0, tiled=True)]
    basis = pl.pallas_call(
        functools.partial(basis_kernel, plan),
        out_shape=jax.ShapeDtypeStruct((2 * LANES, cols), BF16),
        in_specs=[HBM] * 3,
        out_specs=VMEM,
        scratch_shapes=[
            pltpu.VMEM((tenors * dates, path_dev), BF16),
            pltpu.VMEM((1, tenors), F32),
            pltpu.VMEM((tenors, tenors), F32),
            pltpu.VMEM((tenors * dates, path_dev), F32),
            pltpu.SemaphoreType.DMA((3,)),
        ],
        name="basis",
        compiler_params=pltpu.CompilerParams(vmem_limit_bytes=16 << 20),
        cost_estimate=pl.CostEstimate(
            flops=2 * 400 * tenors * cols, bytes_accessed=4 << 20, transcendentals=3 * tenors * cols
        ),
    )(shocks.reshape(tenors * dates, path_dev), forward_start.reshape(1, tenors), loading)

    half_trades = plan.trades // plan.halves
    if plan.halves == 2:
        incoming[0], basis = lax.optimization_barrier((incoming[0], basis))
        pairs = [(p, p ^ 1) for p in range(path_parts)]
        incoming.append(lax.ppermute(incoming[0], "path", pairs))
        incoming.append(
            pl.pallas_call(
                functools.partial(price_kernel, plan),
                out_shape=jax.ShapeDtypeStruct((half_trades, cols), BF16),
                in_specs=[VMEM] * 2,
                out_specs=VMEM,
                name="price_own_half",
                compiler_params=pltpu.CompilerParams(vmem_limit_bytes=24 << 20),
                cost_estimate=pl.CostEstimate(
                    flops=4 * half_trades * LANES * cols, bytes_accessed=6 << 20, transcendentals=0
                ),
            )(basis, incoming[0])
        )

    need = 2 * plan.trades * cols + 8 * plan.trades * plan.step + (8 << 20)
    lines_out = pl.pallas_call(
        functools.partial(main_kernel, plan, path_total),
        out_shape=jax.ShapeDtypeStruct((owners * path_parts, 1, LANES), F32),
        in_specs=[SMEM] * 4 + [VMEM] * (2 + len(incoming)),
        out_specs=VMEM,
        scratch_shapes=[pltpu.VMEM((half_trades, cols), BF16)],
        name="value_and_allocate",
        compiler_params=pltpu.CompilerParams(vmem_limit_bytes=need),
    )(me, agr_of_ns, cpty_of_agr, margin_lag, default_weight, basis, *incoming)

    lines_in = lax.all_to_all(lines_out, ("trade", "path"), split_axis=0, concat_axis=0, tiled=True)
    lines_in = lines_in.reshape(owners * path_parts, LANES)
    allocation, cva = pl.pallas_call(
        functools.partial(finish_kernel, plan),
        out_shape=[
            jax.ShapeDtypeStruct((1, rows), F32),
            jax.ShapeDtypeStruct((1, default_weight.shape[0]), F32),
        ],
        in_specs=[SMEM] + [VMEM] * 3,
        out_specs=[VMEM, VMEM],
        name="finish",
        compiler_params=pltpu.CompilerParams(vmem_limit_bytes=32 << 20),
    )(me, place, notional, lines_in)
    return (allocation.reshape(rows), cva.reshape(default_weight.shape[0]))


def solution(mesh):
    placed = (
        P(None, None, "path"),
        P(),
        P(),
        P("trade", None),
        P("trade"),
        P(),
        P("trade"),
        P("trade"),
        P("trade"),
        P("trade", None),
    )
    return jax.shard_map(
        body, mesh=mesh, in_specs=placed, out_specs=(P("trade"), P("trade")), check_vma=False
    )
```

```python
import functools

import jax
import jax.numpy as jnp
from jax import lax
from jax.experimental import pallas as pl
from jax.experimental.pallas import tpu as pltpu
from jax.sharding import PartitionSpec as P

NS_DEV = 8
AG_DEV = 4
LAG_MAX = 4
LANES = 128
SUBS = 8

RATE_UNIT = 0.03
STEP = 0.25
SMOOTH = 0.5

F32 = jnp.float32
BF16 = jnp.bfloat16
VMEM = pl.BlockSpec(memory_space=pltpu.VMEM)
SMEM = pl.BlockSpec(memory_space=pltpu.SMEM)
HBM = pl.BlockSpec(memory_space=pltpu.HBM)
BOTH_LANES = (((1,), (1,)), ((), ()))


def iota(shape, dim):
    return lax.broadcasted_iota(jnp.int32, shape, dim)


def mask_bf16(mask):
    return mask.astype(F32).astype(BF16)


def split_bf16(x, parts):
    pieces = []
    for _ in range(parts):
        piece = x.astype(BF16)
        pieces.append(piece)
        x = x - piece.astype(F32)
    return pieces


def fetch(sources, targets, sems):
    copies = [pltpu.make_async_copy(a, b, sems.at[n]) for n, (a, b) in enumerate(zip(sources, targets))]
    for copy in copies:
        copy.start()
    return copies


def in_a_row(x):
    return jnp.concatenate([x[r : r + 1] for r in range(x.shape[0])], axis=1)


class Plan:
    def __init__(self, owners, rows, tenors, dates):
        most = 3 * rows // (2 * owners)
        self.owners = owners
        self.halves = 2 if most % 96 == 0 else 1
        most = most // self.halves
        self.groups = 3 if most % 48 == 0 else 1
        self.part = -(-most // (16 * self.groups)) * 16
        self.room = self.groups * self.part
        self.height = self.room + self.part
        self.extra = 2 * tenors - LANES
        self.per_line = LANES // self.part
        self.lines = owners * self.part // LANES
        self.slots = self.halves * self.room
        self.trades = owners * self.slots
        self.dates = dates
        self.width = 1024
        self.step = 2048 if self.trades <= 1024 else 512


def pack_kernel(plan, me_ref, half_ref, sets_hbm, coef_hbm, notional_hbm, place_ref, out_ref, *refs):
    sets_ref, coef_ref, notional_ref, sems = refs
    copies = fetch(
        [sets_hbm, notional_hbm, coef_hbm], [sets_ref, notional_ref, coef_ref], sems
    )
    me = me_ref[0]
    owners, part, room, extra = plan.owners, plan.part, plan.room, plan.extra
    lines = notional_ref.shape[0]
    rows = lines * LANES
    shared = SUBS // lines
    copies[0].wait()
    block = sets_ref[pl.ds(pl.multiple_of(me // shared * SUBS, SUBS), SUBS), :]
    own = block[0:lines]
    for b in range(1, shared):
        own = jnp.where(lax.rem(me, shared) == b, block[b * lines : (b + 1) * lines], own)
    sets = in_a_row(own)
    key = lax.shift_right_logical(sets, 3)
    local = sets - key * NS_DEV
    hot = iota((owners, rows), 0) == key
    before = mask_bf16(iota((rows, rows), 0) < iota((rows, rows), 1))
    count = jnp.dot(mask_bf16(hot), before, preferred_element_type=F32)
    rank = jnp.sum(jnp.where(hot, count, 0.0), axis=0, keepdims=True)
    place_ref[...] = jnp.concatenate(
        [key.astype(F32), rank, jnp.zeros((SUBS - 2, rows), F32)], axis=0
    )
    mine = rank.astype(jnp.int32) - room * half_ref[0]
    spot = jnp.where((mine >= 0) & (mine < room), key * room + mine, -1)
    chosen = mask_bf16(iota((owners * room, rows), 0) == spot)
    copies[1].wait()
    notional = in_a_row(notional_ref[...])
    high = notional.astype(BF16).astype(F32)
    info = jnp.concatenate(
        [high, notional - high, local.astype(F32), jnp.zeros((13, rows), F32)], axis=0
    )
    copies[2].wait()
    table = jnp.concatenate([coef_ref[...], info.astype(BF16)], axis=0)
    moved = lax.dot_general(chosen, table, BOTH_LANES, preferred_element_type=F32)
    ids = LANES + extra
    for d in range(owners):
        message = out_ref.at[d]
        block = moved[d * room : (d + 1) * room]
        message[0:room, :] = block[:, 0:LANES].astype(BF16)
        split = [block[part * g : part * (g + 1)] for g in range(plan.groups)]
        lanes = [x[:, LANES:ids] for x in split]
        if plan.groups < 3:
            lanes.append(jnp.zeros((part, extra * (3 - plan.groups)), F32))
        lanes += [x[:, ids : ids + SUBS] for x in split]
        lanes.append(jnp.zeros((part, SUBS * (4 - plan.groups)), F32))
        message[room:, :] = jnp.concatenate(lanes, axis=1).astype(BF16)


def basis_kernel(plan, shocks_hbm, start_hbm, loading_hbm, out_ref, *refs):
    shocks_ref, start_ref, loading_ref, wide_ref, sems = refs
    copies = fetch(
        [loading_hbm, start_hbm, shocks_hbm], [loading_ref, start_ref, shocks_ref], sems
    )
    tenors = loading_ref.shape[0]
    dates = plan.dates
    copies[0].wait()
    copies[1].wait()
    loading_t = jnp.transpose(loading_ref[...])
    drift = 0.5 * STEP * jnp.sum(loading_t * loading_t, axis=1, keepdims=True)
    diag = iota((tenors, tenors), 0) == iota((tenors, tenors), 1)
    log_start = jnp.log(jnp.sum(jnp.where(diag, start_ref[...], 0.0), axis=1, keepdims=True))
    loads = jnp.concatenate(split_bf16((STEP**0.5) * loading_t, 3), axis=1)
    lower = mask_bf16(iota((tenors, tenors), 1) <= iota((tenors, tenors), 0))
    lower = jnp.concatenate([lower, lower], axis=1)
    log_fwd = jnp.broadcast_to(log_start, (tenors, LANES))
    drift = jnp.broadcast_to(drift, (tenors, LANES))
    head = LANES - tenors
    copies[2].wait()
    wide_ref[...] = shocks_ref[...].astype(F32)
    step = plan.width // LANES
    for c in range(dates // step):
        shock = jnp.concatenate(
            [
                wide_ref[pl.ds(c * step + j, tenors, stride=dates), :].astype(BF16)
                for j in range(step)
            ],
            axis=1,
        )
        change = jnp.dot(
            loads, jnp.concatenate([shock] * 3, axis=0), preferred_element_type=F32
        )
        logs = []
        for j in range(step):
            log_fwd = log_fwd + (change[:, LANES * j : LANES * (j + 1)] - drift)
            logs.append(log_fwd)
        fwd = jnp.exp(jnp.concatenate(logs, axis=1))
        growth = split_bf16(jnp.log(1.0 + STEP * fwd), 2)
        summed = jnp.dot(lower, jnp.concatenate(growth, axis=0), preferred_element_type=F32)
        bond = jnp.exp(-summed)
        cols = slice(c * plan.width, (c + 1) * plan.width)
        out_ref[0:tenors, cols] = (bond * fwd * (1.0 / RATE_UNIT)).astype(BF16)
        bond = bond.astype(BF16)
        out_ref[tenors:LANES, cols] = bond[0:head]
        for g in range(plan.groups):
            out_ref[LANES + plan.extra * g : LANES + plan.extra * (g + 1), cols] = bond[head:]
        used = LANES + plan.extra * plan.groups
        out_ref[used:, cols] = jnp.zeros((2 * LANES - used, plan.width), BF16)


def left_side(plan, in_ref):
    part, extra = plan.part, plan.extra
    rest = in_ref[:, plan.room :, :].reshape(plan.owners * part, LANES)
    lane = iota((1, LANES), 1)
    left = []
    for g in range(plan.groups):
        main = in_ref[:, part * g : part * (g + 1), :].reshape(plan.owners * part, LANES)
        keep = mask_bf16((lane >= extra * g) & (lane < extra * (g + 1)))
        left.append(jnp.concatenate([main, rest * keep], axis=1))
    return jnp.concatenate(left, axis=0), rest


def price(plan, left, basis_ref, val_ref):
    width = plan.step
    for c in range(basis_ref.shape[1] // width):
        cols = slice(c * width, (c + 1) * width)
        under = jnp.dot(left, basis_ref[:, cols], preferred_element_type=F32)
        val_ref[:, cols] = jnp.maximum(under.astype(BF16), 0)


def price_kernel(plan, basis_ref, in_ref, val_ref):
    price(plan, left_side(plan, in_ref)[0], basis_ref, val_ref)


def main_kernel(plan, path_total, me_ref, agr_ref, cpty_ref, lag_ref, weight_ref, basis_ref, *refs):
    *in_refs, out_ref, val_ref = refs
    val_refs = [val_ref]
    if plan.halves == 2:
        val_refs = [in_refs.pop(), val_ref]
    me = me_ref[0]
    part, room, dates = plan.part, plan.room, plan.dates
    cpty_dev = weight_ref.shape[0]

    lane = iota((1, LANES), 1)
    info = []
    for in_ref in in_refs:
        left, rest = left_side(plan, in_ref)
        for g in range(plan.groups):
            first = 3 * plan.extra + SUBS * g
            pick = mask_bf16(iota((SUBS, LANES), 1) == first + iota((SUBS, LANES), 0))
            info.append(lax.dot_general(pick, rest, BOTH_LANES, preferred_element_type=F32))
    info = jnp.concatenate(info, axis=1)
    local = info[2:3].astype(jnp.int32)
    agr = jnp.zeros_like(local)
    for n in range(NS_DEV):
        agr = jnp.where(local == n, agr_ref[n] - me * AG_DEV, agr)
    row = iota((SUBS, plan.trades), 0)
    hot = (row & (AG_DEV - 1)) == agr
    netting = jnp.where(hot, jnp.where(row < AG_DEV, info[0:1], info[1:2]), 0.0).astype(BF16)

    price(plan, left, basis_ref, val_ref)
    size, cols = val_ref.shape
    pieces = [slice(c, c + plan.width) for c in range(0, cols, plan.width)]
    both = []
    for piece in pieces:
        sums = [
            jnp.dot(
                netting[:, size * h : size * (h + 1)],
                values[:, piece],
                preferred_element_type=F32,
            )
            for h, values in enumerate(val_refs)
        ]
        both.append(sum(sums[1:], sums[0]))
    both = jnp.concatenate(both, axis=1)
    both = both + pltpu.roll(both, AG_DEV, 0)
    owed = [both[:, LANES * t : LANES * (t + 1)] for t in range(dates)]

    member = iota((SUBS, LANES), 0) & (AG_DEV - 1)
    lag = jnp.zeros((SUBS, LANES), jnp.int32)
    cpty = jnp.zeros((SUBS, LANES), jnp.int32)
    for a in range(AG_DEV):
        lag = jnp.where(member == a, lag_ref[a], lag)
        cpty = jnp.where(member == a, cpty_ref[a] - me * cpty_dev, cpty)
    lags = [lag == s for s in range(1, LAG_MAX + 1)]
    weight = jnp.zeros((SUBS, dates), F32)
    for c in range(cpty_dev):
        weight = jnp.where(cpty[:, 0:dates] == c, weight_ref[c : c + 1, :], weight)
    zero = jnp.zeros((SUBS, LANES), F32)
    spent, slopes = zero, []
    for t in range(dates):
        before = zero
        for s in range(1, min(t, LAG_MAX) + 1):
            before = jnp.where(lags[s - 1], owed[t - s], before)
        excess = owed[t] - before
        square = excess * excess + SMOOTH * SMOOTH
        inverse = lax.rsqrt(square)
        due = weight[:, t : t + 1]
        spent = spent + due * (0.5 * (excess + square * inverse))
        slopes.append(due * (0.5 * (1.0 + excess * inverse)))
    grads = []
    for t in range(dates):
        after = zero
        for s in range(1, min(dates - 1 - t, LAG_MAX) + 1):
            after = jnp.where(lags[s - 1], slopes[t + s], after)
        grads.append(((slopes[t] - after) * (1.0 / path_total)).astype(BF16))

    grads = jnp.concatenate(grads, axis=1)
    dots = []
    for values in val_refs:
        sums = [
            lax.dot_general(
                grads[:, piece], values[:, piece], BOTH_LANES, preferred_element_type=F32
            )
            for piece in pieces
        ]
        dots.append(sum(sums[1:], sums[0]))
    dots = jnp.concatenate(dots, axis=1)
    share = jnp.sum(jnp.where(hot & (row < AG_DEV), dots, 0.0), axis=0, keepdims=True)
    spent = jnp.sum(spent, axis=1, keepdims=True) * (1.0 / path_total)
    mine = (lane - plan.slots == cpty) & (iota((SUBS, LANES), 0) < AG_DEV)
    cva = jnp.sum(jnp.where(mine, spent, 0.0), axis=0, keepdims=True)
    block = lane // part
    parts = plan.slots // part
    count = parts * plan.lines
    lines = jnp.concatenate([share[:, LANES * k : LANES * (k + 1)] for k in range(count)], axis=0)
    moved = [lines if m == 0 else pltpu.roll(lines, part * m, 1) for m in range(plan.per_line)]
    paths = out_ref.shape[0] // plan.owners
    for k in range(plan.lines):
        for s in range(plan.per_line):
            line = cva
            for g in range(parts):
                n = g * plan.lines + k
                line = jnp.where(block == g, moved[(g - s) % plan.per_line][n : n + 1], line)
            for p in range(paths):
                out_ref[(k * plan.per_line + s) * paths + p] = line


def finish_kernel(plan, me_ref, place_ref, notional_ref, in_ref, alloc_ref, cva_ref):
    me = me_ref[0]
    rows = place_ref.shape[1]
    key = place_ref[0:1, :].astype(jnp.int32)
    rank = place_ref[1:2, :].astype(jnp.int32)
    lines = in_ref[...]
    count = lines.shape[0]
    paths = count // plan.owners
    pieces = jnp.concatenate(split_bf16(lines, 3), axis=0)
    row = iota((pieces.shape[0], 1), 0) & (count - 1)
    shift = paths.bit_length() - 1
    half = row & (plan.halves - 1)
    found = jnp.zeros((pieces.shape[0], rows), F32)
    for h in range(plan.halves):
        slot = rank + plan.room * h
        slot = jnp.where(slot >= plan.slots, slot - plan.slots, slot)
        hot = mask_bf16(iota((LANES, rows), 0) == slot)
        found = jnp.where(half == h, jnp.dot(pieces, hot, preferred_element_type=F32), found)
    wanted = lax.shift_right_logical(row, shift) == key
    share = jnp.sum(jnp.where(wanted, found, 0.0), axis=0, keepdims=True)
    alloc_ref[...] = share * in_a_row(notional_ref[...])
    own = lax.shift_right_logical(iota((count, 1), 0), shift) == me
    cva = jnp.sum(jnp.where(own, lines, 0.0), axis=0, keepdims=True)
    cva_ref[...] = cva[:, plan.slots : plan.slots + cva_ref.shape[1]]


def body(
    shocks,
    forward_start,
    loading,
    coefficient,
    notional,
    ns_of_trade,
    agr_of_ns,
    cpty_of_agr,
    margin_lag,
    default_weight,
):
    owners = lax.axis_size("trade")
    path_parts = lax.axis_size("path")
    tenors, dates, path_dev = shocks.shape
    path_total = float(path_dev * path_parts)
    rows = coefficient.shape[0]
    lines = rows // LANES
    plan = Plan(owners, rows, tenors, dates)
    cols = dates * path_dev
    me = lax.axis_index("trade").astype(jnp.int32).reshape(1)
    half = lax.rem(lax.axis_index("path").astype(jnp.int32), plan.halves).reshape(1)
    notional = notional.reshape(lines, LANES)

    place, outgoing = pl.pallas_call(
        functools.partial(pack_kernel, plan),
        out_shape=[
            jax.ShapeDtypeStruct((SUBS, rows), F32),
            jax.ShapeDtypeStruct((owners, plan.height, LANES), BF16),
        ],
        in_specs=[SMEM] * 2 + [HBM] * 3,
        out_specs=[VMEM, VMEM],
        scratch_shapes=[
            pltpu.VMEM((owners * lines, LANES), jnp.int32),
            pltpu.VMEM((2 * tenors, rows), BF16),
            pltpu.VMEM((lines, LANES), F32),
            pltpu.SemaphoreType.DMA((3,)),
        ],
        name="pack",
        cost_estimate=pl.CostEstimate(flops=1 << 32, bytes_accessed=1 << 19, transcendentals=0),
    )(me, half, ns_of_trade.reshape(owners * lines, LANES), coefficient.T, notional)
    incoming = [lax.all_to_all(outgoing, "trade", split_axis=0, concat_axis=0, tiled=True)]
    basis = pl.pallas_call(
        functools.partial(basis_kernel, plan),
        out_shape=jax.ShapeDtypeStruct((2 * LANES, cols), BF16),
        in_specs=[HBM] * 3,
        out_specs=VMEM,
        scratch_shapes=[
            pltpu.VMEM((tenors * dates, path_dev), BF16),
            pltpu.VMEM((1, tenors), F32),
            pltpu.VMEM((tenors, tenors), F32),
            pltpu.VMEM((tenors * dates, path_dev), F32),
            pltpu.SemaphoreType.DMA((3,)),
        ],
        name="basis",
        compiler_params=pltpu.CompilerParams(vmem_limit_bytes=16 << 20),
        cost_estimate=pl.CostEstimate(
            flops=2 * 400 * tenors * cols, bytes_accessed=4 << 20, transcendentals=3 * tenors * cols
        ),
    )(shocks.reshape(tenors * dates, path_dev), forward_start.reshape(1, tenors), loading)

    half_trades = plan.trades // plan.halves
    if plan.halves == 2:
        incoming[0], basis = lax.optimization_barrier((incoming[0], basis))
        pairs = [(p, p ^ 1) for p in range(path_parts)]
        incoming.append(lax.ppermute(incoming[0], "path", pairs))
        incoming.append(
            pl.pallas_call(
                functools.partial(price_kernel, plan),
                out_shape=jax.ShapeDtypeStruct((half_trades, cols), BF16),
                in_specs=[VMEM] * 2,
                out_specs=VMEM,
                name="price_own_half",
                compiler_params=pltpu.CompilerParams(vmem_limit_bytes=24 << 20),
                cost_estimate=pl.CostEstimate(
                    flops=4 * half_trades * LANES * cols, bytes_accessed=6 << 20, transcendentals=0
                ),
            )(basis, incoming[0])
        )

    need = 2 * plan.trades * cols + 8 * plan.trades * plan.step + (8 << 20)
    lines_out = pl.pallas_call(
        functools.partial(main_kernel, plan, path_total),
        out_shape=jax.ShapeDtypeStruct((owners * path_parts, 1, LANES), F32),
        in_specs=[SMEM] * 4 + [VMEM] * (2 + len(incoming)),
        out_specs=VMEM,
        scratch_shapes=[pltpu.VMEM((half_trades, cols), BF16)],
        name="value_and_allocate",
        compiler_params=pltpu.CompilerParams(vmem_limit_bytes=need),
    )(me, agr_of_ns, cpty_of_agr, margin_lag, default_weight, basis, *incoming)

    lines_in = lax.all_to_all(lines_out, ("trade", "path"), split_axis=0, concat_axis=0, tiled=True)
    lines_in = lines_in.reshape(owners * path_parts, LANES)
    allocation, cva = pl.pallas_call(
        functools.partial(finish_kernel, plan),
        out_shape=[
            jax.ShapeDtypeStruct((1, rows), F32),
            jax.ShapeDtypeStruct((1, default_weight.shape[0]), F32),
        ],
        in_specs=[SMEM] + [VMEM] * 3,
        out_specs=[VMEM, VMEM],
        name="finish",
        compiler_params=pltpu.CompilerParams(vmem_limit_bytes=32 << 20),
    )(me, place, notional, lines_in)
    return (allocation.reshape(rows), cva.reshape(default_weight.shape[0]))


def solution(mesh):
    placed = (
        P(None, None, "path"),
        P(),
        P(),
        P("trade", None),
        P("trade"),
        P(),
        P("trade"),
        P("trade"),
        P("trade"),
        P("trade", None),
    )
    return jax.shard_map(
        body, mesh=mesh, in_specs=placed, out_specs=(P("trade"), P("trade")), check_vma=False
    )
```

```python
import functools

import jax
import jax.numpy as jnp
from jax import lax
from jax.experimental import pallas as pl
from jax.experimental.pallas import tpu as pltpu
from jax.sharding import PartitionSpec as P

NS_DEV = 8
AG_DEV = 4
LAG_MAX = 4
LANES = 128
SUBS = 8

RATE_UNIT = 0.03
STEP = 0.25
SMOOTH = 0.5

F32 = jnp.float32
BF16 = jnp.bfloat16
VMEM = pl.BlockSpec(memory_space=pltpu.VMEM)
SMEM = pl.BlockSpec(memory_space=pltpu.SMEM)
HBM = pl.BlockSpec(memory_space=pltpu.HBM)
BOTH_LANES = (((1,), (1,)), ((), ()))


def iota(shape, dim):
    return lax.broadcasted_iota(jnp.int32, shape, dim)


def mask_bf16(mask):
    return mask.astype(F32).astype(BF16)


def split_bf16(x, parts):
    pieces = []
    for _ in range(parts):
        piece = x.astype(BF16)
        pieces.append(piece)
        x = x - piece.astype(F32)
    return pieces


def fetch(sources, targets, sems):
    copies = [pltpu.make_async_copy(a, b, sems.at[n]) for n, (a, b) in enumerate(zip(sources, targets))]
    for copy in copies:
        copy.start()
    return copies


def in_a_row(x):
    return jnp.concatenate([x[r : r + 1] for r in range(x.shape[0])], axis=1)


class Plan:
    def __init__(self, owners, rows, tenors, dates):
        most = 3 * rows // (2 * owners)
        self.owners = owners
        self.halves = 2 if most % 96 == 0 else 1
        most = most // self.halves
        self.groups = 3 if most % 48 == 0 else 1
        self.part = -(-most // (16 * self.groups)) * 16
        self.room = self.groups * self.part
        self.height = self.room + self.part
        self.extra = 2 * tenors - LANES
        self.per_line = LANES // self.part
        self.lines = owners * self.part // LANES
        self.slots = self.halves * self.room
        self.trades = owners * self.slots
        self.dates = dates
        self.width = 1024
        self.step = 2048 if self.trades <= 1024 else 512


def pack_kernel(plan, me_ref, half_ref, sets_hbm, coef_hbm, notional_hbm, place_ref, out_ref, *refs):
    sets_ref, coef_ref, notional_ref, sems = refs
    copies = fetch(
        [sets_hbm, notional_hbm, coef_hbm], [sets_ref, notional_ref, coef_ref], sems
    )
    me = me_ref[0]
    owners, part, room, extra = plan.owners, plan.part, plan.room, plan.extra
    lines = notional_ref.shape[0]
    rows = lines * LANES
    shared = SUBS // lines
    copies[0].wait()
    block = sets_ref[pl.ds(pl.multiple_of(me // shared * SUBS, SUBS), SUBS), :]
    own = block[0:lines]
    for b in range(1, shared):
        own = jnp.where(lax.rem(me, shared) == b, block[b * lines : (b + 1) * lines], own)
    sets = in_a_row(own)
    key = lax.shift_right_logical(sets, 3)
    local = sets - key * NS_DEV
    hot = iota((owners, rows), 0) == key
    before = mask_bf16(iota((rows, rows), 0) < iota((rows, rows), 1))
    count = jnp.dot(mask_bf16(hot), before, preferred_element_type=F32)
    rank = jnp.sum(jnp.where(hot, count, 0.0), axis=0, keepdims=True)
    place_ref[...] = jnp.concatenate(
        [key.astype(F32), rank, jnp.zeros((SUBS - 2, rows), F32)], axis=0
    )
    mine = rank.astype(jnp.int32) - room * half_ref[0]
    spot = jnp.where((mine >= 0) & (mine < room), key * room + mine, -1)
    chosen = mask_bf16(iota((owners * room, rows), 0) == spot)
    copies[1].wait()
    notional = in_a_row(notional_ref[...])
    high = notional.astype(BF16).astype(F32)
    info = jnp.concatenate(
        [high, notional - high, local.astype(F32), jnp.zeros((13, rows), F32)], axis=0
    )
    copies[2].wait()
    table = jnp.concatenate([coef_ref[...], info.astype(BF16)], axis=0)
    moved = lax.dot_general(chosen, table, BOTH_LANES, preferred_element_type=F32)
    ids = LANES + extra
    for d in range(owners):
        message = out_ref.at[d]
        block = moved[d * room : (d + 1) * room]
        message[0:room, :] = block[:, 0:LANES].astype(BF16)
        split = [block[part * g : part * (g + 1)] for g in range(plan.groups)]
        lanes = [x[:, LANES:ids] for x in split]
        if plan.groups < 3:
            lanes.append(jnp.zeros((part, extra * (3 - plan.groups)), F32))
        lanes += [x[:, ids : ids + SUBS] for x in split]
        lanes.append(jnp.zeros((part, SUBS * (4 - plan.groups)), F32))
        message[room:, :] = jnp.concatenate(lanes, axis=1).astype(BF16)


def basis_kernel(plan, shocks_hbm, start_hbm, loading_hbm, out_ref, *refs):
    shocks_ref, start_ref, loading_ref, wide_ref, sems = refs
    copies = fetch(
        [loading_hbm, start_hbm, shocks_hbm], [loading_ref, start_ref, shocks_ref], sems
    )
    tenors = loading_ref.shape[0]
    dates = plan.dates
    copies[0].wait()
    copies[1].wait()
    loading_t = jnp.transpose(loading_ref[...])
    drift = 0.5 * STEP * jnp.sum(loading_t * loading_t, axis=1, keepdims=True)
    diag = iota((tenors, tenors), 0) == iota((tenors, tenors), 1)
    log_start = jnp.log(jnp.sum(jnp.where(diag, start_ref[...], 0.0), axis=1, keepdims=True))
    loads = jnp.concatenate(split_bf16((STEP**0.5) * loading_t, 3), axis=1)
    lower = mask_bf16(iota((tenors, tenors), 1) <= iota((tenors, tenors), 0))
    lower = jnp.concatenate([lower, lower], axis=1)
    log_fwd = jnp.broadcast_to(log_start, (tenors, LANES))
    drift = jnp.broadcast_to(drift, (tenors, LANES))
    head = LANES - tenors
    copies[2].wait()
    wide_ref[...] = shocks_ref[...].astype(F32)
    step = plan.width // LANES
    for c in range(dates // step):
        shock = jnp.concatenate(
            [
                wide_ref[pl.ds(c * step + j, tenors, stride=dates), :].astype(BF16)
                for j in range(step)
            ],
            axis=1,
        )
        change = jnp.dot(
            loads, jnp.concatenate([shock] * 3, axis=0), preferred_element_type=F32
        )
        logs = []
        for j in range(step):
            log_fwd = log_fwd + (change[:, LANES * j : LANES * (j + 1)] - drift)
            logs.append(log_fwd)
        fwd = jnp.exp(jnp.concatenate(logs, axis=1))
        growth = split_bf16(jnp.log(1.0 + STEP * fwd), 2)
        summed = jnp.dot(lower, jnp.concatenate(growth, axis=0), preferred_element_type=F32)
        bond = jnp.exp(-summed)
        cols = slice(c * plan.width, (c + 1) * plan.width)
        out_ref[0:tenors, cols] = (bond * fwd * (1.0 / RATE_UNIT)).astype(BF16)
        bond = bond.astype(BF16)
        out_ref[tenors:LANES, cols] = bond[0:head]
        for g in range(plan.groups):
            out_ref[LANES + plan.extra * g : LANES + plan.extra * (g + 1), cols] = bond[head:]
        used = LANES + plan.extra * plan.groups
        out_ref[used:, cols] = jnp.zeros((2 * LANES - used, plan.width), BF16)


def left_side(plan, in_ref):
    part, extra = plan.part, plan.extra
    rest = in_ref[:, plan.room :, :].reshape(plan.owners * part, LANES)
    lane = iota((1, LANES), 1)
    left = []
    for g in range(plan.groups):
        main = in_ref[:, part * g : part * (g + 1), :].reshape(plan.owners * part, LANES)
        keep = mask_bf16((lane >= extra * g) & (lane < extra * (g + 1)))
        left.append(jnp.concatenate([main, rest * keep], axis=1))
    return jnp.concatenate(left, axis=0), rest


def price(plan, left, basis_ref, val_ref):
    width = plan.step
    for c in range(basis_ref.shape[1] // width):
        cols = slice(c * width, (c + 1) * width)
        under = jnp.dot(left, basis_ref[:, cols], preferred_element_type=F32)
        val_ref[:, cols] = jnp.maximum(under.astype(BF16), 0)


def membership(plan, me, agr_ref, rest):
    info = []
    for g in range(plan.groups):
        first = 3 * plan.extra + SUBS * g
        pick = mask_bf16(iota((SUBS, LANES), 1) == first + iota((SUBS, LANES), 0))
        info.append(lax.dot_general(pick, rest, BOTH_LANES, preferred_element_type=F32))
    info = jnp.concatenate(info, axis=1)
    local = info[2:3].astype(jnp.int32)
    agr = jnp.zeros_like(local)
    for n in range(NS_DEV):
        agr = jnp.where(local == n, agr_ref[n] - me * AG_DEV, agr)
    row = iota((SUBS, info.shape[1]), 0)
    hot = (row & (AG_DEV - 1)) == agr
    netting = jnp.where(hot, jnp.where(row < AG_DEV, info[0:1], info[1:2]), 0.0).astype(BF16)
    return hot & (row < AG_DEV), netting


def price_kernel(plan, me_ref, agr_ref, basis_ref, in_ref, val_ref, sum_ref):
    left, rest = left_side(plan, in_ref)
    netting = membership(plan, me_ref[0], agr_ref, rest)[1]
    price(plan, left, basis_ref, val_ref)
    sum_ref[...] = jnp.dot(netting, val_ref[...], preferred_element_type=F32)


def main_kernel(plan, path_total, me_ref, agr_ref, cpty_ref, lag_ref, weight_ref, basis_ref, *refs):
    *in_refs, out_ref, val_ref = refs
    val_refs = [val_ref]
    if plan.halves == 2:
        *in_refs, own_ref, sum_ref = in_refs
        val_refs = [own_ref, val_ref]
    me = me_ref[0]
    part, room, dates = plan.part, plan.room, plan.dates
    cpty_dev = weight_ref.shape[0]

    lane = iota((1, LANES), 1)
    hot = []
    for in_ref in in_refs:
        left, rest = left_side(plan, in_ref)
        member, netting = membership(plan, me, agr_ref, rest)
        hot.append(member)
    hot = jnp.concatenate([member.astype(F32) for member in hot], axis=1)

    price(plan, left, basis_ref, val_ref)
    both = jnp.dot(netting, val_ref[...], preferred_element_type=F32)
    if plan.halves == 2:
        both = both + sum_ref[...]
    both = both + pltpu.roll(both, AG_DEV, 0)
    owed = [both[:, LANES * t : LANES * (t + 1)] for t in range(dates)]

    member = iota((SUBS, LANES), 0) & (AG_DEV - 1)
    lag = jnp.zeros((SUBS, LANES), jnp.int32)
    cpty = jnp.zeros((SUBS, LANES), jnp.int32)
    for a in range(AG_DEV):
        lag = jnp.where(member == a, lag_ref[a], lag)
        cpty = jnp.where(member == a, cpty_ref[a] - me * cpty_dev, cpty)
    lags = [lag == s for s in range(1, LAG_MAX + 1)]
    weight = jnp.zeros((SUBS, dates), F32)
    for c in range(cpty_dev):
        weight = jnp.where(cpty[:, 0:dates] == c, weight_ref[c : c + 1, :], weight)
    zero = jnp.zeros((SUBS, LANES), F32)
    spent, slopes = zero, []
    for t in range(dates):
        before = zero
        for s in range(1, min(t, LAG_MAX) + 1):
            before = jnp.where(lags[s - 1], owed[t - s], before)
        excess = owed[t] - before
        square = excess * excess + SMOOTH * SMOOTH
        inverse = lax.rsqrt(square)
        due = weight[:, t : t + 1]
        spent = spent + due * (0.5 * (excess + square * inverse))
        slopes.append(due * (0.5 * (1.0 + excess * inverse)))
    grads = []
    for t in range(dates):
        after = zero
        for s in range(1, min(dates - 1 - t, LAG_MAX) + 1):
            after = jnp.where(lags[s - 1], slopes[t + s], after)
        grads.append(((slopes[t] - after) * (1.0 / path_total)).astype(BF16))

    grads = jnp.concatenate(grads, axis=1)
    dots = [
        lax.dot_general(grads, values[...], BOTH_LANES, preferred_element_type=F32)
        for values in val_refs
    ]
    dots = jnp.concatenate(dots, axis=1)
    share = jnp.sum(hot * dots, axis=0, keepdims=True)
    spent = jnp.sum(spent, axis=1, keepdims=True) * (1.0 / path_total)
    mine = (lane - plan.slots == cpty) & (iota((SUBS, LANES), 0) < AG_DEV)
    cva = jnp.sum(jnp.where(mine, spent, 0.0), axis=0, keepdims=True)
    block = lane // part
    parts = plan.slots // part
    count = parts * plan.lines
    lines = jnp.concatenate([share[:, LANES * k : LANES * (k + 1)] for k in range(count)], axis=0)
    moved = [lines if m == 0 else pltpu.roll(lines, part * m, 1) for m in range(plan.per_line)]
    paths = out_ref.shape[0] // plan.owners
    for k in range(plan.lines):
        for s in range(plan.per_line):
            line = cva
            for g in range(parts):
                n = g * plan.lines + k
                line = jnp.where(block == g, moved[(g - s) % plan.per_line][n : n + 1], line)
            for p in range(paths):
                out_ref[(k * plan.per_line + s) * paths + p] = line


def finish_kernel(plan, me_ref, place_ref, notional_ref, in_ref, alloc_ref, cva_ref):
    me = me_ref[0]
    rows = place_ref.shape[1]
    key = place_ref[0:1, :].astype(jnp.int32)
    rank = place_ref[1:2, :].astype(jnp.int32)
    lines = in_ref[...]
    count = lines.shape[0]
    paths = count // plan.owners
    pieces = jnp.concatenate(split_bf16(lines, 3), axis=0)
    row = iota((pieces.shape[0], 1), 0) & (count - 1)
    shift = paths.bit_length() - 1
    half = row & (plan.halves - 1)
    found = jnp.zeros((pieces.shape[0], rows), F32)
    for h in range(plan.halves):
        slot = rank + plan.room * h
        slot = jnp.where(slot >= plan.slots, slot - plan.slots, slot)
        hot = mask_bf16(iota((LANES, rows), 0) == slot)
        found = jnp.where(half == h, jnp.dot(pieces, hot, preferred_element_type=F32), found)
    wanted = lax.shift_right_logical(row, shift) == key
    share = jnp.sum(jnp.where(wanted, found, 0.0), axis=0, keepdims=True)
    alloc_ref[...] = share * in_a_row(notional_ref[...])
    own = lax.shift_right_logical(iota((count, 1), 0), shift) == me
    cva = jnp.sum(jnp.where(own, lines, 0.0), axis=0, keepdims=True)
    cva_ref[...] = cva[:, plan.slots : plan.slots + cva_ref.shape[1]]


def body(
    shocks,
    forward_start,
    loading,
    coefficient,
    notional,
    ns_of_trade,
    agr_of_ns,
    cpty_of_agr,
    margin_lag,
    default_weight,
):
    owners = lax.axis_size("trade")
    path_parts = lax.axis_size("path")
    tenors, dates, path_dev = shocks.shape
    path_total = float(path_dev * path_parts)
    rows = coefficient.shape[0]
    lines = rows // LANES
    plan = Plan(owners, rows, tenors, dates)
    cols = dates * path_dev
    me = lax.axis_index("trade").astype(jnp.int32).reshape(1)
    half = lax.rem(lax.axis_index("path").astype(jnp.int32), plan.halves).reshape(1)
    notional = notional.reshape(lines, LANES)

    place, outgoing = pl.pallas_call(
        functools.partial(pack_kernel, plan),
        out_shape=[
            jax.ShapeDtypeStruct((SUBS, rows), F32),
            jax.ShapeDtypeStruct((owners, plan.height, LANES), BF16),
        ],
        in_specs=[SMEM] * 2 + [HBM] * 3,
        out_specs=[VMEM, VMEM],
        scratch_shapes=[
            pltpu.VMEM((owners * lines, LANES), jnp.int32),
            pltpu.VMEM((2 * tenors, rows), BF16),
            pltpu.VMEM((lines, LANES), F32),
            pltpu.SemaphoreType.DMA((3,)),
        ],
        name="pack",
        cost_estimate=pl.CostEstimate(flops=1 << 32, bytes_accessed=1 << 19, transcendentals=0),
    )(me, half, ns_of_trade.reshape(owners * lines, LANES), coefficient.T, notional)
    incoming = [lax.all_to_all(outgoing, "trade", split_axis=0, concat_axis=0, tiled=True)]
    basis = pl.pallas_call(
        functools.partial(basis_kernel, plan),
        out_shape=jax.ShapeDtypeStruct((2 * LANES, cols), BF16),
        in_specs=[HBM] * 3,
        out_specs=VMEM,
        scratch_shapes=[
            pltpu.VMEM((tenors * dates, path_dev), BF16),
            pltpu.VMEM((1, tenors), F32),
            pltpu.VMEM((tenors, tenors), F32),
            pltpu.VMEM((tenors * dates, path_dev), F32),
            pltpu.SemaphoreType.DMA((3,)),
        ],
        name="basis",
        compiler_params=pltpu.CompilerParams(vmem_limit_bytes=16 << 20),
        cost_estimate=pl.CostEstimate(
            flops=2 * 400 * tenors * cols, bytes_accessed=4 << 20, transcendentals=3 * tenors * cols
        ),
    )(shocks.reshape(tenors * dates, path_dev), forward_start.reshape(1, tenors), loading)

    half_trades = plan.trades // plan.halves
    if plan.halves == 2:
        incoming[0], basis = lax.optimization_barrier((incoming[0], basis))
        pairs = [(p, p ^ 1) for p in range(path_parts)]
        incoming.append(lax.ppermute(incoming[0], "path", pairs))
        incoming.extend(
            pl.pallas_call(
                functools.partial(price_kernel, plan),
                out_shape=[
                    jax.ShapeDtypeStruct((half_trades, cols), BF16),
                    jax.ShapeDtypeStruct((SUBS, cols), F32),
                ],
                in_specs=[SMEM] * 2 + [VMEM] * 2,
                out_specs=[VMEM, VMEM],
                name="price_own_half",
                compiler_params=pltpu.CompilerParams(vmem_limit_bytes=24 << 20),
                cost_estimate=pl.CostEstimate(
                    flops=4 * half_trades * LANES * cols, bytes_accessed=6 << 20, transcendentals=0
                ),
            )(me, agr_of_ns, basis, incoming[0])
        )

    need = 2 * plan.trades * cols + 8 * plan.trades * plan.step + (8 << 20)
    lines_out = pl.pallas_call(
        functools.partial(main_kernel, plan, path_total),
        out_shape=jax.ShapeDtypeStruct((owners * path_parts, 1, LANES), F32),
        in_specs=[SMEM] * 4 + [VMEM] * (2 + len(incoming)),
        out_specs=VMEM,
        scratch_shapes=[pltpu.VMEM((half_trades, cols), BF16)],
        name="value_and_allocate",
        compiler_params=pltpu.CompilerParams(vmem_limit_bytes=need),
    )(me, agr_of_ns, cpty_of_agr, margin_lag, default_weight, basis, *incoming)

    lines_in = lax.all_to_all(lines_out, ("trade", "path"), split_axis=0, concat_axis=0, tiled=True)
    lines_in = lines_in.reshape(owners * path_parts, LANES)
    allocation, cva = pl.pallas_call(
        functools.partial(finish_kernel, plan),
        out_shape=[
            jax.ShapeDtypeStruct((1, rows), F32),
            jax.ShapeDtypeStruct((1, default_weight.shape[0]), F32),
        ],
        in_specs=[SMEM] + [VMEM] * 3,
        out_specs=[VMEM, VMEM],
        name="finish",
        compiler_params=pltpu.CompilerParams(vmem_limit_bytes=32 << 20),
    )(me, place, notional, lines_in)
    return (allocation.reshape(rows), cva.reshape(default_weight.shape[0]))


def solution(mesh):
    placed = (
        P(None, None, "path"),
        P(),
        P(),
        P("trade", None),
        P("trade"),
        P(),
        P("trade"),
        P("trade"),
        P("trade"),
        P("trade", None),
    )
    return jax.shard_map(
        body, mesh=mesh, in_specs=placed, out_specs=(P("trade"), P("trade")), check_vma=False
    )
```

```python
import functools

import jax
import jax.numpy as jnp
from jax import lax
from jax.experimental import pallas as pl
from jax.experimental.pallas import tpu as pltpu
from jax.sharding import PartitionSpec as P

NS_DEV = 8
AG_DEV = 4
LAG_MAX = 4
LANES = 128
SUBS = 8

RATE_UNIT = 0.03
STEP = 0.25
SMOOTH = 0.5

F32 = jnp.float32
BF16 = jnp.bfloat16
VMEM = pl.BlockSpec(memory_space=pltpu.VMEM)
SMEM = pl.BlockSpec(memory_space=pltpu.SMEM)
HBM = pl.BlockSpec(memory_space=pltpu.HBM)
BOTH_LANES = (((1,), (1,)), ((), ()))


def iota(shape, dim):
    return lax.broadcasted_iota(jnp.int32, shape, dim)


def mask_bf16(mask):
    return mask.astype(F32).astype(BF16)


def split_bf16(x, parts):
    pieces = []
    for _ in range(parts):
        piece = x.astype(BF16)
        pieces.append(piece)
        x = x - piece.astype(F32)
    return pieces


def fetch(sources, targets, sems):
    copies = [pltpu.make_async_copy(a, b, sems.at[n]) for n, (a, b) in enumerate(zip(sources, targets))]
    for copy in copies:
        copy.start()
    return copies


def in_a_row(x):
    return jnp.concatenate([x[r : r + 1] for r in range(x.shape[0])], axis=1)


class Plan:
    def __init__(self, owners, rows, tenors, dates):
        most = 3 * rows // (2 * owners)
        self.owners = owners
        self.halves = 2 if most % 96 == 0 else 1
        most = most // self.halves
        self.groups = 3 if most % 48 == 0 else 1
        self.part = -(-most // (16 * self.groups)) * 16
        self.room = self.groups * self.part
        self.height = self.room + self.part
        self.extra = 2 * tenors - LANES
        self.per_line = LANES // self.part
        self.lines = owners * self.part // LANES
        self.slots = self.halves * self.room
        self.trades = owners * self.slots
        self.dates = dates
        self.width = 1024
        self.step = 2048 if self.trades <= 1024 else 512


def pack_kernel(plan, me_ref, half_ref, sets_hbm, coef_hbm, notional_hbm, place_ref, out_ref, *refs):
    sets_ref, coef_ref, notional_ref, sems = refs
    copies = fetch(
        [sets_hbm, notional_hbm, coef_hbm], [sets_ref, notional_ref, coef_ref], sems
    )
    me = me_ref[0]
    owners, part, room, extra = plan.owners, plan.part, plan.room, plan.extra
    lines = notional_ref.shape[0]
    rows = lines * LANES
    shared = SUBS // lines
    copies[0].wait()
    block = sets_ref[pl.ds(pl.multiple_of(me // shared * SUBS, SUBS), SUBS), :]
    own = block[0:lines]
    for b in range(1, shared):
        own = jnp.where(lax.rem(me, shared) == b, block[b * lines : (b + 1) * lines], own)
    sets = in_a_row(own)
    key = lax.shift_right_logical(sets, 3)
    local = sets - key * NS_DEV
    hot = iota((owners, rows), 0) == key
    before = mask_bf16(iota((rows, rows), 0) < iota((rows, rows), 1))
    count = jnp.dot(mask_bf16(hot), before, preferred_element_type=F32)
    rank = jnp.sum(jnp.where(hot, count, 0.0), axis=0, keepdims=True)
    place_ref[...] = jnp.concatenate(
        [key.astype(F32), rank, jnp.zeros((SUBS - 2, rows), F32)], axis=0
    )
    mine = rank.astype(jnp.int32) - room * half_ref[0]
    spot = jnp.where((mine >= 0) & (mine < room), key * room + mine, -1)
    chosen = mask_bf16(iota((owners * room, rows), 0) == spot)
    copies[1].wait()
    notional = in_a_row(notional_ref[...])
    high = notional.astype(BF16).astype(F32)
    info = jnp.concatenate(
        [high, notional - high, local.astype(F32), jnp.zeros((13, rows), F32)], axis=0
    )
    copies[2].wait()
    table = jnp.concatenate([coef_ref[...], info.astype(BF16)], axis=0)
    moved = lax.dot_general(chosen, table, BOTH_LANES, preferred_element_type=F32)
    ids = LANES + extra
    for d in range(owners):
        message = out_ref.at[d]
        block = moved[d * room : (d + 1) * room]
        message[0:room, :] = block[:, 0:LANES].astype(BF16)
        split = [block[part * g : part * (g + 1)] for g in range(plan.groups)]
        lanes = [x[:, LANES:ids] for x in split]
        if plan.groups < 3:
            lanes.append(jnp.zeros((part, extra * (3 - plan.groups)), F32))
        lanes += [x[:, ids : ids + SUBS] for x in split]
        lanes.append(jnp.zeros((part, SUBS * (4 - plan.groups)), F32))
        message[room:, :] = jnp.concatenate(lanes, axis=1).astype(BF16)


def basis_kernel(plan, shocks_hbm, start_hbm, loading_hbm, out_ref, *refs):
    shocks_ref, start_ref, loading_ref, wide_ref, sems = refs
    copies = fetch(
        [loading_hbm, start_hbm, shocks_hbm], [loading_ref, start_ref, shocks_ref], sems
    )
    tenors = loading_ref.shape[0]
    dates = plan.dates
    copies[0].wait()
    copies[1].wait()
    loading_t = jnp.transpose(loading_ref[...])
    drift = 0.5 * STEP * jnp.sum(loading_t * loading_t, axis=1, keepdims=True)
    diag = iota((tenors, tenors), 0) == iota((tenors, tenors), 1)
    log_start = jnp.log(jnp.sum(jnp.where(diag, start_ref[...], 0.0), axis=1, keepdims=True))
    loads = jnp.concatenate(split_bf16((STEP**0.5) * loading_t, 3), axis=1)
    lower = mask_bf16(iota((tenors, tenors), 1) <= iota((tenors, tenors), 0))
    lower = jnp.concatenate([lower, lower], axis=1)
    log_fwd = jnp.broadcast_to(log_start, (tenors, LANES))
    drift = jnp.broadcast_to(drift, (tenors, LANES))
    head = LANES - tenors
    copies[2].wait()
    wide_ref[...] = shocks_ref[...].astype(F32)
    step = plan.width // LANES
    for c in range(dates // step):
        shock = jnp.concatenate(
            [
                wide_ref[pl.ds(c * step + j, tenors, stride=dates), :].astype(BF16)
                for j in range(step)
            ],
            axis=1,
        )
        change = jnp.dot(
            loads, jnp.concatenate([shock] * 3, axis=0), preferred_element_type=F32
        )
        logs = []
        for j in range(step):
            log_fwd = log_fwd + (change[:, LANES * j : LANES * (j + 1)] - drift)
            logs.append(log_fwd)
        fwd = jnp.exp(jnp.concatenate(logs, axis=1))
        growth = split_bf16(jnp.log(1.0 + STEP * fwd), 2)
        summed = jnp.dot(lower, jnp.concatenate(growth, axis=0), preferred_element_type=F32)
        bond = jnp.exp(-summed)
        cols = slice(c * plan.width, (c + 1) * plan.width)
        out_ref[0:tenors, cols] = (bond * fwd * (1.0 / RATE_UNIT)).astype(BF16)
        bond = bond.astype(BF16)
        out_ref[tenors:LANES, cols] = bond[0:head]
        for g in range(plan.groups):
            out_ref[LANES + plan.extra * g : LANES + plan.extra * (g + 1), cols] = bond[head:]
        used = LANES + plan.extra * plan.groups
        out_ref[used:, cols] = jnp.zeros((2 * LANES - used, plan.width), BF16)


def left_side(plan, in_ref):
    part, extra = plan.part, plan.extra
    rest = in_ref[:, plan.room :, :].reshape(plan.owners * part, LANES)
    lane = iota((1, LANES), 1)
    left = []
    for g in range(plan.groups):
        main = in_ref[:, part * g : part * (g + 1), :].reshape(plan.owners * part, LANES)
        keep = mask_bf16((lane >= extra * g) & (lane < extra * (g + 1)))
        left.append(jnp.concatenate([main, rest * keep], axis=1))
    return jnp.concatenate(left, axis=0), rest


def price(plan, left, basis_ref, val_ref):
    width = plan.step
    for c in range(basis_ref.shape[1] // width):
        cols = slice(c * width, (c + 1) * width)
        under = jnp.dot(left, basis_ref[:, cols], preferred_element_type=F32)
        val_ref[:, cols] = jnp.maximum(under.astype(BF16), 0)


def price_kernel(plan, basis_ref, in_ref, val_ref):
    price(plan, left_side(plan, in_ref)[0], basis_ref, val_ref)


def main_kernel(plan, path_total, me_ref, agr_ref, cpty_ref, lag_ref, weight_ref, basis_ref, *refs):
    *in_refs, out_ref, val_ref = refs
    val_refs = [val_ref]
    if plan.halves == 2:
        val_refs = [in_refs.pop(), val_ref]
    me = me_ref[0]
    part, room, dates = plan.part, plan.room, plan.dates
    cpty_dev = weight_ref.shape[0]

    lane = iota((1, LANES), 1)
    info = []
    for in_ref in in_refs:
        left, rest = left_side(plan, in_ref)
        for g in range(plan.groups):
            first = 3 * plan.extra + SUBS * g
            pick = mask_bf16(iota((SUBS, LANES), 1) == first + iota((SUBS, LANES), 0))
            info.append(lax.dot_general(pick, rest, BOTH_LANES, preferred_element_type=F32))
    info = jnp.concatenate(info, axis=1)
    local = info[2:3].astype(jnp.int32)
    agr = jnp.zeros_like(local)
    for n in range(NS_DEV):
        agr = jnp.where(local == n, agr_ref[n] - me * AG_DEV, agr)
    row = iota((SUBS, plan.trades), 0)
    hot = (row & (AG_DEV - 1)) == agr
    netting = jnp.where(hot, jnp.where(row < AG_DEV, info[0:1], info[1:2]), 0.0).astype(BF16)

    size = val_ref.shape[0]
    both = jnp.zeros((SUBS, val_ref.shape[1]), F32)
    for h, values in enumerate(val_refs):
        if h == len(val_refs) - 1:
            price(plan, left, basis_ref, val_ref)
        both = both + jnp.dot(
            netting[:, size * h : size * (h + 1)], values[...], preferred_element_type=F32
        )
    both = both + pltpu.roll(both, AG_DEV, 0)
    owed = [both[:, LANES * t : LANES * (t + 1)] for t in range(dates)]

    member = iota((SUBS, LANES), 0) & (AG_DEV - 1)
    lag = jnp.zeros((SUBS, LANES), jnp.int32)
    cpty = jnp.zeros((SUBS, LANES), jnp.int32)
    for a in range(AG_DEV):
        lag = jnp.where(member == a, lag_ref[a], lag)
        cpty = jnp.where(member == a, cpty_ref[a] - me * cpty_dev, cpty)
    lags = [lag == s for s in range(1, LAG_MAX + 1)]
    weight = jnp.zeros((SUBS, dates), F32)
    for c in range(cpty_dev):
        weight = jnp.where(cpty[:, 0:dates] == c, weight_ref[c : c + 1, :], weight)
    zero = jnp.zeros((SUBS, LANES), F32)
    spent, slopes = zero, []
    for t in range(dates):
        before = zero
        for s in range(1, min(t, LAG_MAX) + 1):
            before = jnp.where(lags[s - 1], owed[t - s], before)
        excess = owed[t] - before
        square = excess * excess + SMOOTH * SMOOTH
        inverse = lax.rsqrt(square)
        due = weight[:, t : t + 1]
        spent = spent + due * (0.5 * (excess + square * inverse))
        slopes.append(due * (0.5 * (1.0 + excess * inverse)))
    grads = []
    for t in range(dates):
        after = zero
        for s in range(1, min(dates - 1 - t, LAG_MAX) + 1):
            after = jnp.where(lags[s - 1], slopes[t + s], after)
        grads.append(((slopes[t] - after) * (1.0 / path_total)).astype(BF16))

    grads = jnp.concatenate(grads, axis=1)
    dots = [
        lax.dot_general(grads, values[...], BOTH_LANES, preferred_element_type=F32)
        for values in val_refs
    ]
    dots = jnp.concatenate(dots, axis=1)
    share = jnp.sum(jnp.where(hot & (row < AG_DEV), dots, 0.0), axis=0, keepdims=True)
    spent = jnp.sum(spent, axis=1, keepdims=True) * (1.0 / path_total)
    mine = (lane - plan.slots == cpty) & (iota((SUBS, LANES), 0) < AG_DEV)
    cva = jnp.sum(jnp.where(mine, spent, 0.0), axis=0, keepdims=True)
    block = lane // part
    parts = plan.slots // part
    count = parts * plan.lines
    lines = jnp.concatenate([share[:, LANES * k : LANES * (k + 1)] for k in range(count)], axis=0)
    moved = [lines if m == 0 else pltpu.roll(lines, part * m, 1) for m in range(plan.per_line)]
    paths = out_ref.shape[0] // plan.owners
    for k in range(plan.lines):
        for s in range(plan.per_line):
            line = cva
            for g in range(parts):
                n = g * plan.lines + k
                line = jnp.where(block == g, moved[(g - s) % plan.per_line][n : n + 1], line)
            for p in range(paths):
                out_ref[(k * plan.per_line + s) * paths + p] = line


def finish_kernel(plan, me_ref, place_ref, notional_ref, in_ref, alloc_ref, cva_ref):
    me = me_ref[0]
    rows = place_ref.shape[1]
    key = place_ref[0:1, :].astype(jnp.int32)
    rank = place_ref[1:2, :].astype(jnp.int32)
    lines = in_ref[...]
    count = lines.shape[0]
    paths = count // plan.owners
    pieces = jnp.concatenate(split_bf16(lines, 3), axis=0)
    row = iota((pieces.shape[0], 1), 0) & (count - 1)
    shift = paths.bit_length() - 1
    half = row & (plan.halves - 1)
    found = jnp.zeros((pieces.shape[0], rows), F32)
    for h in range(plan.halves):
        slot = rank + plan.room * h
        slot = jnp.where(slot >= plan.slots, slot - plan.slots, slot)
        hot = mask_bf16(iota((LANES, rows), 0) == slot)
        found = jnp.where(half == h, jnp.dot(pieces, hot, preferred_element_type=F32), found)
    wanted = lax.shift_right_logical(row, shift) == key
    share = jnp.sum(jnp.where(wanted, found, 0.0), axis=0, keepdims=True)
    alloc_ref[...] = share * in_a_row(notional_ref[...])
    own = lax.shift_right_logical(iota((count, 1), 0), shift) == me
    cva = jnp.sum(jnp.where(own, lines, 0.0), axis=0, keepdims=True)
    cva_ref[...] = cva[:, plan.slots : plan.slots + cva_ref.shape[1]]


def body(
    shocks,
    forward_start,
    loading,
    coefficient,
    notional,
    ns_of_trade,
    agr_of_ns,
    cpty_of_agr,
    margin_lag,
    default_weight,
):
    owners = lax.axis_size("trade")
    path_parts = lax.axis_size("path")
    tenors, dates, path_dev = shocks.shape
    path_total = float(path_dev * path_parts)
    rows = coefficient.shape[0]
    lines = rows // LANES
    plan = Plan(owners, rows, tenors, dates)
    cols = dates * path_dev
    me = lax.axis_index("trade").astype(jnp.int32).reshape(1)
    half = lax.rem(lax.axis_index("path").astype(jnp.int32), plan.halves).reshape(1)
    notional = notional.reshape(lines, LANES)

    place, outgoing = pl.pallas_call(
        functools.partial(pack_kernel, plan),
        out_shape=[
            jax.ShapeDtypeStruct((SUBS, rows), F32),
            jax.ShapeDtypeStruct((owners, plan.height, LANES), BF16),
        ],
        in_specs=[SMEM] * 2 + [HBM] * 3,
        out_specs=[VMEM, VMEM],
        scratch_shapes=[
            pltpu.VMEM((owners * lines, LANES), jnp.int32),
            pltpu.VMEM((2 * tenors, rows), BF16),
            pltpu.VMEM((lines, LANES), F32),
            pltpu.SemaphoreType.DMA((3,)),
        ],
        name="pack",
        cost_estimate=pl.CostEstimate(flops=1 << 32, bytes_accessed=1 << 19, transcendentals=0),
    )(me, half, ns_of_trade.reshape(owners * lines, LANES), coefficient.T, notional)
    incoming = [lax.all_to_all(outgoing, "trade", split_axis=0, concat_axis=0, tiled=True)]
    basis = pl.pallas_call(
        functools.partial(basis_kernel, plan),
        out_shape=jax.ShapeDtypeStruct((2 * LANES, cols), BF16),
        in_specs=[HBM] * 3,
        out_specs=VMEM,
        scratch_shapes=[
            pltpu.VMEM((tenors * dates, path_dev), BF16),
            pltpu.VMEM((1, tenors), F32),
            pltpu.VMEM((tenors, tenors), F32),
            pltpu.VMEM((tenors * dates, path_dev), F32),
            pltpu.SemaphoreType.DMA((3,)),
        ],
        name="basis",
        compiler_params=pltpu.CompilerParams(vmem_limit_bytes=16 << 20),
        cost_estimate=pl.CostEstimate(
            flops=2 * 400 * tenors * cols, bytes_accessed=4 << 20, transcendentals=3 * tenors * cols
        ),
    )(shocks.reshape(tenors * dates, path_dev), forward_start.reshape(1, tenors), loading)

    half_trades = plan.trades // plan.halves
    if plan.halves == 2:
        incoming[0], basis = lax.optimization_barrier((incoming[0], basis))
        pairs = [(p, p ^ 1) for p in range(path_parts)]
        incoming.append(lax.ppermute(incoming[0], "path", pairs))
        incoming.append(
            pl.pallas_call(
                functools.partial(price_kernel, plan),
                out_shape=jax.ShapeDtypeStruct((half_trades, cols), BF16),
                in_specs=[VMEM] * 2,
                out_specs=VMEM,
                name="price_own_half",
                compiler_params=pltpu.CompilerParams(vmem_limit_bytes=24 << 20),
                cost_estimate=pl.CostEstimate(
                    flops=4 * half_trades * LANES * cols, bytes_accessed=6 << 20, transcendentals=0
                ),
            )(basis, incoming[0])
        )

    need = 2 * plan.trades * cols + 8 * plan.trades * plan.step + (8 << 20)
    lines_out = pl.pallas_call(
        functools.partial(main_kernel, plan, path_total),
        out_shape=jax.ShapeDtypeStruct((owners * path_parts, 1, LANES), F32),
        in_specs=[SMEM] * 4 + [VMEM] * (2 + len(incoming)),
        out_specs=VMEM,
        scratch_shapes=[pltpu.VMEM((half_trades, cols), BF16)],
        name="value_and_allocate",
        compiler_params=pltpu.CompilerParams(vmem_limit_bytes=need),
    )(me, agr_of_ns, cpty_of_agr, margin_lag, default_weight, basis, *incoming)

    lines_in = lax.all_to_all(lines_out, ("trade", "path"), split_axis=0, concat_axis=0, tiled=True)
    lines_in = lines_in.reshape(owners * path_parts, LANES)
    allocation, cva = pl.pallas_call(
        functools.partial(finish_kernel, plan),
        out_shape=[
            jax.ShapeDtypeStruct((1, rows), F32),
            jax.ShapeDtypeStruct((1, default_weight.shape[0]), F32),
        ],
        in_specs=[SMEM] + [VMEM] * 3,
        out_specs=[VMEM, VMEM],
        name="finish",
        compiler_params=pltpu.CompilerParams(vmem_limit_bytes=32 << 20),
    )(me, place, notional, lines_in)
    return (allocation.reshape(rows), cva.reshape(default_weight.shape[0]))


def solution(mesh):
    placed = (
        P(None, None, "path"),
        P(),
        P(),
        P("trade", None),
        P("trade"),
        P(),
        P("trade"),
        P("trade"),
        P("trade"),
        P("trade", None),
    )
    return jax.shard_map(
        body, mesh=mesh, in_specs=placed, out_specs=(P("trade"), P("trade")), check_vma=False
    )
```

```python
import functools

import jax
import jax.numpy as jnp
from jax import lax
from jax.experimental import pallas as pl
from jax.experimental.pallas import tpu as pltpu
from jax.sharding import PartitionSpec as P

NS_DEV = 8
AG_DEV = 4
LAG_MAX = 4
LANES = 128
SUBS = 8

RATE_UNIT = 0.03
STEP = 0.25
SMOOTH = 0.5

F32 = jnp.float32
BF16 = jnp.bfloat16
VMEM = pl.BlockSpec(memory_space=pltpu.VMEM)
SMEM = pl.BlockSpec(memory_space=pltpu.SMEM)
HBM = pl.BlockSpec(memory_space=pltpu.HBM)
BOTH_LANES = (((1,), (1,)), ((), ()))


def iota(shape, dim):
    return lax.broadcasted_iota(jnp.int32, shape, dim)


def mask_bf16(mask):
    return mask.astype(F32).astype(BF16)


def split_bf16(x, parts):
    pieces = []
    for _ in range(parts):
        piece = x.astype(BF16)
        pieces.append(piece)
        x = x - piece.astype(F32)
    return pieces


def fetch(sources, targets, sems):
    copies = [pltpu.make_async_copy(a, b, sems.at[n]) for n, (a, b) in enumerate(zip(sources, targets))]
    for copy in copies:
        copy.start()
    return copies


def in_a_row(x):
    return jnp.concatenate([x[r : r + 1] for r in range(x.shape[0])], axis=1)


class Plan:
    def __init__(self, owners, rows, tenors, dates):
        most = 3 * rows // (2 * owners)
        self.owners = owners
        self.halves = 2 if most % 96 == 0 else 1
        most = most // self.halves
        self.groups = 3 if most % 48 == 0 else 1
        self.part = -(-most // (16 * self.groups)) * 16
        self.room = self.groups * self.part
        self.height = self.room + self.part
        self.extra = 2 * tenors - LANES
        self.per_line = LANES // self.part
        self.lines = owners * self.part // LANES
        self.slots = self.halves * self.room
        self.trades = owners * self.slots
        self.dates = dates
        self.width = 1024
        self.step = 1024 if self.trades <= 1024 else 512


def pack_kernel(plan, me_ref, half_ref, sets_hbm, coef_hbm, notional_hbm, place_ref, out_ref, *refs):
    sets_ref, coef_ref, notional_ref, sems = refs
    copies = fetch(
        [sets_hbm, notional_hbm, coef_hbm], [sets_ref, notional_ref, coef_ref], sems
    )
    me = me_ref[0]
    owners, part, room, extra = plan.owners, plan.part, plan.room, plan.extra
    lines = notional_ref.shape[0]
    rows = lines * LANES
    shared = SUBS // lines
    copies[0].wait()
    block = sets_ref[pl.ds(pl.multiple_of(me // shared * SUBS, SUBS), SUBS), :]
    own = block[0:lines]
    for b in range(1, shared):
        own = jnp.where(lax.rem(me, shared) == b, block[b * lines : (b + 1) * lines], own)
    sets = in_a_row(own)
    key = lax.shift_right_logical(sets, 3)
    local = sets - key * NS_DEV
    hot = iota((owners, rows), 0) == key
    before = mask_bf16(iota((rows, rows), 0) < iota((rows, rows), 1))
    count = jnp.dot(mask_bf16(hot), before, preferred_element_type=F32)
    rank = jnp.sum(jnp.where(hot, count, 0.0), axis=0, keepdims=True)
    place_ref[...] = jnp.concatenate(
        [key.astype(F32), rank, jnp.zeros((SUBS - 2, rows), F32)], axis=0
    )
    mine = rank.astype(jnp.int32) - room * half_ref[0]
    spot = jnp.where((mine >= 0) & (mine < room), key * room + mine, -1)
    chosen = mask_bf16(iota((owners * room, rows), 0) == spot)
    copies[1].wait()
    notional = in_a_row(notional_ref[...])
    high = notional.astype(BF16).astype(F32)
    info = jnp.concatenate(
        [high, notional - high, local.astype(F32), jnp.zeros((13, rows), F32)], axis=0
    )
    copies[2].wait()
    table = jnp.concatenate([coef_ref[...], info.astype(BF16)], axis=0)
    moved = lax.dot_general(chosen, table, BOTH_LANES, preferred_element_type=F32)
    ids = LANES + extra
    for d in range(owners):
        message = out_ref.at[d]
        block = moved[d * room : (d + 1) * room]
        message[0:room, :] = block[:, 0:LANES].astype(BF16)
        split = [block[part * g : part * (g + 1)] for g in range(plan.groups)]
        lanes = [x[:, LANES:ids] for x in split]
        if plan.groups < 3:
            lanes.append(jnp.zeros((part, extra * (3 - plan.groups)), F32))
        lanes += [x[:, ids : ids + SUBS] for x in split]
        lanes.append(jnp.zeros((part, SUBS * (4 - plan.groups)), F32))
        message[room:, :] = jnp.concatenate(lanes, axis=1).astype(BF16)


def basis_kernel(plan, shocks_hbm, start_hbm, loading_hbm, out_ref, *refs):
    shocks_ref, start_ref, loading_ref, wide_ref, sems = refs
    copies = fetch(
        [loading_hbm, start_hbm, shocks_hbm], [loading_ref, start_ref, shocks_ref], sems
    )
    tenors = loading_ref.shape[0]
    dates = plan.dates
    copies[0].wait()
    copies[1].wait()
    loading_t = jnp.transpose(loading_ref[...])
    drift = 0.5 * STEP * jnp.sum(loading_t * loading_t, axis=1, keepdims=True)
    diag = iota((tenors, tenors), 0) == iota((tenors, tenors), 1)
    log_start = jnp.log(jnp.sum(jnp.where(diag, start_ref[...], 0.0), axis=1, keepdims=True))
    loads = jnp.concatenate(split_bf16((STEP**0.5) * loading_t, 3), axis=1)
    lower = mask_bf16(iota((tenors, tenors), 1) <= iota((tenors, tenors), 0))
    lower = jnp.concatenate([lower, lower], axis=1)
    log_fwd = jnp.broadcast_to(log_start, (tenors, LANES))
    drift = jnp.broadcast_to(drift, (tenors, LANES))
    head = LANES - tenors
    copies[2].wait()
    wide_ref[...] = shocks_ref[...].astype(F32)
    step = plan.width // LANES
    for c in range(dates // step):
        shock = jnp.concatenate(
            [
                wide_ref[pl.ds(c * step + j, tenors, stride=dates), :].astype(BF16)
                for j in range(step)
            ],
            axis=1,
        )
        change = jnp.dot(
            loads, jnp.concatenate([shock] * 3, axis=0), preferred_element_type=F32
        )
        logs = []
        for j in range(step):
            log_fwd = log_fwd + (change[:, LANES * j : LANES * (j + 1)] - drift)
            logs.append(log_fwd)
        fwd = jnp.exp(jnp.concatenate(logs, axis=1))
        growth = split_bf16(jnp.log(1.0 + STEP * fwd), 2)
        summed = jnp.dot(lower, jnp.concatenate(growth, axis=0), preferred_element_type=F32)
        bond = jnp.exp(-summed)
        cols = slice(c * plan.width, (c + 1) * plan.width)
        out_ref[0:tenors, cols] = (bond * fwd * (1.0 / RATE_UNIT)).astype(BF16)
        bond = bond.astype(BF16)
        out_ref[tenors:LANES, cols] = bond[0:head]
        for g in range(plan.groups):
            out_ref[LANES + plan.extra * g : LANES + plan.extra * (g + 1), cols] = bond[head:]
        used = LANES + plan.extra * plan.groups
        out_ref[used:, cols] = jnp.zeros((2 * LANES - used, plan.width), BF16)


def left_side(plan, in_ref):
    part, extra = plan.part, plan.extra
    rest = in_ref[:, plan.room :, :].reshape(plan.owners * part, LANES)
    lane = iota((1, LANES), 1)
    left = []
    for g in range(plan.groups):
        main = in_ref[:, part * g : part * (g + 1), :].reshape(plan.owners * part, LANES)
        keep = mask_bf16((lane >= extra * g) & (lane < extra * (g + 1)))
        left.append(jnp.concatenate([main, rest * keep], axis=1))
    return jnp.concatenate(left, axis=0), rest


def price(plan, left, basis_ref, val_ref):
    width = plan.step
    for c in range(basis_ref.shape[1] // width):
        cols = slice(c * width, (c + 1) * width)
        under = jnp.dot(left, basis_ref[:, cols], preferred_element_type=F32)
        val_ref[:, cols] = jnp.maximum(under.astype(BF16), 0)


def price_kernel(plan, basis_ref, in_ref, val_ref):
    price(plan, left_side(plan, in_ref)[0], basis_ref, val_ref)


def main_kernel(plan, path_total, me_ref, agr_ref, cpty_ref, lag_ref, weight_ref, basis_ref, *refs):
    *in_refs, out_ref, val_ref = refs
    val_refs = [val_ref]
    if plan.halves == 2:
        val_refs = [in_refs.pop(), val_ref]
    me = me_ref[0]
    part, room, dates = plan.part, plan.room, plan.dates
    cpty_dev = weight_ref.shape[0]

    lane = iota((1, LANES), 1)
    info = []
    for in_ref in in_refs:
        left, rest = left_side(plan, in_ref)
        for g in range(plan.groups):
            first = 3 * plan.extra + SUBS * g
            pick = mask_bf16(iota((SUBS, LANES), 1) == first + iota((SUBS, LANES), 0))
            info.append(lax.dot_general(pick, rest, BOTH_LANES, preferred_element_type=F32))
    info = jnp.concatenate(info, axis=1)
    local = info[2:3].astype(jnp.int32)
    agr = jnp.zeros_like(local)
    for n in range(NS_DEV):
        agr = jnp.where(local == n, agr_ref[n] - me * AG_DEV, agr)
    row = iota((SUBS, plan.trades), 0)
    hot = (row & (AG_DEV - 1)) == agr
    netting = jnp.where(hot, jnp.where(row < AG_DEV, info[0:1], info[1:2]), 0.0).astype(BF16)

    price(plan, left, basis_ref, val_ref)
    size = val_ref.shape[0]
    both = jnp.zeros((SUBS, val_ref.shape[1]), F32)
    for h, values in enumerate(val_refs):
        both = both + jnp.dot(
            netting[:, size * h : size * (h + 1)], values[...], preferred_element_type=F32
        )
    both = both + pltpu.roll(both, AG_DEV, 0)
    owed = [both[:, LANES * t : LANES * (t + 1)] for t in range(dates)]

    member = iota((SUBS, LANES), 0) & (AG_DEV - 1)
    lag = jnp.zeros((SUBS, LANES), jnp.int32)
    cpty = jnp.zeros((SUBS, LANES), jnp.int32)
    for a in range(AG_DEV):
        lag = jnp.where(member == a, lag_ref[a], lag)
        cpty = jnp.where(member == a, cpty_ref[a] - me * cpty_dev, cpty)
    lags = [lag == s for s in range(1, LAG_MAX + 1)]
    weight = jnp.zeros((SUBS, dates), F32)
    for c in range(cpty_dev):
        weight = jnp.where(cpty[:, 0:dates] == c, weight_ref[c : c + 1, :], weight)
    zero = jnp.zeros((SUBS, LANES), F32)
    spent, slopes = zero, []
    for t in range(dates):
        before = zero
        for s in range(1, min(t, LAG_MAX) + 1):
            before = jnp.where(lags[s - 1], owed[t - s], before)
        excess = owed[t] - before
        square = excess * excess + SMOOTH * SMOOTH
        inverse = lax.rsqrt(square)
        due = weight[:, t : t + 1]
        spent = spent + due * (0.5 * (excess + square * inverse))
        slopes.append(due * (0.5 * (1.0 + excess * inverse)))
    grads = []
    for t in range(dates):
        after = zero
        for s in range(1, min(dates - 1 - t, LAG_MAX) + 1):
            after = jnp.where(lags[s - 1], slopes[t + s], after)
        grads.append(((slopes[t] - after) * (1.0 / path_total)).astype(BF16))

    grads = jnp.concatenate(grads, axis=1)
    dots = [
        lax.dot_general(grads, values[...], BOTH_LANES, preferred_element_type=F32)
        for values in val_refs
    ]
    dots = jnp.concatenate(dots, axis=1)
    share = jnp.sum(jnp.where(hot & (row < AG_DEV), dots, 0.0), axis=0, keepdims=True)
    spent = jnp.sum(spent, axis=1, keepdims=True) * (1.0 / path_total)
    mine = (lane - plan.slots == cpty) & (iota((SUBS, LANES), 0) < AG_DEV)
    cva = jnp.sum(jnp.where(mine, spent, 0.0), axis=0, keepdims=True)
    block = lane // part
    parts = plan.slots // part
    count = parts * plan.lines
    lines = jnp.concatenate([share[:, LANES * k : LANES * (k + 1)] for k in range(count)], axis=0)
    moved = [lines if m == 0 else pltpu.roll(lines, part * m, 1) for m in range(plan.per_line)]
    paths = out_ref.shape[0] // plan.owners
    for k in range(plan.lines):
        for s in range(plan.per_line):
            line = cva
            for g in range(parts):
                n = g * plan.lines + k
                line = jnp.where(block == g, moved[(g - s) % plan.per_line][n : n + 1], line)
            for p in range(paths):
                out_ref[(k * plan.per_line + s) * paths + p] = line


def finish_kernel(plan, me_ref, place_ref, notional_ref, in_ref, alloc_ref, cva_ref):
    me = me_ref[0]
    rows = place_ref.shape[1]
    key = place_ref[0:1, :].astype(jnp.int32)
    rank = place_ref[1:2, :].astype(jnp.int32)
    lines = in_ref[...]
    count = lines.shape[0]
    paths = count // plan.owners
    pieces = jnp.concatenate(split_bf16(lines, 3), axis=0)
    row = iota((pieces.shape[0], 1), 0) & (count - 1)
    shift = paths.bit_length() - 1
    half = row & (plan.halves - 1)
    found = jnp.zeros((pieces.shape[0], rows), F32)
    for h in range(plan.halves):
        slot = rank + plan.room * h
        slot = jnp.where(slot >= plan.slots, slot - plan.slots, slot)
        hot = mask_bf16(iota((LANES, rows), 0) == slot)
        found = jnp.where(half == h, jnp.dot(pieces, hot, preferred_element_type=F32), found)
    wanted = lax.shift_right_logical(row, shift) == key
    share = jnp.sum(jnp.where(wanted, found, 0.0), axis=0, keepdims=True)
    alloc_ref[...] = share * in_a_row(notional_ref[...])
    own = lax.shift_right_logical(iota((count, 1), 0), shift) == me
    cva = jnp.sum(jnp.where(own, lines, 0.0), axis=0, keepdims=True)
    cva_ref[...] = cva[:, plan.slots : plan.slots + cva_ref.shape[1]]


def body(
    shocks,
    forward_start,
    loading,
    coefficient,
    notional,
    ns_of_trade,
    agr_of_ns,
    cpty_of_agr,
    margin_lag,
    default_weight,
):
    owners = lax.axis_size("trade")
    path_parts = lax.axis_size("path")
    tenors, dates, path_dev = shocks.shape
    path_total = float(path_dev * path_parts)
    rows = coefficient.shape[0]
    lines = rows // LANES
    plan = Plan(owners, rows, tenors, dates)
    cols = dates * path_dev
    me = lax.axis_index("trade").astype(jnp.int32).reshape(1)
    half = lax.rem(lax.axis_index("path").astype(jnp.int32), plan.halves).reshape(1)
    notional = notional.reshape(lines, LANES)

    place, outgoing = pl.pallas_call(
        functools.partial(pack_kernel, plan),
        out_shape=[
            jax.ShapeDtypeStruct((SUBS, rows), F32),
            jax.ShapeDtypeStruct((owners, plan.height, LANES), BF16),
        ],
        in_specs=[SMEM] * 2 + [HBM] * 3,
        out_specs=[VMEM, VMEM],
        scratch_shapes=[
            pltpu.VMEM((owners * lines, LANES), jnp.int32),
            pltpu.VMEM((2 * tenors, rows), BF16),
            pltpu.VMEM((lines, LANES), F32),
            pltpu.SemaphoreType.DMA((3,)),
        ],
        name="pack",
        cost_estimate=pl.CostEstimate(flops=1 << 32, bytes_accessed=1 << 19, transcendentals=0),
    )(me, half, ns_of_trade.reshape(owners * lines, LANES), coefficient.T, notional)
    incoming = [lax.all_to_all(outgoing, "trade", split_axis=0, concat_axis=0, tiled=True)]
    basis = pl.pallas_call(
        functools.partial(basis_kernel, plan),
        out_shape=jax.ShapeDtypeStruct((2 * LANES, cols), BF16),
        in_specs=[HBM] * 3,
        out_specs=VMEM,
        scratch_shapes=[
            pltpu.VMEM((tenors * dates, path_dev), BF16),
            pltpu.VMEM((1, tenors), F32),
            pltpu.VMEM((tenors, tenors), F32),
            pltpu.VMEM((tenors * dates, path_dev), F32),
            pltpu.SemaphoreType.DMA((3,)),
        ],
        name="basis",
        compiler_params=pltpu.CompilerParams(vmem_limit_bytes=16 << 20),
        cost_estimate=pl.CostEstimate(
            flops=2 * 400 * tenors * cols, bytes_accessed=4 << 20, transcendentals=3 * tenors * cols
        ),
    )(shocks.reshape(tenors * dates, path_dev), forward_start.reshape(1, tenors), loading)

    half_trades = plan.trades // plan.halves
    if plan.halves == 2:
        incoming[0], basis = lax.optimization_barrier((incoming[0], basis))
        pairs = [(p, p ^ 1) for p in range(path_parts)]
        incoming.append(lax.ppermute(incoming[0], "path", pairs))
        incoming.append(
            pl.pallas_call(
                functools.partial(price_kernel, plan),
                out_shape=jax.ShapeDtypeStruct((half_trades, cols), BF16),
                in_specs=[VMEM] * 2,
                out_specs=VMEM,
                name="price_own_half",
                compiler_params=pltpu.CompilerParams(vmem_limit_bytes=24 << 20),
                cost_estimate=pl.CostEstimate(
                    flops=4 * half_trades * LANES * cols, bytes_accessed=6 << 20, transcendentals=0
                ),
            )(basis, incoming[0])
        )

    need = 2 * plan.trades * cols + 8 * plan.trades * plan.step + (8 << 20)
    lines_out = pl.pallas_call(
        functools.partial(main_kernel, plan, path_total),
        out_shape=jax.ShapeDtypeStruct((owners * path_parts, 1, LANES), F32),
        in_specs=[SMEM] * 4 + [VMEM] * (2 + len(incoming)),
        out_specs=VMEM,
        scratch_shapes=[pltpu.VMEM((half_trades, cols), BF16)],
        name="value_and_allocate",
        compiler_params=pltpu.CompilerParams(vmem_limit_bytes=need),
    )(me, agr_of_ns, cpty_of_agr, margin_lag, default_weight, basis, *incoming)

    lines_in = lax.all_to_all(lines_out, ("trade", "path"), split_axis=0, concat_axis=0, tiled=True)
    lines_in = lines_in.reshape(owners * path_parts, LANES)
    allocation, cva = pl.pallas_call(
        functools.partial(finish_kernel, plan),
        out_shape=[
            jax.ShapeDtypeStruct((1, rows), F32),
            jax.ShapeDtypeStruct((1, default_weight.shape[0]), F32),
        ],
        in_specs=[SMEM] + [VMEM] * 3,
        out_specs=[VMEM, VMEM],
        name="finish",
        compiler_params=pltpu.CompilerParams(vmem_limit_bytes=32 << 20),
    )(me, place, notional, lines_in)
    return (allocation.reshape(rows), cva.reshape(default_weight.shape[0]))


def solution(mesh):
    placed = (
        P(None, None, "path"),
        P(),
        P(),
        P("trade", None),
        P("trade"),
        P(),
        P("trade"),
        P("trade"),
        P("trade"),
        P("trade", None),
    )
    return jax.shard_map(
        body, mesh=mesh, in_specs=placed, out_specs=(P("trade"), P("trade")), check_vma=False
    )
```
